32 devices in a mesh: seq: 8 (over z, x), tp: 4 (over y, core).
Axes of the slice: x: 2, y: 2, z: 4, core: 2. Of those that a mesh axis runs over, the one named last changes fastest.
Arguments:
- inputs: bfloat16 [8192, 2048], P('seq'), may hold values from -6 to 6
- cotangent: bfloat16 [8192, 2048], P('seq'), may hold values from -6 to 6
- lengths: int32 [9], replicated, may hold values from 0 to 2048, as said below
- offsets: int32 [9], replicated, may hold values from 0 to 8192, as said below
- first_gain: float32 [2048], P('seq'), may hold values from 0.5 to 1.5
- first_bias: float32 [2048], P('seq'), may hold values from -2.5 to 2.5
- query_weight: float32 [2048, 2048], P('seq', 'tp'), may hold values from -0.125 to 0.125
- key_weight: float32 [2048, 2048], P('seq', 'tp'), may hold values from -0.125 to 0.125
- value_weight: float32 [2048, 4096], P('seq', 'tp'), may hold values from -0.125 to 0.125
- gate_weight: float32 [2048, 4096], P('seq', 'tp'), may hold values from -0.125 to 0.125
- group_gain: float32 [4096], P(('tp', 'seq')), may hold values from 0.5 to 1.5
- group_bias: float32 [4096], P(('tp', 'seq')), may hold values from -2.5 to 2.5
- out_weight: float32 [4096, 2048], P('tp', 'seq'), may hold values from -0.09375 to 0.09375
- second_gain: float32 [2048], P('seq'), may hold values from 0.5 to 1.5
- second_bias: float32 [2048], P('seq'), may hold values from -2.5 to 2.5
- up_weight: float32 [2048, 4096], P('seq', 'tp'), may hold values from -0.125 to 0.125
- up_bias: float32 [4096], P(('tp', 'seq')), may hold values from -2.5 to 2.5
- down_weight: float32 [4096, 2048], P('tp', 'seq'), may hold values from -0.09375 to 0.09375
- down_bias: float32 [2048], P('seq'), may hold values from -2.5 to 2.5
Outputs:
- output: bfloat16 [8192, 2048], P('seq')
- grad_inputs: float32 [8192, 2048], P('seq')
- grad_first_gain: float32 [2048], P('seq')
- grad_first_bias: float32 [2048], P('seq')
- grad_query_weight: float32 [2048, 2048], P('seq', 'tp')
- grad_key_weight: float32 [2048, 2048], P('seq', 'tp')
- grad_value_weight: float32 [2048, 4096], P('seq', 'tp')
- grad_gate_weight: float32 [2048, 4096], P('seq', 'tp')
- grad_group_gain: float32 [4096], P(('tp', 'seq'))
- grad_group_bias: float32 [4096], P(('tp', 'seq'))
- grad_out_weight: float32 [4096, 2048], P('tp', 'seq')
- grad_second_gain: float32 [2048], P('seq')
- grad_second_bias: float32 [2048], P('seq')
- grad_up_weight: float32 [2048, 4096], P('seq', 'tp')
- grad_up_bias: float32 [4096], P(('tp', 'seq'))
- grad_down_weight: float32 [4096, 2048], P('tp', 'seq')
- grad_down_bias: float32 [2048], P('seq')
The draws below stay inside these ranges and needn't reach their ends.
Inputs may be any that keep to these rules, and one draw needn't show every extreme that they name: `lengths`: sequences lie in order without intersection, the first at slot 0 and the last ending at slot 8192; each has 1024 to 2048 tokens, entry 1 or 2 exactly 2048; between two sequences lie 0 to 128 padding slots; entries after the last sequence have length 0 and offset 8192. Every block of 1024 slots but the first begins inside a sequence that began in an earlier block. `offsets`: the first slots of the sequences of lengths, increasing.
All inputs are finite; a program needn't handle non-finite values.
Results may differ from the reference program's by a relative error of at most 0.013.
The reference program's roundings to bfloat16 on the way count: a program that leaves them out, or rounds other values in their place, can miss the bound.
Values may be sent and summed in bfloat16 or wider, within the bound.
No kernel may reach another device: no remote copies, remote signals or barrier semaphores. Data moves between devices by JAX's collectives and lax.ppermute only.
A program may use at most 320 MiB of HBM per device.

```python
import math
import jax
import jax.numpy as jnp
from jax import lax

D = 2048
H = 8
KD = 256
VD = 512
FF = 4096
KALL = 2048
VALL = 4096
TOK_DEV = 1024
TOKENS = 8192
SEQ_MIN = 1024
LONGEST = 2048
GAP = 128
NSEQ = 9


def pack_layout(key):
    length_key, padding_key, choose_key = jax.random.split(key, 3)
    wanted = jax.random.randint(length_key, (NSEQ,), SEQ_MIN, LONGEST)
    chosen = jax.random.randint(choose_key, (), 1, 3)
    wanted = jnp.where(jnp.arange(NSEQ) == chosen, LONGEST, wanted).astype(jnp.int32)
    padding = jax.random.randint(padding_key, (NSEQ,), 0, GAP + 1).astype(jnp.int32)

    def place(carry, item):
        start, finished = carry
        want, spare = item
        avail = TOKENS - start
        closing = avail <= LONGEST
        spare = jnp.minimum(spare, jnp.maximum(avail - 2 * SEQ_MIN - 1, 0))
        size = jnp.minimum(want, avail - spare - SEQ_MIN)
        rest = (start + size) % TOK_DEV
        clash = (rest == 0) | (rest + spare >= TOK_DEV)
        spare = jnp.where(clash, 0, spare)
        size = jnp.where(rest == 0, jnp.where(size > SEQ_MIN, size - 1, size + 1), size)
        size = jnp.where(closing, avail, size)
        spare = jnp.where(closing, 0, spare)
        length = jnp.where(finished, 0, size)
        offset = jnp.where(finished, TOKENS, start)
        next_start = jnp.where(finished, start, start + size + spare)
        return ((next_start.astype(jnp.int32), finished | closing), (offset.astype(jnp.int32), length.astype(jnp.int32)))
    begin = (jnp.zeros((), jnp.int32), jnp.zeros((), jnp.bool_))
    _, (offsets, lengths) = lax.scan(place, begin, (wanted, padding))
    return (offsets, lengths)


def draw_lengths(key, part):
    shared = pack_layout(key)
    return shared[1]


def draw_offsets(key, part):
    shared = pack_layout(key)
    return shared[0]


def with_spikes(values, stream_key, source, target, parts, factor):
    def block_of(dim):
        return (jnp.arange(values.shape[dim]) // (values.shape[dim] // parts)).reshape((-1,) + (1,) * (values.ndim - 1 - dim))

    near = jax.random.permutation(stream_key, parts)[block_of(target)]
    second = (block_of(target) + parts // 2) % parts
    return jnp.where((block_of(source) == near) | (block_of(source) == second), factor * values, values)


def block_scale(own_key, dims, shards, low, high):
    factor_of, own = 1.0, jax.random.fold_in(own_key, 6)
    for axis_at, shards_of in shards:
        heights = jnp.exp(jax.random.uniform(jax.random.fold_in(own, axis_at), (shards_of,), jnp.float32, low / len(shards), high / len(shards)))
        factor_of = factor_of * jnp.repeat(heights, dims[axis_at] // shards_of).reshape([-1 if axis == axis_at else 1 for axis in range(len(dims))])
    return factor_of


def noise(own_key, shape, width, bound, cuts=(), kind=jnp.bfloat16):
    values = jax.random.normal(own_key, shape, jnp.float32) * width
    if len(cuts) > 0:
        values = block_scale(own_key, shape, cuts, -0.22, 0.18) * values
    return jnp.clip(values, min=-bound, max=bound).astype(kind)


def heavy_noise(rng, dims, width, bound, cuts, heavy, kind=jnp.bfloat16):
    entries = width * jax.random.normal(rng, dims, jnp.float32)
    if cuts:
        entries = entries * block_scale(rng, dims, cuts, -0.22, 0.18)
    return jnp.clip(with_spikes(entries, jax.random.fold_in(rng, 3), *heavy), -bound, bound).astype(kind)


def setup_inputs(seed: int = 0) -> dict:
    splits = jax.random.split(jax.random.key(seed), 20)
    inputs = heavy_noise(splits[0], (TOKENS, D), 1.0, 6.0, ((0, 8),), (0, 1, 8, 2.0))
    cotangent = heavy_noise(splits[1], (TOKENS, D), 1.0, 6.0, ((0, 8),), (0, 1, 8, 2.0))
    lengths = draw_lengths(jax.random.fold_in(splits[19], 71), 0)
    offsets = draw_offsets(jax.random.fold_in(splits[19], 71), 0)
    first_gain = jnp.clip(1.0 + 0.1 * jax.random.normal(splits[4], (D,), jnp.float32), 0.5, 1.5)
    first_bias = noise(splits[5], (D,), 0.3, 2.5, ((0, 8),), jnp.float32)
    query_weight = noise(splits[6], (D, KALL), D ** -0.5, 0.125, ((0, 8), (1, 4)), jnp.float32)
    key_weight = noise(splits[7], (D, KALL), D ** -0.5, 0.125, ((0, 8), (1, 4)), jnp.float32)
    value_weight = noise(splits[8], (D, VALL), D ** -0.5, 0.125, ((0, 8), (1, 4)), jnp.float32)
    gate_weight = noise(splits[9], (D, VALL), D ** -0.5, 0.125, ((0, 8), (1, 4)), jnp.float32)
    group_gain = jnp.clip(1.0 + 0.1 * jax.random.normal(splits[10], (VALL,), jnp.float32), 0.5, 1.5)
    group_bias = noise(splits[11], (VALL,), 0.3, 2.5, ((0, 32),), jnp.float32)
    out_weight = noise(splits[12], (VALL, D), VALL ** -0.5, 0.09375, ((0, 4), (1, 8)), jnp.float32)
    second_gain = jnp.clip(1.0 + 0.1 * jax.random.normal(splits[13], (D,), jnp.float32), 0.5, 1.5)
    second_bias = noise(splits[14], (D,), 0.3, 2.5, ((0, 8),), jnp.float32)
    up_weight = noise(splits[15], (D, FF), D ** -0.5, 0.125, ((0, 8), (1, 4)), jnp.float32)
    up_bias = noise(splits[16], (FF,), 0.3, 2.5, ((0, 32),), jnp.float32)
    down_weight = noise(splits[17], (FF, D), FF ** -0.5, 0.09375, ((0, 4), (1, 8)), jnp.float32)
    down_bias = noise(splits[18], (D,), 0.3, 2.5, ((0, 8),), jnp.float32)
    return dict(inputs=inputs, cotangent=cotangent, lengths=lengths, offsets=offsets, first_gain=first_gain, first_bias=first_bias, query_weight=query_weight, key_weight=key_weight, value_weight=value_weight, gate_weight=gate_weight, group_gain=group_gain, group_bias=group_bias, out_weight=out_weight, second_gain=second_gain, second_bias=second_bias, up_weight=up_weight, up_bias=up_bias, down_weight=down_weight, down_bias=down_bias)


@jax.custom_vjp
def lower_precision(v):
    return lax.optimization_barrier(v.astype(jnp.bfloat16)).astype(jnp.float32)

@jax.custom_vjp
def lower_precision_backward(v):
    return v

def low_keep(v):
    return (lower_precision(v), None)

def low_pass(kept, grad):
    return (grad,)

def back_keep(v):
    return (v, None)

def back_low(kept, grad):
    return (lower_precision(grad),)
lower_precision.defvjp(low_keep, low_pass)
lower_precision_backward.defvjp(back_keep, back_low)
epsilon = 1e-05
highest_precision = lax.Precision.HIGHEST

def precise(left, right):
    return jnp.dot(left, right, precision=highest_precision)

def layer_norm(values, gain_vec, bias_vec):
    average = lax.optimization_barrier(jnp.mean(values, axis=-1, keepdims=True))
    centred = values - average
    variance = lax.optimization_barrier(jnp.mean(centred * centred, axis=-1, keepdims=True))
    return centred * lax.rsqrt(variance + epsilon) * gain_vec + bias_vec

def gate_norm(retained, gate_raw, gain_vec, bias_vec):
    average = lax.optimization_barrier(jnp.mean(retained, axis=-1, keepdims=True))
    centred = retained - average
    variance = lax.optimization_barrier(jnp.mean(centred * centred, axis=-1, keepdims=True))
    normed = (centred * lax.rsqrt(variance + epsilon)).reshape(gate_raw.shape)
    return (normed * gain_vec + bias_vec) * jax.nn.silu(gate_raw)

def smooth(values):
    return jax.nn.gelu(values, approximate=False)

def rotate(values, cosine_table, sine_table):
    half_size = values.shape[-1] // 2
    turned = jnp.concatenate([-values[..., half_size:], values[..., :half_size]], axis=-1)
    return values * cosine_table + turned * sine_table

def token_layout(first_row, row_total, lengths, offsets):
    position = first_row + jnp.arange(row_total, dtype=jnp.int32)
    inside = (position[:, None] >= offsets[None, :]) & (position[:, None] < offsets[None, :] + lengths[None, :])
    member = inside.astype(jnp.int32)
    labels = jnp.arange(1, lengths.shape[0] + 1, dtype=jnp.int32)
    number = lax.optimization_barrier(jnp.sum(member * labels[None, :], axis=1)) - 1
    seq_start = lax.optimization_barrier(jnp.sum(member * offsets[None, :], axis=1))
    return (number, position - seq_start)

def block_decay(first_row, row_total, lengths, offsets, log_decay, key_size):
    number, within = token_layout(first_row, row_total, lengths, offsets)
    before = token_layout(first_row - 1, 1, lengths, offsets)[0][0]
    final_seq = number[row_total - 1]
    slot_index = jnp.arange(row_total).astype(jnp.float32)
    distance = slot_index[:, None] - slot_index[None, :]
    linked = (number[:, None] == number[None, :]) & (number[:, None] >= 0) & (distance >= 0)
    exponent = jnp.where(linked, distance, 0.0)
    decay_mask = jnp.where(linked[None], jnp.exp(log_decay[:, None, None] * exponent[None]), 0.0)
    entry_weight = jnp.where(((number == before) & (number >= 0))[None, :], jnp.exp(log_decay[:, None] * (slot_index[None, :] + 1.0)), 0.0)
    exit_weight = jnp.where(((number == final_seq) & (number >= 0))[None, :], jnp.exp(log_decay[:, None] * (row_total - 1.0 - slot_index[None, :])), 0.0)
    passing = jnp.where((final_seq == before) & (before >= 0), jnp.exp(log_decay * row_total), 0.0)
    half_size = key_size // 2
    frequency = jnp.exp(-math.log(10000.0) * 2.0 * jnp.arange(half_size).astype(jnp.float32) / key_size)
    angles = within.astype(jnp.float32)[:, None] * frequency[None, :]
    angles = jnp.concatenate([angles, angles], axis=-1)[:, None, :]
    return (decay_mask, entry_weight, exit_weight, passing, jnp.cos(angles), jnp.sin(angles))

def reference(inputs, cotangent, lengths, offsets, first_gain, first_bias, query_weight, key_weight, value_weight, gate_weight, group_gain, group_bias, out_weight, second_gain, second_bias, up_weight, up_bias, down_weight, down_bias):
    log_decay = jnp.log(1.0 - jnp.exp2(-5.0 - jnp.arange(H, dtype=jnp.int32).astype(jnp.float32)))
    block_total = TOKENS // TOK_DEV

    def forward(residual_in, *params):
        gain_one, bias_one, query_mat, key_mat, value_mat, gate_mat, group_scale, group_shift, out_mat, gain_two, bias_two, up_mat, up_shift, down_mat, down_shift = [lower_precision(tensor) for tensor in params]

        def block_step(carried_over_state, block_item):
            block_rows, block_id = block_item
            first_row = block_id * TOK_DEV
            decay_mask, entry_weight, exit_weight, passing, cosine_table, sine_table = block_decay(first_row, TOK_DEV, lengths, offsets, log_decay, KD)
            normed_bf = lower_precision(layer_norm(block_rows, gain_one, bias_one))
            query_raw = lower_precision_backward(precise(normed_bf, query_mat)).reshape(TOK_DEV, H, KD)
            key_raw = lower_precision_backward(precise(normed_bf, key_mat)).reshape(TOK_DEV, H, KD)
            value_half_width = lower_precision(lower_precision_backward(precise(normed_bf, value_mat))).reshape(TOK_DEV, H, VD)
            gate_raw = lower_precision_backward(precise(normed_bf, gate_mat))
            query_bf = lower_precision(rotate(query_raw, cosine_table, sine_table))
            key_bf = lower_precision(rotate(key_raw, cosine_table, sine_table))
            query_decay_factor = lower_precision(query_bf * entry_weight.T[:, :, None])
            key_decay_factor = lower_precision(key_bf * exit_weight.T[:, :, None])
            scores = jnp.einsum('bhk,chk->hbc', query_bf, key_bf, precision=highest_precision)
            retained = lower_precision(lower_precision_backward(scores) * decay_mask)
            local_out = jnp.einsum('hbc,chv->bhv', retained, value_half_width, precision=highest_precision)
            cross_block_output = jnp.einsum('lda,daf->ldf', query_decay_factor, lower_precision(carried_over_state), precision=highest_precision)
            retained_out = lower_precision_backward(local_out + cross_block_output)
            local_block_term = lower_precision_backward(jnp.einsum('scr,scq->crq', key_decay_factor, value_half_width, precision=highest_precision))
            new_state = passing[:, None, None] * carried_over_state + local_block_term
            gated = lower_precision(gate_norm(retained_out, gate_raw, group_scale, group_shift))
            branch = lower_precision_backward(precise(gated, out_mat))
            mid_rows = block_rows + branch
            normed_two = lower_precision(layer_norm(mid_rows, gain_two, bias_two))
            up_rows = lower_precision_backward(precise(normed_two, up_mat) + up_shift)
            acted = lower_precision(smooth(up_rows))
            ffn_rows = lower_precision_backward(precise(acted, down_mat) + down_shift)
            return (new_state, mid_rows + ffn_rows)
        blocks = residual_in.reshape(block_total, TOK_DEV, D)
        _, outputs = lax.scan(jax.checkpoint(block_step), jnp.zeros((H, KD, VD), jnp.float32), (blocks, jnp.arange(block_total, dtype=jnp.int32)))
        return outputs.reshape(TOKENS, D)
    output, pull_back = jax.vjp(forward, inputs.astype(jnp.float32), first_gain, first_bias, query_weight, key_weight, value_weight, gate_weight, group_gain, group_bias, out_weight, second_gain, second_bias, up_weight, up_bias, down_weight, down_bias)
    gradients = pull_back(cotangent.astype(jnp.float32))
    return (output.astype(jnp.bfloat16), gradients[0], gradients[1], gradients[2], gradients[3], gradients[4], gradients[5], gradients[6], gradients[7], gradients[8], gradients[9], gradients[10], gradients[11], gradients[12], gradients[13], gradients[14], gradients[15])
```

```python
import math

import jax
import jax.numpy as jnp
from jax import lax
from jax.experimental import pallas as pl
from jax.experimental.pallas import tpu as pltpu
from jax.sharding import PartitionSpec as P

KD = 256
VD = 512
EPS = 1e-05
BF = jnp.bfloat16
F32 = jnp.float32
RING_MOST = 16


def dot(a, b, dims):
    return lax.dot_general(a, b, (dims, ((), ())), preferred_element_type=F32)


def from_others(block, direction, send=lax.ppermute):
    size = lax.axis_size("seq")
    parts = []
    for turn in range(1, max(1, size // 4) + 1):
        distance = direction * turn
        route = [(i - distance, i) for i in range(size) if 0 <= i - distance < size]
        parts.append(send(block, "seq", route))
    return parts


def ring_owner(place, size):
    place = lax.rem(place + 2 * size, size)
    return jnp.where(place < size // 2, 2 * place, 2 * (size - 1 - place) + 1)


def ring_place(index, size):
    return jnp.where(index % 2 == 0, index // 2, size - 1 - index // 2)


def ring_routes(size):
    order = list(range(0, size, 2)) + list(range(size - 1, 0, -2))
    ahead = [(order[i], order[(i + 1) % size]) for i in range(size)]
    return ahead, [(b, a) for a, b in ahead]


def assemble(own, ahead_parts, back_parts):
    size = lax.axis_size("seq")
    rows, cols = own.shape
    half = rows // 2
    count = 2 * (size - 1) + 1

    def kernel(*refs):
        parts, out, sems = refs[:count], refs[count], refs[count + 1]
        me = lax.axis_index("seq")
        place = ring_place(me, size)
        copies = [pltpu.make_async_copy(parts[0], out.at[pl.ds(me * rows, rows)], sems.at[0])]
        for k in range(1, size):
            a = ring_owner(place - k, size)
            b = ring_owner(place + k, size)
            copies.append(
                pltpu.make_async_copy(parts[k], out.at[pl.ds(a * rows, half)], sems.at[k])
            )
            copies.append(
                pltpu.make_async_copy(
                    parts[size - 1 + k],
                    out.at[pl.ds(b * rows + half, half)],
                    sems.at[size - 1 + k],
                )
            )
        for copy in copies:
            copy.start()
        for copy in copies:
            copy.wait()

    return pl.pallas_call(
        kernel,
        out_shape=jax.ShapeDtypeStruct((size * rows, cols), own.dtype),
        in_specs=[pl.BlockSpec(memory_space=pl.ANY)] * count,
        out_specs=pl.BlockSpec(memory_space=pltpu.VMEM),
        scratch_shapes=[pltpu.SemaphoreType.DMA((count,))],
        compiler_params=pltpu.CompilerParams(vmem_limit_bytes=60 * 2**20),
        cost_estimate=pl.CostEstimate(
            flops=4 * 10**9, bytes_accessed=0, transcendentals=0
        ),
        name="assemble",
    )(own, *ahead_parts, *back_parts)


def barrier(*values):
    return lax.optimization_barrier(values)


class Gather:
    def __init__(self, own, extra=None):
        self.size = lax.axis_size("seq")
        self.own = own
        half = own.shape[0] // 2
        self.now = [own[:half], own[half:]] + ([] if extra is None else [extra])
        self.parts = [[own[:half]], [own[half:]], [extra]]
        self.left = self.size - 1

    def tick(self, *values):
        count = len(self.now)
        done = barrier(*self.now, *values)
        self.now, values = list(done[:count]), done[count:]
        if self.left > 0:
            ahead, back = ring_routes(self.size)
            routes = [ahead, back, ahead]
            self.now = [
                lax.ppermute(block, "seq", route) for block, route in zip(self.now, routes)
            ]
            for part, block in zip(self.parts, self.now):
                part.append(block)
        self.left -= 1
        return values

    @property
    def ended(self):
        return self.left < 0

    def result(self):
        return assemble(self.own, self.parts[0][1:], self.parts[1][1:])

    def table(self):
        place = ring_place(lax.axis_index("seq"), self.size)
        stack = jnp.concatenate(self.parts[2], axis=0)
        index = jnp.arange(self.size)
        return stack[lax.rem(place - ring_place(index, self.size) + self.size, self.size)]


class Line:
    def __init__(self, token):
        self.token = token

    def run(self, function, *values):
        *values, self.token = barrier(*values, self.token)
        out = function(*values)
        first, *rest = out if isinstance(out, (tuple, list)) else (out,)
        first, self.token = barrier(first, self.token)
        return (first, *rest) if len(rest) else first

    def send(self, block, axis, route):
        block, self.token = barrier(block, self.token)
        return lax.ppermute(block, axis, route)

    def tick(self, *rings):
        for ring in rings:
            if not ring.ended:
                (self.token,) = ring.tick(self.token)

    def meet(self, *values):
        *values, self.token = barrier(*values, self.token)
        return values


class Reduce:
    def __init__(self, ahead, back=None):
        self.size = lax.axis_size("seq")
        self.halves = back is None
        self.grads = (ahead, ahead if back is None else back)
        self.place = ring_place(lax.axis_index("seq"), self.size)
        self.arrived = ()
        self.step = 0

    def tick(self, *values):
        self.step += 1
        if self.arrived:
            *self.arrived, first = barrier(*self.arrived, values[0])
            values = (first, *values[1:])
        self.now = ring_add(self.grads, self.arrived, self.place, self.step, self.halves)
        *self.now, first = barrier(*self.now, values[0])
        if self.step < self.size:
            routes = ring_routes(self.size)
            self.arrived = [
                lax.ppermute(block, "seq", route) for block, route in zip(self.now, routes)
            ]
        return (first, *values[1:])

    @property
    def ended(self):
        return self.step >= self.size

    def result(self):
        if self.halves:
            return jnp.concatenate(self.now, axis=0)
        return self.now


class Builtin:
    def __init__(self, value):
        self.value = value
        self.ended = True

    def result(self):
        return self.value


class Clock:
    def __init__(self, lanes):
        self.lanes = [[] for _ in range(lanes)]
        self.turn = 0

    def add(self, lane, chain, *values):
        self.lanes[lane].append(chain)
        if len(self.lanes[lane]) == 1:
            values = self.settle(lane, values)
        return values

    def settle(self, lane, values):
        queue = self.lanes[lane]
        while queue:
            if not queue[0].ended:
                values = queue[0].tick(*values)
            if not queue[0].ended:
                break
            queue.pop(0)
        return values

    def until(self, ring, *values):
        while any(ring in lane for lane in self.lanes):
            values = self.tick(*values)
            values = values if isinstance(values, tuple) else (values,)
        return values[0] if len(values) == 1 else values

    def tick(self, *values, count=1):
        for _ in range(count):
            for _ in self.lanes:
                lane = self.turn
                self.turn = (self.turn + 1) % len(self.lanes)
                if self.lanes[lane]:
                    values = self.settle(lane, values)
                    break
        return values[0] if len(values) == 1 else tuple(values)


def gather(own, extra=None):
    if lax.axis_size("seq") > RING_MOST:
        return Builtin(lax.all_gather(own, "seq", axis=0, tiled=True))
    return Gather(own, extra)


def reduce(ahead, back=None):
    if lax.axis_size("seq") > RING_MOST:
        total = [
            lax.psum_scatter(grad.astype(F32), "seq", scatter_dimension=0, tiled=True)
            for grad in (ahead, back)
            if grad is not None
        ]
        return Builtin(total[0] if back is None else total)
    return Reduce(ahead, back)


def small_reduce(table):
    me = lax.axis_index("seq")
    distance = table.shape[0] // 2
    while distance >= 1:
        route = [(i, i ^ distance) for i in range(lax.axis_size("seq"))]
        high = (me // distance) % 2
        kept = lax.dynamic_slice_in_dim(table, high * distance, distance)
        sent = lax.dynamic_slice_in_dim(table, (1 - high) * distance, distance)
        table = kept + lax.ppermute(sent, "seq", route)
        distance //= 2
    return table[0]


def swap(block, bit):
    return lax.ppermute(block, "tp", [(i, i ^ bit) for i in range(lax.axis_size("tp"))])


def token_layout(first_row, row_total, lengths, offsets):
    position = first_row + jnp.arange(row_total, dtype=jnp.int32)
    inside = (position[:, None] >= offsets[None, :]) & (
        position[:, None] < offsets[None, :] + lengths[None, :]
    )
    member = inside.astype(jnp.int32)
    labels = jnp.arange(1, lengths.shape[0] + 1, dtype=jnp.int32)
    number = jnp.sum(member * labels[None, :], axis=1) - 1
    seq_start = jnp.sum(member * offsets[None, :], axis=1)
    return (number, position - seq_start)


def passing_weight(first_row, row_total, lengths, offsets, log_decay):
    before = token_layout(first_row - 1, 1, lengths, offsets)[0][0]
    last = token_layout(first_row + row_total - 1, 1, lengths, offsets)[0][0]
    return jnp.where((last == before) & (before >= 0), jnp.exp(log_decay * row_total), 0.0)


def block_decay(first_row, row_total, lengths, offsets, log_decay):
    number, within = token_layout(first_row, row_total, lengths, offsets)
    before = token_layout(first_row - 1, 1, lengths, offsets)[0][0]
    final_seq = number[row_total - 1]
    slot_index = jnp.arange(row_total).astype(jnp.float32)
    entry_weight = jnp.where(
        ((number == before) & (number >= 0))[None, :],
        jnp.exp(log_decay[:, None] * (slot_index[None, :] + 1.0)),
        0.0,
    )
    exit_weight = jnp.where(
        ((number == final_seq) & (number >= 0))[None, :],
        jnp.exp(log_decay[:, None] * (row_total - 1.0 - slot_index[None, :])),
        0.0,
    )
    half_size = KD // 2
    frequency = jnp.exp(-math.log(10000.0) * 2.0 * jnp.arange(half_size).astype(jnp.float32) / KD)
    angles = within.astype(jnp.float32)[:, None] * frequency[None, :]
    return (number, entry_weight, exit_weight, jnp.cos(angles), jnp.sin(angles))


def standardize(values):
    average = jnp.mean(values, axis=-1, keepdims=True)
    centred = values - average
    variance = jnp.mean(centred * centred, axis=-1, keepdims=True)
    scale = lax.rsqrt(variance + EPS)
    return centred * scale, scale


def standardize_back(d_normed, normed, scale):
    first = jnp.mean(d_normed, axis=-1, keepdims=True)
    second = jnp.mean(d_normed * normed, axis=-1, keepdims=True)
    return scale * (d_normed - first - normed * second)


def kernel_call(body, name, grid, ins, outs, shapes, weight, prefetch=(), vmem=60):
    arrays = [a for a, _, _ in ins]
    return pl.pallas_call(
        body,
        out_shape=[jax.ShapeDtypeStruct(s, t) for s, t in shapes],
        grid_spec=pltpu.PrefetchScalarGridSpec(
            num_scalar_prefetch=len(prefetch),
            grid=grid,
            in_specs=[pl.BlockSpec(block, index) for _, block, index in ins],
            out_specs=[pl.BlockSpec(block, index) for block, index in outs],
        ),
        compiler_params=pltpu.CompilerParams(vmem_limit_bytes=vmem * 2**20),
        cost_estimate=pl.CostEstimate(
            flops=weight * 10**9, bytes_accessed=0, transcendentals=0
        ),
        name=name,
    )(*prefetch, *arrays)


def row_tile(i, *_):
    return (i, 0)


def fixed(*_):
    return (0, 0)


def fixed3(*_):
    return (0, 0, 0)


def turn(values, cosine, sine):
    low, high = values[:, : KD // 2], values[:, KD // 2 :]
    return jnp.concatenate([low * cosine - high * sine, high * cosine + low * sine], axis=1)


def norm_rows(x, gain, shift, tile=256):
    rows, width = x.shape

    def kernel(x_ref, gain_ref, shift_ref, out_ref):
        hat, _ = standardize(x_ref[...].astype(F32))
        out_ref[...] = (hat * gain_ref[...] + shift_ref[...]).astype(BF)

    return kernel_call(
        kernel,
        "first_norm",
        (rows // tile,),
        [
            (x, (tile, width), row_tile),
            (gain[None, :], (1, width), fixed),
            (shift[None, :], (1, width), fixed),
        ],
        [((tile, width), row_tile)],
        [((rows, width), BF)],
        6,
    )[0]


def project_turn(n1, qk_mat, cosine, sine, tile=256):
    rows, width = n1.shape
    cols = qk_mat.shape[1] // 2

    def kernel(n1_ref, mat_ref, cos_ref, sin_ref, q_ref, k_ref):
        raw = jnp.dot(n1_ref[...], mat_ref[...], preferred_element_type=F32)
        cos, sin = cos_ref[...], sin_ref[...]
        for at in range(0, cols, KD):
            q_ref[:, at : at + KD] = turn(raw[:, at : at + KD], cos, sin).astype(BF)
            k_ref[:, at : at + KD] = turn(raw[:, cols + at : cols + at + KD], cos, sin).astype(BF)

    return kernel_call(
        kernel,
        "query_key",
        (rows // tile,),
        [
            (n1, (tile, width), row_tile),
            (qk_mat, (width, 2 * cols), fixed),
            (cosine, (tile, KD // 2), row_tile),
            (sine, (tile, KD // 2), row_tile),
        ],
        [((tile, cols), row_tile)] * 2,
        [((rows, cols), BF)] * 2,
        9,
    )


def decay_block(first, count, wide, number_col, number_row, log_decay):
    distance = (
        first
        + lax.broadcasted_iota(jnp.int32, (count, wide), 0)
        - lax.broadcasted_iota(jnp.int32, (count, wide), 1)
    )
    linked = (number_col == number_row) & (number_col >= 0) & (distance >= 0)
    exponent = jnp.maximum(distance, 0).astype(F32)
    return jnp.where(linked, jnp.exp(log_decay * exponent), 0.0)


def own_column(table):
    here = lax.broadcasted_iota(jnp.int32, table.shape, 1) == pl.program_id(0)
    return jnp.sum(jnp.where(here, table, 0.0), axis=1, keepdims=True)


def retain(q, k, v, number, exit_weight, log_decay, tile=256):
    rows = q.shape[0]
    heads = q.shape[1] // KD

    def kernel(decay_ref, q_ref, k_ref, v_ref, col_ref, row_ref, exit_ref, out_ref, state_ref):
        decay = decay_ref[pl.program_id(0)]
        for first in range(0, rows, tile):
            wide = first + tile
            scores = lax.dot_general(
                q_ref[first:wide], k_ref[:wide], (((1,), (1,)), ((), ())), preferred_element_type=F32
            )
            mask = decay_block(first, tile, wide, col_ref[first:wide], row_ref[:, :wide], decay)
            out_ref[first:wide] = jnp.dot(
                (scores * mask).astype(BF), v_ref[:wide], preferred_element_type=F32
            )
        kd = (k_ref[...].astype(F32) * own_column(exit_ref[...])).astype(BF)
        state_ref[0] = lax.dot_general(
            kd, v_ref[...], (((0,), (0,)), ((), ())), preferred_element_type=F32
        )

    def head(h, *_):
        return (0, h)

    def head3(h, *_):
        return (h, 0, 0)

    return kernel_call(
        kernel,
        "retain",
        (heads,),
        [
            (q, (rows, KD), head),
            (k, (rows, KD), head),
            (v, (rows, VD), head),
            (number[:, None], (rows, 1), fixed),
            (number[None, :], (1, rows), fixed),
            (exit_weight, (rows, heads), fixed),
        ],
        [((rows, VD), head), ((1, KD, VD), head3)],
        [((rows, heads * VD), F32), ((heads, KD, VD), F32)],
        8,
        prefetch=(log_decay,),
    )


def gate_forward(n1, gate_mat, q, entry, state, local_out, scale, shift, tile=256):
    rows, width = n1.shape
    cols = gate_mat.shape[1]
    heads = cols // VD

    def kernel(
        n1_ref, mat_ref, q_ref, entry_ref, state_ref, local_ref, scale_ref, shift_ref,
        y_ref, gate_ref, hat_ref, dev_ref,
    ):
        gate = jnp.dot(n1_ref[...], mat_ref[...], preferred_element_type=F32)
        gate_ref[...] = gate
        swish = gate * jax.nn.sigmoid(gate)
        devs = []
        for h in range(heads):
            at = slice(h * VD, (h + 1) * VD)
            qd = (q_ref[:, h * KD : (h + 1) * KD].astype(F32) * entry_ref[:, h : h + 1]).astype(BF)
            r = local_ref[:, at] + jnp.dot(qd, state_ref[h], preferred_element_type=F32)
            hat, dev = standardize(r)
            hat_ref[:, at] = hat
            devs.append(dev)
            affine = hat * scale_ref[:, at] + shift_ref[:, at]
            y_ref[:, at] = (affine * swish[:, at]).astype(BF)
        dev_ref[...] = jnp.concatenate(devs, axis=1)

    return kernel_call(
        kernel,
        "gate_forward",
        (rows // tile,),
        [
            (n1, (tile, width), row_tile),
            (gate_mat, (width, cols), fixed),
            (q, (tile, heads * KD), row_tile),
            (entry, (tile, heads), row_tile),
            (state, state.shape, fixed3),
            (local_out, (tile, cols), row_tile),
            (scale[None, :], (1, cols), fixed),
            (shift[None, :], (1, cols), fixed),
        ],
        [((tile, cols), row_tile)] * 3 + [((tile, heads), row_tile)],
        [((rows, cols), BF), ((rows, cols), F32), ((rows, cols), F32), ((rows, heads), F32)],
        12,
    )


def gate_backward(d_branch, out_mat, gate, hat, dev, scale, shift, tile=256):
    rows, width = d_branch.shape
    cols = out_mat.shape[1]
    heads = cols // VD

    def kernel(
        db_ref, mat_ref, gate_ref, hat_ref, dev_ref, scale_ref, shift_ref,
        dg_ref, dr_ref, gain_ref, bias_ref,
    ):
        @pl.when(pl.program_id(0) == 0)
        def _():
            gain_ref[...] = jnp.zeros_like(gain_ref)
            bias_ref[...] = jnp.zeros_like(bias_ref)

        d_y = jnp.dot(db_ref[...], mat_ref[...], preferred_element_type=F32)
        for h in range(heads):
            at = slice(h * VD, (h + 1) * VD)
            z, dy, r_hat = gate_ref[:, at], d_y[:, at], hat_ref[:, at]
            sigma = jax.nn.sigmoid(z)
            affine = r_hat * scale_ref[:, at] + shift_ref[:, at]
            dg_ref[:, at] = (dy * affine * (sigma * (1.0 + z * (1.0 - sigma)))).astype(BF)
            d_affine = dy * (z * sigma)
            gain_ref[:, at] += jnp.sum(d_affine * r_hat, axis=0, keepdims=True)
            bias_ref[:, at] += jnp.sum(d_affine, axis=0, keepdims=True)
            d_hat = d_affine * scale_ref[:, at]
            dr_ref[:, at] = standardize_back(d_hat, r_hat, dev_ref[:, h : h + 1]).astype(BF)

    return kernel_call(
        kernel,
        "gate_backward",
        (rows // tile,),
        [
            (d_branch, (tile, width), row_tile),
            (out_mat, (width, cols), fixed),
            (gate, (tile, cols), row_tile),
            (hat, (tile, cols), row_tile),
            (dev, (tile, heads), row_tile),
            (scale[None, :], (1, cols), fixed),
            (shift[None, :], (1, cols), fixed),
        ],
        [((tile, cols), row_tile)] * 2 + [((1, cols), fixed)] * 2,
        [((rows, cols), BF), ((rows, cols), BF), ((1, cols), F32), ((1, cols), F32)],
        0,
    )


def feed_forward(n2, up_mat, up_shift, cotangent, down_mat, tile=256):
    rows, width = n2.shape
    cols = up_mat.shape[1]

    def kernel(n2_ref, up_ref, shift_ref, cot_ref, down_ref, act_ref, dup_ref, sum_ref):
        @pl.when(pl.program_id(0) == 0)
        def _():
            sum_ref[...] = jnp.zeros_like(sum_ref)

        for at in range(0, cols, 256):
            part = slice(at, at + 256)
            z = jnp.dot(n2_ref[...], up_ref[:, part], preferred_element_type=F32)
            z = z + shift_ref[:, part]
            d_act = jnp.dot(cot_ref[...], down_ref[:, part], preferred_element_type=F32)
            half = 0.5 * (1.0 + lax.erf(z * (0.5**0.5)))
            act_ref[:, part] = (z * half).astype(BF)
            slope = half + z * (jnp.exp(-0.5 * z * z) * (1.0 / math.sqrt(2.0 * math.pi)))
            d_up = (slope * d_act).astype(BF)
            dup_ref[:, part] = d_up
            sum_ref[:, part] += jnp.sum(d_up.astype(F32), axis=0, keepdims=True)

    return kernel_call(
        kernel,
        "feed_forward",
        (rows // tile,),
        [
            (n2, (tile, width), row_tile),
            (up_mat, (width, cols), fixed),
            (up_shift[None, :], (1, cols), fixed),
            (cotangent, (tile, width), row_tile),
            (down_mat, (width, cols), fixed),
        ],
        [((tile, cols), row_tile)] * 2 + [((1, cols), fixed)],
        [((rows, cols), BF), ((rows, cols), BF), ((1, cols), F32)],
        16,
    )


def retain_backward(q, k, v, d_r, state, number, entry, log_decay, cosine, sine, tile=256):
    rows = q.shape[0]
    heads = q.shape[1] // KD

    def kernel(
        decay_ref, q_ref, k_ref, v_ref, dr_ref, state_ref, col_ref, row_ref, entry_ref,
        cos_ref, sin_ref, dq_ref, dk_ref, dv_ref,
    ):
        decay = decay_ref[pl.program_id(0)]
        across = (((1,), (1,)), ((), ()))
        down = (((0,), (0,)), ((), ()))
        for first in reversed(range(0, rows, tile)):
            wide = first + tile
            here = slice(first, wide)
            q_i, dr_i = q_ref[here], dr_ref[here]
            mask = decay_block(first, tile, wide, col_ref[here], row_ref[:, :wide], decay)
            scores = lax.dot_general(q_i, k_ref[:wide], across, preferred_element_type=F32)
            weights = (scores * mask).astype(BF)
            d_scores = lax.dot_general(dr_i, v_ref[:wide], across, preferred_element_type=F32)
            d_scores = (d_scores * mask).astype(BF)
            dq = jnp.dot(d_scores, k_ref[:wide], preferred_element_type=F32)
            dq = dq + own_column(entry_ref[here]) * lax.dot_general(
                dr_i, state_ref[0], across, preferred_element_type=F32
            )
            dq_ref[here] = turn(dq, cos_ref[here], -sin_ref[here]).astype(BF)
            dk = lax.dot_general(d_scores, q_i, down, preferred_element_type=F32)
            dv = lax.dot_general(weights, dr_i, down, preferred_element_type=F32)
            if wide == rows:
                dk_ref[...] = dk
                dv_ref[...] = dv
            else:
                dk_ref[:wide] += dk
                dv_ref[:wide] += dv

    def head(h, *_):
        return (0, h)

    def head3(h, *_):
        return (h, 0, 0)

    return kernel_call(
        kernel,
        "retain_backward",
        (heads,),
        [
            (q, (rows, KD), head),
            (k, (rows, KD), head),
            (v, (rows, VD), head),
            (d_r, (rows, VD), head),
            (state, (1, KD, VD), head3),
            (number[:, None], (rows, 1), fixed),
            (number[None, :], (1, rows), fixed),
            (entry, (rows, heads), fixed),
            (cosine, (rows, KD // 2), fixed),
            (sine, (rows, KD // 2), fixed),
        ],
        [((rows, KD), head), ((rows, KD), head), ((rows, VD), head)],
        [((rows, heads * KD), BF), ((rows, heads * KD), F32), ((rows, heads * VD), F32)],
        0,
        prefetch=(log_decay,),
    )


def state_backward(k, v, exit_weight, leaving, dk, dv, cosine, sine, tile=256):
    rows = k.shape[0]
    heads = k.shape[1] // KD

    def kernel(
        k_ref, v_ref, exit_ref, leaving_ref, dk_in, dv_in, cos_ref, sin_ref, dk_ref, dv_ref
    ):
        for h in range(heads):
            at, wide = slice(h * KD, (h + 1) * KD), slice(h * VD, (h + 1) * VD)
            weight = exit_ref[:, h : h + 1]
            kd = (k_ref[:, at].astype(F32) * weight).astype(BF)
            d_k = dk_in[:, at] + weight * lax.dot_general(
                v_ref[:, wide], leaving_ref[h], (((1,), (1,)), ((), ())), preferred_element_type=F32
            )
            dk_ref[:, at] = turn(d_k, cos_ref[...], -sin_ref[...]).astype(BF)
            d_v = dv_in[:, wide] + jnp.dot(kd, leaving_ref[h], preferred_element_type=F32)
            dv_ref[:, wide] = d_v.astype(BF)

    return kernel_call(
        kernel,
        "state_backward",
        (rows // tile,),
        [
            (k, (tile, heads * KD), row_tile),
            (v, (tile, heads * VD), row_tile),
            (exit_weight, (tile, heads), row_tile),
            (leaving, leaving.shape, fixed3),
            (dk, (tile, heads * KD), row_tile),
            (dv, (tile, heads * VD), row_tile),
            (cosine, (tile, KD // 2), row_tile),
            (sine, (tile, KD // 2), row_tile),
        ],
        [((tile, heads * KD), row_tile), ((tile, heads * VD), row_tile)],
        [((rows, heads * KD), BF), ((rows, heads * VD), BF)],
        0,
    )


def second_norm(inputs, side, kept, other, gain, shift, tile=128):
    half, width = kept.shape
    steps = half // tile

    def kernel(side_ref, x_ref, kept_ref, other_ref, gain_ref, shift_ref, mid_ref, n2_ref):
        mid = x_ref[...].astype(F32) + (kept_ref[...].astype(F32) + other_ref[...].astype(F32))
        mid_ref[...] = mid
        hat, _ = standardize(mid)
        n2_ref[...] = (hat * gain_ref[...] + shift_ref[...]).astype(BF)

    return kernel_call(
        kernel,
        "second_norm",
        (steps,),
        [
            (inputs, (tile, width), lambda i, side_ref: (side_ref[0] * steps + i, 0)),
            (kept, (tile, width), row_tile),
            (other, (tile, width), row_tile),
            (gain[None, :], (1, width), fixed),
            (shift[None, :], (1, width), fixed),
        ],
        [((tile, width), row_tile)] * 2,
        [((half, width), F32), ((half, width), BF)],
        6,
        prefetch=(side[None],),
    )


def norm_backward(x, x_rows, kept, other, base, base_rows, gain, side, tile=128):
    half, width = kept.shape
    steps = half // tile

    def kernel(
        side_ref, x_ref, kept_ref, other_ref, base_ref, gain_ref,
        out_ref, low_ref, gain_out, bias_out,
    ):
        @pl.when(pl.program_id(0) == 0)
        def _():
            gain_out[...] = jnp.zeros_like(gain_out)
            bias_out[...] = jnp.zeros_like(bias_out)

        d_n = kept_ref[...].astype(F32) + other_ref[...].astype(F32)
        hat, dev = standardize(x_ref[...].astype(F32))
        gain_out[...] += jnp.sum(d_n * hat, axis=0, keepdims=True)
        bias_out[...] += jnp.sum(d_n, axis=0, keepdims=True)
        out = base_ref[...].astype(F32) + standardize_back(d_n * gain_ref[...], hat, dev)
        out_ref[...] = out
        low_ref[...] = out.astype(BF)

    def picked(i, side_ref):
        return (side_ref[0] * steps + i, 0)

    return kernel_call(
        kernel,
        "norm_backward",
        (steps,),
        [
            (x, (tile, width), picked if x_rows else row_tile),
            (kept, (tile, width), row_tile),
            (other, (tile, width), row_tile),
            (base, (tile, width), picked if base_rows else row_tile),
            (gain[None, :], (1, width), fixed),
        ],
        [((tile, width), row_tile)] * 2 + [((1, width), fixed)] * 2,
        [((half, width), F32), ((half, width), BF), ((1, width), F32), ((1, width), F32)],
        0,
        prefetch=(side[None],),
    )


def partial_rows(values, mats, which, added=(), pieces=1, tile=512):
    rows, width = values[0].shape[0], mats[0].shape[0]
    half, count = rows // 2, len(values)

    def kernel(which_ref, *refs):
        total = sum(
            lax.dot_general(v[...], m[...], (((1,), (1,)), ((), ())), preferred_element_type=F32)
            for v, m in zip(refs[:count], refs[count : 2 * count])
        )
        if added:
            total = total + jnp.concatenate(
                [ref[...].astype(F32) for ref in refs[2 * count : 2 * count + len(added)]], axis=0
            )
        for piece, ref in enumerate(refs[-pieces:]):
            ref[...] = total[piece * half // pieces : (piece + 1) * half // pieces].astype(BF)

    def column_tile(i, *_):
        return (0, i)

    ins = [(v, (half, v.shape[1]), lambda i, which_ref: (which_ref[0], 0)) for v in values]
    ins += [(m, (tile, m.shape[1]), row_tile) for m in mats]
    ins += [(part, (part.shape[0], tile), column_tile) for part in added]
    return kernel_call(
        kernel,
        "partial_rows",
        (width // tile,),
        ins,
        [((half // pieces, tile), column_tile)] * pieces,
        [((half // pieces, width), BF)] * pieces,
        0,
        prefetch=(which[None],),
    )


def finish_output(mid, kept, other, shift, tile=256):
    half, width = mid.shape

    def kernel(mid_ref, kept_ref, other_ref, shift_ref, out_ref):
        ffn = kept_ref[...].astype(F32) + other_ref[...].astype(F32)
        out_ref[...] = (mid_ref[...] + ffn + shift_ref[...]).astype(BF)

    return kernel_call(
        kernel,
        "finish_output",
        (half // tile,),
        [
            (mid, (tile, width), row_tile),
            (kept, (tile, width), row_tile),
            (other, (tile, width), row_tile),
            (shift[None, :], (1, width), fixed),
        ],
        [((tile, width), row_tile)],
        [((half, width), BF)],
        0,
    )[0]


def both_halves(mine, others, side, tile=256):
    half, width = mine.shape
    tile = min(tile, half // len(others))
    steps = half // tile
    each = steps // len(others)

    def kernel(side_ref, mine_ref, *refs):
        out_ref = refs[-1]
        at = pl.program_id(0)

        @pl.when(at // steps == side_ref[0])
        def _():
            out_ref[...] = mine_ref[...]

        for piece, ref in enumerate(refs[:-1]):

            @pl.when((at // steps != side_ref[0]) & (at % steps // each == piece))
            def _(ref=ref):
                out_ref[...] = ref[...]

    def within(which, first, count):
        def index(i, side_ref):
            return (jnp.clip(i - (side_ref[0] ^ which) * steps - first, 0, count - 1), 0)

        return index

    return kernel_call(
        kernel,
        "both_halves",
        (2 * steps,),
        [(mine, (tile, width), within(0, 0, steps))]
        + [(ref, (tile, width), within(1, p * each, each)) for p, ref in enumerate(others)],
        [((tile, width), row_tile)],
        [((2 * half, width), mine.dtype)],
        0,
        prefetch=(side[None],),
    )[0]


def ring_add(grads, arrived, place, step, halves):
    size = lax.axis_size("seq")
    rows = grads[0].shape[0] // size // (2 if halves else 1)
    kind = BF if step < size else F32

    def kernel(place_ref, *refs):
        for i in range(2):
            total = refs[i][...].astype(F32)
            if arrived:
                total = total + refs[2 + i][...].astype(F32)
            refs[i - 2][...] = total.astype(kind)

    def own(sign, low):
        def index(i, place_ref):
            owner = ring_owner(place_ref[0] + sign * step, size)
            return (2 * owner + low if halves else owner, 0)

        return index

    blocks = [(rows, grad.shape[1]) for grad in grads]
    ins = [(grads[0], blocks[0], own(-1, 0)), (grads[1], blocks[1], own(1, 1))]
    ins += [(block, block.shape, fixed) for block in arrived]
    return kernel_call(
        kernel,
        "ring_add",
        (1,),
        ins,
        [(block, fixed) for block in blocks],
        [(block, kind) for block in blocks],
        0,
        prefetch=(place[None],),
    )


def body(
    inputs,
    cotangent,
    lengths,
    offsets,
    first_gain,
    first_bias,
    query_weight,
    key_weight,
    value_weight,
    gate_weight,
    group_gain,
    group_bias,
    out_weight,
    second_gain,
    second_bias,
    up_weight,
    up_bias,
    down_weight,
    down_bias,
):
    size = lax.axis_size("seq")
    rows, width = inputs.shape
    shard = first_gain.shape[0]
    unit = group_gain.shape[0]
    heads = query_weight.shape[1] // KD
    half = rows // 2
    tp_me = lax.axis_index("tp")
    side = lax.rem(tp_me, 2)
    mine = side * half

    qk_own = jnp.concatenate([query_weight, key_weight], axis=1).astype(BF)
    v_own = value_weight.astype(BF)
    own_vector = jnp.concatenate(
        [
            first_gain,
            first_bias,
            second_gain,
            second_bias,
            down_bias,
            group_gain,
            group_bias,
            up_bias,
        ]
    ).astype(BF)[None, :]
    clock = Clock(2)
    qk_ring = gather(qk_own, own_vector)
    v_ring = gather(v_own)
    x = inputs
    (x,) = clock.add(0, qk_ring, x)
    (x,) = clock.add(1, v_ring, x)
    g_own = gate_weight.astype(BF)
    o_own = out_weight.astype(BF).T
    u_own = up_weight.astype(BF)
    w_own = down_weight.astype(BF).T
    g_ring, o_ring, u_ring, w_ring = [gather(own) for own in (g_own, o_own, u_own, w_own)]
    for lane, ring in enumerate((g_ring, o_ring, u_ring, w_ring)):
        clock.add(lane % 2, ring)

    first_row = lax.axis_index("seq") * rows
    log_decay = jnp.log(
        1.0
        - jnp.exp2(-5.0 - (tp_me * heads + jnp.arange(heads, dtype=jnp.int32)).astype(jnp.float32))
    )
    number, entry_weight, exit_weight, cosine, sine = block_decay(
        first_row, rows, lengths, offsets, log_decay
    )
    entry_cols, exit_cols = entry_weight.T, exit_weight.T
    x = clock.tick(x, count=3)
    x, cosine, sine, number, entry_cols, exit_cols = clock.tick(
        x, cosine, sine, number, entry_cols, exit_cols
    )
    x = clock.until(v_ring, x)

    if isinstance(qk_ring, Builtin):
        table = lax.all_gather(own_vector, "seq", axis=0, tiled=True).astype(F32)
    else:
        table = qk_ring.table().astype(F32)

    def wide(i):
        return table[:, i * shard : (i + 1) * shard].reshape(-1)

    def narrow(i):
        start = 5 * shard + i * unit
        return table[:, start : start + unit].reshape(-1)

    gain_one, bias_one, gain_two, bias_two, down_shift = [wide(i) for i in range(5)]
    group_scale, group_shift, up_shift = [narrow(i) for i in range(3)]

    n1 = norm_rows(x, gain_one, bias_one)
    n1 = clock.tick(n1)
    qk_mat = qk_ring.result()
    n1, qk_mat = clock.tick(n1, qk_mat)
    q, k = project_turn(n1, qk_mat, cosine, sine)
    q, k, n1 = clock.tick(q, k, n1, count=2)
    v_mat = v_ring.result()
    n1, v_mat = clock.tick(n1, v_mat)
    v = dot(n1, v_mat, ((1,), (0,))).astype(BF)
    q, k, v = clock.tick(q, k, v)
    local_out, local_state = retain(q, k, v, number, exit_cols, log_decay)
    local_out, local_state = clock.tick(local_out, local_state)
    state_parts = from_others(local_state.astype(BF), 1)
    local_out = clock.until(o_ring, local_out)

    def gathered_state(first, rest, direction):
        total, weight = first.astype(F32), 1.0
        for turn, part in enumerate(rest, 1):
            block = first_row - direction * turn * rows
            passed = passing_weight(block, rows, lengths, offsets, log_decay)
            weight = weight * passed
            total = total + weight[:, None, None] * part.astype(F32)
        return total.astype(BF)

    state = gathered_state(state_parts[0], state_parts[1:], 1)
    state, local_out = barrier(state, local_out)
    g_mat = g_ring.result()
    g_mat, state = clock.tick(g_mat, state)
    y, gate, r_hat, r_dev = gate_forward(
        n1, g_mat, q, entry_cols, state, local_out, group_scale, group_shift
    )
    y = clock.tick(y, count=2)
    o_mat = o_ring.result()
    y, o_mat = clock.tick(y, o_mat)

    def pick(values, which):
        return lax.dynamic_slice_in_dim(values, which * half, half)

    def tp_first(make, value):
        sent = make(pick(value, 1 - side)).astype(BF)
        sent, value = clock.tick(sent, value)
        sent = swap(sent, 1)
        return (make(pick(value, side)) + sent.astype(F32)).astype(BF)

    kept = tp_first(lambda part: dot(part, o_mat, ((1,), (1,))), y)
    kept = clock.tick(kept)
    other = swap(kept, 2)
    kept = clock.tick(kept, count=7)
    kept, other = barrier(kept, other)
    mid, n2_mine = second_norm(inputs, side, kept, other, gain_two, bias_two)
    n2_mine = clock.tick(n2_mine)
    n2 = both_halves(n2_mine, [swap(n2_mine, 1)], side)
    n2 = clock.until(w_ring, n2)
    u_mat = u_ring.result()
    w_mat = w_ring.result()
    act, d_up, grad_up_bias = feed_forward(n2, u_mat, up_shift, cotangent, w_mat)

    line = Line(grad_up_bias)
    pairs_two = [(i, i ^ 2) for i in range(lax.axis_size("tp"))]
    pairs_one = [(i, i ^ 1) for i in range(lax.axis_size("tp"))]

    def to_partner(block, pieces=2):
        count = block.shape[0] // pieces
        return [
            line.send(block[i * count : (i + 1) * count], "tp", pairs_one) for i in range(pieces)
        ]

    def partial_sent(values, mats, pieces=2):
        parts = line.run(lambda *v: partial_rows(v, mats, 1 - side, pieces=pieces), *values)
        parts = parts if isinstance(parts, tuple) else (parts,)
        return [line.send(part, "tp", pairs_one) for part in parts]

    def partial_kept(values, mats, sent):
        return line.run(lambda *v: partial_rows(v, mats, side, sent), *values)

    def gradient(x, dy):
        return dot(x, dy, ((0,), (0,)))

    grad_w = line.run(gradient, cotangent, act)
    sent_two = partial_sent((d_up,), (u_mat,), 1)
    grad_u = line.run(gradient, n2, d_up)
    kept_two = partial_kept((d_up,), (u_mat,), sent_two)
    other_two = line.send(kept_two, "tp", pairs_two)
    wu_back = reduce(grad_w, grad_u)
    line.tick(wu_back)
    sent_out = partial_sent((act,), (w_mat,), 1)
    kept_out = partial_kept((act,), (w_mat,), sent_out)
    line.tick(wu_back)
    line.tick(wu_back)
    d_mid, d_branch_mine, grad_second_gain, grad_second_bias = line.run(
        lambda kept, other: norm_backward(
            mid, False, kept, other, cotangent, True, gain_two, side
        ),
        kept_two,
        other_two,
    )
    d_branch_other = to_partner(d_branch_mine, 1)
    line.tick(wu_back)
    d_branch = line.run(lambda mine: both_halves(mine, d_branch_other, side), d_branch_mine)

    d_gate, d_r, grad_group_gain, grad_group_bias = line.run(
        lambda d: gate_backward(d, o_mat, gate, r_hat, r_dev, group_scale, group_shift), d_branch
    )
    line.tick(wu_back)

    def state_part(d_r):
        qd = (q.reshape(rows, heads, KD) * entry_cols[:, :, None]).astype(BF)
        return jnp.einsum(
            "scr,scq->crq", qd, d_r.reshape(rows, heads, VD), preferred_element_type=F32
        ).astype(BF)

    own_grad = line.run(state_part, d_r)
    leaving_parts = from_others(own_grad, -1, line.send)
    grad_o = line.run(gradient, d_branch, y)
    grad_g = line.run(gradient, n1, d_gate)
    line.tick(wu_back)
    og_back = reduce(grad_o, grad_g)
    line.tick(og_back)
    d_q, d_k, d_v = line.run(
        lambda d_r: retain_backward(
            q, k, v, d_r, state, number, entry_cols, log_decay, cosine, sine
        ),
        d_r,
    )
    line.tick(wu_back, og_back)
    leaving = line.run(lambda first, *rest: gathered_state(first, rest, -1), *leaving_parts)
    d_k, d_v = line.run(
        lambda d_k, d_v: state_backward(k, v, exit_cols, leaving, d_k, d_v, cosine, sine),
        d_k,
        d_v,
    )
    line.tick(wu_back)
    grad_v = line.run(gradient, n1, d_v)
    grad_qk = line.run(gradient, n1, jnp.concatenate([d_q, d_k], axis=1))
    line.tick(og_back)
    vqk_back = reduce(grad_v, grad_qk)
    line.tick(vqk_back)
    d_all = (d_gate, d_v, d_q, d_k)
    mats_all = (g_mat, v_mat, qk_mat[:, : heads * KD], qk_mat[:, heads * KD :])
    sent_one = partial_sent(d_all, mats_all, 1)
    line.tick(og_back, vqk_back)
    kept_one = partial_kept(d_all, mats_all, sent_one)
    other_one = line.send(kept_one, "tp", pairs_two)
    line.tick(og_back, vqk_back, og_back, vqk_back, og_back)
    grad_mine, _, grad_first_gain, grad_first_bias = line.run(
        lambda kept, other: norm_backward(
            inputs, True, kept, other, d_mid, False, gain_one, side
        ),
        kept_one,
        other_one,
    )
    other_out = line.send(kept_out, "tp", pairs_two)
    grad_other = to_partner(grad_mine, 1)
    line.tick(vqk_back, og_back)
    grad_inputs = line.run(lambda mine: both_halves(mine, grad_other, side), grad_mine)
    line.tick(vqk_back, og_back)

    grad_up_bias = line.token
    grad_down_bias = jnp.sum(cotangent.astype(F32), axis=0)
    vectors = jnp.concatenate(
        [
            vector.reshape(size, -1)
            for vector in (
                grad_first_gain,
                grad_first_bias,
                grad_second_gain,
                grad_second_bias,
                grad_down_bias,
                grad_group_gain,
                grad_group_bias,
                grad_up_bias,
            )
        ],
        axis=1,
    )
    small = small_reduce(vectors)
    halves = small[: 4 * shard]
    halves = halves + swap(halves, 1)
    line.token = halves
    line.tick(vqk_back, og_back)
    output_mine = line.run(
        lambda kept: finish_output(mid, kept, other_out, down_shift), kept_out
    )
    output_other = to_partner(output_mine, 1)
    line.tick(vqk_back)
    output = line.run(lambda mine: both_halves(mine, output_other, side), output_mine)
    while not (og_back.ended and vqk_back.ended):
        line.tick(og_back, vqk_back)
    halves = line.token
    own = [halves[i * shard : (i + 1) * shard] for i in range(4)]
    own_down_bias = small[4 * shard : 5 * shard]
    own_units = [small[5 * shard + i * unit : 5 * shard + (i + 1) * unit] for i in range(3)]
    own_w, own_u = wu_back.result()
    own_o, own_g = og_back.result()
    own_v, own_qk = vqk_back.result()
    own_q, own_k = own_qk[:, : heads * KD], own_qk[:, heads * KD :]
    return (
        output,
        grad_inputs,
        own[0],
        own[1],
        own_q,
        own_k,
        own_v,
        own_g,
        own_units[0],
        own_units[1],
        own_o.T,
        own[2],
        own[3],
        own_u,
        own_units[2],
        own_w.T,
        own_down_bias,
    )


def solution(mesh):
    placed = (
        P("seq", None),
        P("seq", None),
        P(),
        P(),
        P("seq"),
        P("seq"),
        P("seq", "tp"),
        P("seq", "tp"),
        P("seq", "tp"),
        P("seq", "tp"),
        P(("tp", "seq")),
        P(("tp", "seq")),
        P("tp", "seq"),
        P("seq"),
        P("seq"),
        P("seq", "tp"),
        P(("tp", "seq")),
        P("tp", "seq"),
        P("seq"),
    )
    return jax.shard_map(
        body,
        mesh=mesh,
        in_specs=placed,
        out_specs=(
            P("seq", None),
            P("seq", None),
            P("seq"),
            P("seq"),
            P("seq", "tp"),
            P("seq", "tp"),
            P("seq", "tp"),
            P("seq", "tp"),
            P(("tp", "seq")),
            P(("tp", "seq")),
            P("tp", "seq"),
            P("seq"),
            P("seq"),
            P("seq", "tp"),
            P(("tp", "seq")),
            P("tp", "seq"),
            P("seq"),
        ),
        check_vma=False,
    )
```

```python
import math

import jax
import jax.numpy as jnp
from jax import lax
from jax.experimental import pallas as pl
from jax.experimental.pallas import tpu as pltpu
from jax.sharding import PartitionSpec as P

KD = 256
VD = 512
EPS = 1e-05
BF = jnp.bfloat16
F32 = jnp.float32
RING_MOST = 16


def dot(a, b, dims):
    return lax.dot_general(a, b, (dims, ((), ())), preferred_element_type=F32)


class Others:
    def __init__(self, block, direction, send=lax.ppermute):
        self.size = lax.axis_size("seq")
        self.block, self.direction, self.send = block, direction, send
        turns = max(1, self.size // 4)
        self.paired = turns == 2
        steps = [2] if self.paired else range(1, turns + 1)
        self.parts = [self.shift(direction * step) for step in steps]

    def shift(self, distance):
        route = [(i, i + distance) for i in range(self.size) if 0 <= i + distance < self.size]
        return self.send(self.block, "seq", route)

    def second(self):
        if self.paired:
            (far,) = self.parts
            first = lax.rem(lax.axis_index("seq"), 2) == (0 if self.direction > 0 else 1)
            near = jnp.where(first, self.block, far)
            near = self.send(near, "seq", [(i, i ^ 1) for i in range(self.size)])
            self.parts = [near, far]
        return self.parts


def ring_owner(place, size):
    place = lax.rem(place + 2 * size, size)
    return jnp.where(place < size // 2, 2 * place, 2 * (size - 1 - place) + 1)


def ring_place(index, size):
    return jnp.where(index % 2 == 0, index // 2, size - 1 - index // 2)


def ring_routes(size):
    order = list(range(0, size, 2)) + list(range(size - 1, 0, -2))
    ahead = [(order[i], order[(i + 1) % size]) for i in range(size)]
    return ahead, [(b, a) for a, b in ahead]


class Weight:
    def __init__(self, own, ahead=(), back=()):
        self.size = lax.axis_size("seq") if ahead else 1
        self.rows, self.cols = own.shape
        self.arrays = [own, *ahead, *back]
        self.count = len(self.arrays)
        self.shape = (self.size * self.rows, self.cols)
        self.ins = [(array, None, None) for array in self.arrays]
        self.outs = [(None, None)]
        self.shapes = [(self.shape, own.dtype)]
        self.scratch = [
            pltpu.VMEM(self.shape, own.dtype),
            pltpu.SemaphoreType.DMA((self.count,)),
            pltpu.SemaphoreType.DMA,
        ]

    def copies(self, parts, whole, sems):
        if self.size == 1:
            return [pltpu.make_async_copy(parts[0], whole, sems.at[0])]
        me = lax.axis_index("seq")
        place = ring_place(me, self.size)
        half = self.rows // 2
        at = [(me * self.rows, self.rows)]
        at += [(ring_owner(place - k, self.size) * self.rows, half) for k in range(1, self.size)]
        at += [
            (ring_owner(place + k, self.size) * self.rows + half, half)
            for k in range(1, self.size)
        ]
        return [
            pltpu.make_async_copy(part, whole.at[pl.ds(first, rows)], sems.at[i])
            for i, (part, (first, rows)) in enumerate(zip(parts, at))
        ]

    def load(self, parts, out, whole, sems, out_sem):
        @pl.when(pl.program_id(0) == 0)
        def _():
            copies = self.copies(parts, whole, sems)
            for copy in copies:
                copy.start()
            for copy in copies:
                copy.wait()
            pltpu.make_async_copy(whole, out, out_sem).start()

    def end(self, out, whole, out_sem):
        @pl.when(pl.program_id(0) == pl.num_programs(0) - 1)
        def _():
            pltpu.make_async_copy(whole, out, out_sem).wait()


def assemble(weight):
    def kernel(*refs):
        parts, (out, whole, sems, out_sem) = refs[: weight.count], refs[weight.count :]
        weight.load(parts, out, whole, sems, out_sem)
        weight.end(out, whole, out_sem)

    return kernel_call(
        kernel, "assemble", (1,), weight.ins, weight.outs, weight.shapes, 4, scratch=weight.scratch
    )[0]


def barrier(*values):
    return lax.optimization_barrier(values)


class Gather:
    def __init__(self, own):
        self.size = lax.axis_size("seq")
        self.own = own
        half = own.shape[0] // 2
        self.now = [own[:half], own[half:]]
        self.parts = [[], []]
        self.left = self.size - 1

    def tick(self, *values):
        *self.now, first = barrier(*self.now, values[0])
        if self.left > 0:
            self.now = [
                lax.ppermute(block, "seq", route)
                for block, route in zip(self.now, ring_routes(self.size))
            ]
            for part, block in zip(self.parts, self.now):
                part.append(block)
        self.left -= 1
        return (first, *values[1:])

    @property
    def ended(self):
        return self.left < 0

    def result(self):
        return Weight(self.own, *self.parts)


class Line:
    cost = 0

    def __init__(self, token):
        self.token = token

    def run(self, function, *values, cost=0):
        *values, self.token = barrier(*values, self.token)
        Line.cost = cost
        out = function(*values)
        Line.cost = 0
        first, *rest = out if isinstance(out, (tuple, list)) else (out,)
        first, self.token = barrier(first, self.token)
        return (first, *rest) if len(rest) else first

    def send(self, block, axis, route):
        block, self.token = barrier(block, self.token)
        return lax.ppermute(block, axis, route)

    def tick(self, *rings, cost=0):
        for ring in rings:
            if not ring.ended:
                self.token = ring.go(ring.add(self.token, cost))

    def fill(self, small, cost):
        return self.run(passed, small, cost=cost)

    def meet(self, *values):
        *values, self.token = barrier(*values, self.token)
        return values


class Reduce:
    def __init__(self, ahead, back, part=(0, 0, 1)):
        self.size = lax.axis_size("seq")
        self.part = part
        self.grads = (ahead, back)
        self.place = ring_place(lax.axis_index("seq"), self.size)
        self.arrived = ()
        self.step = 0

    def add(self, token, cost=0):
        self.step += 1
        if self.arrived:
            *self.arrived, token = barrier(*self.arrived, token)
        Line.cost = cost
        self.now = ring_add(self.grads, self.arrived, self.place, self.step, *self.part)
        Line.cost = 0
        *self.now, token = barrier(*self.now, token)
        return token

    def go(self, token):
        if self.step < self.size:
            *self.now, token = barrier(*self.now, token)
            self.arrived = [
                lax.ppermute(block, "seq", route)
                for block, route in zip(self.now, ring_routes(self.size))
            ]
        return token

    @property
    def ended(self):
        return self.step >= self.size

    def result(self):
        return self.now


class Builtin:
    def __init__(self, value):
        self.value = value
        self.ended = True

    def result(self):
        return self.value


class Clock:
    def __init__(self, lanes):
        self.lanes = [[] for _ in range(lanes)]
        self.turn = 0

    def add(self, lane, chain, *values):
        self.lanes[lane].append(chain)
        if len(self.lanes[lane]) == 1:
            values = self.settle(lane, values)
        return values

    def settle(self, lane, values):
        queue = self.lanes[lane]
        while queue:
            if not queue[0].ended:
                values = queue[0].tick(*values)
            if not queue[0].ended:
                break
            queue.pop(0)
        return values

    def until(self, ring, *values):
        while any(ring in lane for lane in self.lanes):
            values = self.tick(*values)
            values = values if isinstance(values, tuple) else (values,)
        return values[0] if len(values) == 1 else values

    def tick(self, *values, count=1):
        for _ in range(count):
            for _ in self.lanes:
                lane = self.turn
                self.turn = (self.turn + 1) % len(self.lanes)
                if self.lanes[lane]:
                    values = self.settle(lane, values)
                    break
        return values[0] if len(values) == 1 else tuple(values)


def gather(own):
    if lax.axis_size("seq") > RING_MOST:
        return Builtin(Weight(lax.all_gather(own, "seq", axis=0, tiled=True)))
    return Gather(own)


def doubled(rows, distance):
    route = [(i, i ^ distance) for i in range(lax.axis_size("seq"))]
    return jnp.concatenate([rows, lax.ppermute(rows, "seq", route)], axis=0)


def reduce(ahead, back):
    if lax.axis_size("seq") > RING_MOST:
        total = [
            lax.psum_scatter(grad.astype(F32), "seq", scatter_dimension=0, tiled=True)
            for grad in (ahead, back)
        ]
        return Builtin(total)
    return Reduce(ahead, back)


def reduce_one(grad):
    if lax.axis_size("seq") > RING_MOST:
        return reduce(grad, grad[:, :0])
    return Reduce(grad, grad, (0, 1, 2))


def reduced_one(ring):
    return jnp.concatenate(ring.result(), axis=1)


def halved(line, table):
    distance = table.shape[0] // 2
    route = [(i, i ^ distance) for i in range(lax.axis_size("seq"))]
    high = (lax.axis_index("seq") // distance) % 2
    kept = lax.dynamic_slice_in_dim(table, high * distance, distance)
    sent = lax.dynamic_slice_in_dim(table, (1 - high) * distance, distance)
    return kept, line.send(sent, "seq", route)


def swap(block, bit):
    return lax.ppermute(block, "tp", [(i, i ^ bit) for i in range(lax.axis_size("tp"))])


def token_layout(first_row, row_total, lengths, offsets):
    position = first_row + jnp.arange(row_total, dtype=jnp.int32)
    inside = (position[:, None] >= offsets[None, :]) & (
        position[:, None] < offsets[None, :] + lengths[None, :]
    )
    member = inside.astype(jnp.int32)
    labels = jnp.arange(1, lengths.shape[0] + 1, dtype=jnp.int32)
    number = jnp.sum(member * labels[None, :], axis=1) - 1
    seq_start = jnp.sum(member * offsets[None, :], axis=1)
    return (number, position - seq_start)


def passing_weight(first_row, row_total, lengths, offsets, log_decay):
    before = token_layout(first_row - 1, 1, lengths, offsets)[0][0]
    last = token_layout(first_row + row_total - 1, 1, lengths, offsets)[0][0]
    return jnp.where((last == before) & (before >= 0), jnp.exp(log_decay * row_total), 0.0)


def block_decay(first_row, row_total, lengths, offsets, log_decay):
    number, within = token_layout(first_row, row_total, lengths, offsets)
    before = token_layout(first_row - 1, 1, lengths, offsets)[0][0]
    final_seq = number[row_total - 1]
    slot_index = jnp.arange(row_total).astype(jnp.float32)
    entry_weight = jnp.where(
        ((number == before) & (number >= 0))[None, :],
        jnp.exp(log_decay[:, None] * (slot_index[None, :] + 1.0)),
        0.0,
    )
    exit_weight = jnp.where(
        ((number == final_seq) & (number >= 0))[None, :],
        jnp.exp(log_decay[:, None] * (row_total - 1.0 - slot_index[None, :])),
        0.0,
    )
    half_size = KD // 2
    frequency = jnp.exp(-math.log(10000.0) * 2.0 * jnp.arange(half_size).astype(jnp.float32) / KD)
    angles = within.astype(jnp.float32)[:, None] * frequency[None, :]
    return (number, entry_weight, exit_weight, jnp.cos(angles), jnp.sin(angles))


def standardize(values):
    average = jnp.mean(values, axis=-1, keepdims=True)
    centred = values - average
    variance = jnp.mean(centred * centred, axis=-1, keepdims=True)
    scale = lax.rsqrt(variance + EPS)
    return centred * scale, scale


def standardize_back(d_normed, normed, scale):
    first = jnp.mean(d_normed, axis=-1, keepdims=True)
    second = jnp.mean(d_normed * normed, axis=-1, keepdims=True)
    return scale * (d_normed - first - normed * second)


def kernel_call(body, name, grid, ins, outs, shapes, weight, prefetch=(), vmem=24, scratch=(), stay=False):
    arrays = [a for a, _, _ in ins]
    arrays = [
        pltpu.with_memory_space_constraint(a, pltpu.HBM) if stay or block is None else a
        for a, block, _ in ins
    ]
    return pl.pallas_call(
        body,
        out_shape=[jax.ShapeDtypeStruct(s, t) for s, t in shapes],
        grid_spec=pltpu.PrefetchScalarGridSpec(
            num_scalar_prefetch=len(prefetch),
            grid=grid,
            in_specs=[spec(block, index) for _, block, index in ins],
            out_specs=[
                pl.BlockSpec(memory_space=pl.ANY) if block is None else pl.BlockSpec(block, index)
                for block, index in outs
            ],
            scratch_shapes=list(scratch),
        ),
        compiler_params=pltpu.CompilerParams(vmem_limit_bytes=vmem * 2**20),
        cost_estimate=pl.CostEstimate(
            flops=weight * 10**9 // 2 + Line.cost * 10**9, bytes_accessed=0, transcendentals=0
        ),
        name=name,
    )(*prefetch, *arrays)


def spec(block, index):
    if block is None:
        return pl.BlockSpec(memory_space=pl.ANY)
    if index in (fixed, fixed3):
        return pl.BlockSpec(block, index, pipeline_mode=pl.Buffered(1))
    return pl.BlockSpec(block, index)


def row_tile(i, *_):
    return (i, 0)


def fixed(*_):
    return (0, 0)


def fixed3(*_):
    return (0, 0, 0)


def turn(values, cosine, sine):
    low, high = values[:, : KD // 2], values[:, KD // 2 :]
    return jnp.concatenate([low * cosine - high * sine, high * cosine + low * sine], axis=1)


def norm_rows(x, gain, shift, tile=256):
    rows, width = x.shape

    def kernel(x_ref, gain_ref, shift_ref, out_ref):
        hat, _ = standardize(x_ref[...].astype(F32))
        out_ref[...] = (hat * gain_ref[...] + shift_ref[...]).astype(BF)

    return kernel_call(
        kernel,
        "first_norm",
        (rows // tile,),
        [
            (x, (tile, width), row_tile),
            (gain[None, :], (1, width), fixed),
            (shift[None, :], (1, width), fixed),
        ],
        [((tile, width), row_tile)],
        [((rows, width), BF)],
        6,
    )[0]


def project_turn(n1, weight, cosine, sine, tile=256):
    rows, width = n1.shape
    cols = weight.cols // 2

    def kernel(n1_ref, cos_ref, sin_ref, *refs):
        parts, (q_ref, k_ref, out, mat_ref, sems, out_sem) = (
            refs[: weight.count],
            refs[weight.count :],
        )
        weight.load(parts, out, mat_ref, sems, out_sem)
        raw = jnp.dot(n1_ref[...], mat_ref[...], preferred_element_type=F32)
        cos, sin = cos_ref[...], sin_ref[...]
        for at in range(0, cols, KD):
            q_ref[:, at : at + KD] = turn(raw[:, at : at + KD], cos, sin).astype(BF)
            k_ref[:, at : at + KD] = turn(raw[:, cols + at : cols + at + KD], cos, sin).astype(BF)
        weight.end(out, mat_ref, out_sem)

    return kernel_call(
        kernel,
        "query_key",
        (rows // tile,),
        [
            (n1, (tile, width), row_tile),
            (cosine, (tile, KD // 2), row_tile),
            (sine, (tile, KD // 2), row_tile),
            *weight.ins,
        ],
        [((tile, cols), row_tile)] * 2 + weight.outs,
        [((rows, cols), BF)] * 2 + weight.shapes,
        9,
        scratch=weight.scratch,
    )


def project(n1, weight, tile=256):
    rows, width = n1.shape

    def kernel(n1_ref, *refs):
        parts, (v_ref, out, mat_ref, sems, out_sem) = refs[: weight.count], refs[weight.count :]
        weight.load(parts, out, mat_ref, sems, out_sem)
        v_ref[...] = jnp.dot(n1_ref[...], mat_ref[...], preferred_element_type=F32).astype(BF)
        weight.end(out, mat_ref, out_sem)

    return kernel_call(
        kernel,
        "value",
        (rows // tile,),
        [(n1, (tile, width), row_tile), *weight.ins],
        [((tile, weight.cols), row_tile)] + weight.outs,
        [((rows, weight.cols), BF)] + weight.shapes,
        9,
        scratch=weight.scratch,
    )


def decay_block(first, count, wide, number_col, number_row, log_decay):
    distance = (
        first
        + lax.broadcasted_iota(jnp.int32, (count, wide), 0)
        - lax.broadcasted_iota(jnp.int32, (count, wide), 1)
    )
    linked = (number_col == number_row) & (number_col >= 0) & (distance >= 0)
    exponent = jnp.maximum(distance, 0).astype(F32)
    return jnp.where(linked, jnp.exp(log_decay * exponent), 0.0)


def own_column(table):
    here = lax.broadcasted_iota(jnp.int32, table.shape, 1) == pl.program_id(0)
    return jnp.sum(jnp.where(here, table, 0.0), axis=1, keepdims=True)


def retain(q, k, v, number, exit_weight, log_decay, tile=256):
    rows = q.shape[0]
    heads = q.shape[1] // KD

    def kernel(decay_ref, q_ref, k_ref, v_ref, col_ref, row_ref, exit_ref, out_ref, state_ref):
        decay = decay_ref[pl.program_id(0)]
        for first in range(0, rows, tile):
            wide = first + tile
            scores = lax.dot_general(
                q_ref[first:wide], k_ref[:wide], (((1,), (1,)), ((), ())), preferred_element_type=F32
            )
            mask = decay_block(first, tile, wide, col_ref[first:wide], row_ref[:, :wide], decay)
            out_ref[first:wide] = jnp.dot(
                (scores * mask).astype(BF), v_ref[:wide], preferred_element_type=F32
            )
        kd = (k_ref[...].astype(F32) * own_column(exit_ref[...])).astype(BF)
        state_ref[0] = lax.dot_general(
            kd, v_ref[...], (((0,), (0,)), ((), ())), preferred_element_type=F32
        )

    def head(h, *_):
        return (0, h)

    def head3(h, *_):
        return (h, 0, 0)

    return kernel_call(
        kernel,
        "retain",
        (heads,),
        [
            (q, (rows, KD), head),
            (k, (rows, KD), head),
            (v, (rows, VD), head),
            (number[:, None], (rows, 1), fixed),
            (number[None, :], (1, rows), fixed),
            (exit_weight, (rows, heads), fixed),
        ],
        [((rows, VD), head), ((1, KD, VD), head3)],
        [((rows, heads * VD), F32), ((heads, KD, VD), F32)],
        8,
        prefetch=(log_decay,),
    )


def gate_forward(n1, weight, q, entry, state, local_out, scale, shift, tile=256):
    rows, width = n1.shape
    cols = weight.cols
    heads = cols // VD

    def kernel(
        n1_ref, q_ref, entry_ref, state_ref, local_ref, scale_ref, shift_ref, *refs
    ):
        parts, (y_ref, gate_ref, hat_ref, dev_ref, out, mat_ref, sems, out_sem) = (
            refs[: weight.count],
            refs[weight.count :],
        )
        weight.load(parts, out, mat_ref, sems, out_sem)
        gate = jnp.dot(n1_ref[...], mat_ref[...], preferred_element_type=F32)
        gate_ref[...] = gate
        swish = gate * jax.nn.sigmoid(gate)
        devs = []
        for h in range(heads):
            at = slice(h * VD, (h + 1) * VD)
            qd = (q_ref[:, h * KD : (h + 1) * KD].astype(F32) * entry_ref[:, h : h + 1]).astype(BF)
            r = local_ref[:, at] + jnp.dot(qd, state_ref[h], preferred_element_type=F32)
            hat, dev = standardize(r)
            hat_ref[:, at] = hat
            devs.append(dev)
            affine = hat * scale_ref[:, at] + shift_ref[:, at]
            y_ref[:, at] = (affine * swish[:, at]).astype(BF)
        dev_ref[...] = jnp.concatenate(devs, axis=1)
        weight.end(out, mat_ref, out_sem)

    return kernel_call(
        kernel,
        "gate_forward",
        (rows // tile,),
        [
            (n1, (tile, width), row_tile),
            (q, (tile, heads * KD), row_tile),
            (entry, (tile, heads), row_tile),
            (state, state.shape, fixed3),
            (local_out, (tile, cols), row_tile),
            (scale[None, :], (1, cols), fixed),
            (shift[None, :], (1, cols), fixed),
            *weight.ins,
        ],
        [((tile, cols), row_tile)] * 3 + [((tile, heads), row_tile)] + weight.outs,
        [((rows, cols), BF), ((rows, cols), F32), ((rows, cols), F32), ((rows, heads), F32)]
        + weight.shapes,
        12,
        scratch=weight.scratch,
        vmem=32,
    )


def gate_backward(
    db_mine, db_other, side, out_mat, gate, hat, dev, scale, shift, q, entry, tile=256
):
    half, width = db_mine.shape
    rows = 2 * half
    cols = out_mat.shape[1]
    heads = cols // VD
    mine_block, other_block, pick = half_tiles(side, half // tile, tile, width)

    def kernel(
        side_ref, mine_ref, other_ref, mat_ref, gate_ref, hat_ref, dev_ref, scale_ref, shift_ref,
        q_ref, entry_ref, db_ref, dg_ref, dr_ref, gain_ref, bias_ref, state_ref, total_ref,
    ):
        pick(side_ref, mine_ref, other_ref, db_ref)

        @pl.when(pl.program_id(0) == 0)
        def _():
            gain_ref[...] = jnp.zeros_like(gain_ref)
            bias_ref[...] = jnp.zeros_like(bias_ref)
            total_ref[...] = jnp.zeros_like(total_ref)

        d_y = jnp.dot(db_ref[...], mat_ref[...], preferred_element_type=F32)
        for h in range(heads):
            at = slice(h * VD, (h + 1) * VD)
            z, dy, r_hat = gate_ref[:, at], d_y[:, at], hat_ref[:, at]
            sigma = jax.nn.sigmoid(z)
            affine = r_hat * scale_ref[:, at] + shift_ref[:, at]
            dg_ref[:, at] = (dy * affine * (sigma * (1.0 + z * (1.0 - sigma)))).astype(BF)
            d_affine = dy * (z * sigma)
            gain_ref[:, at] += jnp.sum(d_affine * r_hat, axis=0, keepdims=True)
            bias_ref[:, at] += jnp.sum(d_affine, axis=0, keepdims=True)
            d_hat = d_affine * scale_ref[:, at]
            d_r = standardize_back(d_hat, r_hat, dev_ref[:, h : h + 1]).astype(BF)
            dr_ref[:, at] = d_r
            qd = (q_ref[:, h * KD : (h + 1) * KD].astype(F32) * entry_ref[:, h : h + 1]).astype(BF)
            total_ref[h] += lax.dot_general(
                qd, d_r, (((0,), (0,)), ((), ())), preferred_element_type=F32
            )

        @pl.when(pl.program_id(0) == pl.num_programs(0) - 1)
        def _():
            state_ref[...] = total_ref[...].astype(BF)

    return kernel_call(
        kernel,
        "gate_backward",
        (rows // tile,),
        [
            (db_mine, *mine_block),
            (db_other, *other_block),
            (out_mat, (width, cols), fixed),
            (gate, (tile, cols), row_tile),
            (hat, (tile, cols), row_tile),
            (dev, (tile, heads), row_tile),
            (scale[None, :], (1, cols), fixed),
            (shift[None, :], (1, cols), fixed),
            (q, (tile, heads * KD), row_tile),
            (entry, (tile, heads), row_tile),
        ],
        [((tile, width), row_tile)] + [((tile, cols), row_tile)] * 2 + [((1, cols), fixed)] * 2
        + [((heads, KD, VD), fixed3)],
        [
            ((rows, width), BF),
            ((rows, cols), BF),
            ((rows, cols), BF),
            ((1, cols), F32),
            ((1, cols), F32),
            ((heads, KD, VD), BF),
        ],
        0,
        prefetch=(side[None],),
        scratch=[pltpu.VMEM((heads, KD, VD), F32)],
        stay=True,
    )


def half_tiles(side, steps, tile, width):
    def within(which):
        def index(i, side_ref):
            return (jnp.clip(i - (side_ref[0] ^ which) * steps, 0, steps - 1), 0)

        return index

    def pick(side_ref, mine_ref, other_ref, out_ref):
        own = pl.program_id(0) // steps == side_ref[0]

        @pl.when(own)
        def _():
            out_ref[...] = mine_ref[...].astype(out_ref.dtype)

        @pl.when(jnp.logical_not(own))
        def _():
            out_ref[...] = other_ref[...].astype(out_ref.dtype)

    return ((tile, width), within(0)), ((tile, width), within(1)), pick


def feed_forward(n2_mine, n2_other, side, up, up_shift, cotangent, down, tile=256):
    half, width = n2_mine.shape
    rows = 2 * half
    cols = up.cols
    mine_block, other_block, pick = half_tiles(side, half // tile, tile, width)

    def kernel(
        side_ref, mine_ref, other_ref, shift_ref, cot_ref, *refs
    ):
        up_parts, refs = refs[: up.count], refs[up.count :]
        down_parts, refs = refs[: down.count], refs[down.count :]
        n2_ref, act_ref, dup_ref, sum_ref, up_out, down_out, *refs = refs
        up_ref, up_sems, up_sem, down_ref, down_sems, down_sem = refs
        up.load(up_parts, up_out, up_ref, up_sems, up_sem)
        down.load(down_parts, down_out, down_ref, down_sems, down_sem)

        @pl.when(pl.program_id(0) == 0)
        def _():
            sum_ref[...] = jnp.zeros_like(sum_ref)

        pick(side_ref, mine_ref, other_ref, n2_ref)

        for at in range(0, cols, 256):
            part = slice(at, at + 256)
            z = jnp.dot(n2_ref[...], up_ref[:, part], preferred_element_type=F32)
            z = z + shift_ref[:, part]
            d_act = jnp.dot(cot_ref[...], down_ref[:, part], preferred_element_type=F32)
            half = 0.5 * (1.0 + lax.erf(z * (0.5**0.5)))
            act_ref[:, part] = (z * half).astype(BF)
            slope = half + z * (jnp.exp(-0.5 * z * z) * (1.0 / math.sqrt(2.0 * math.pi)))
            d_up = (slope * d_act).astype(BF)
            dup_ref[:, part] = d_up
            sum_ref[:, part] += jnp.sum(d_up.astype(F32), axis=0, keepdims=True)
        up.end(up_out, up_ref, up_sem)
        down.end(down_out, down_ref, down_sem)

    return kernel_call(
        kernel,
        "feed_forward",
        (rows // tile,),
        [
            (n2_mine, *mine_block),
            (n2_other, *other_block),
            (up_shift[None, :], (1, cols), fixed),
            (cotangent, (tile, width), row_tile),
            *up.ins,
            *down.ins,
        ],
        [((tile, width), row_tile)]
        + [((tile, cols), row_tile)] * 2
        + [((1, cols), fixed)]
        + up.outs
        + down.outs,
        [((rows, width), BF), ((rows, cols), BF), ((rows, cols), BF), ((1, cols), F32)]
        + up.shapes
        + down.shapes,
        16,
        scratch=up.scratch + down.scratch,
        vmem=32,
        prefetch=(side[None],),
    )


def retain_backward(q, k, v, d_r, state, number, entry, log_decay, cosine, sine, tile=256):
    rows = q.shape[0]
    heads = q.shape[1] // KD

    def kernel(
        decay_ref, q_ref, k_ref, v_ref, dr_ref, state_ref, col_ref, row_ref, entry_ref,
        cos_ref, sin_ref, dq_ref, dk_ref, dv_ref,
    ):
        decay = decay_ref[pl.program_id(0)]
        across = (((1,), (1,)), ((), ()))
        down = (((0,), (0,)), ((), ()))
        for first in reversed(range(0, rows, tile)):
            wide = first + tile
            here = slice(first, wide)
            q_i, dr_i = q_ref[here], dr_ref[here]
            mask = decay_block(first, tile, wide, col_ref[here], row_ref[:, :wide], decay)
            scores = lax.dot_general(q_i, k_ref[:wide], across, preferred_element_type=F32)
            weights = (scores * mask).astype(BF)
            d_scores = lax.dot_general(dr_i, v_ref[:wide], across, preferred_element_type=F32)
            d_scores = (d_scores * mask).astype(BF)
            dq = jnp.dot(d_scores, k_ref[:wide], preferred_element_type=F32)
            dq = dq + own_column(entry_ref[here]) * lax.dot_general(
                dr_i, state_ref[0], across, preferred_element_type=F32
            )
            dq_ref[here] = turn(dq, cos_ref[here], -sin_ref[here]).astype(BF)
            dk = lax.dot_general(d_scores, q_i, down, preferred_element_type=F32)
            dv = lax.dot_general(weights, dr_i, down, preferred_element_type=F32)
            if wide == rows:
                dk_ref[...] = dk
                dv_ref[...] = dv
            else:
                dk_ref[:wide] += dk
                dv_ref[:wide] += dv

    def head(h, *_):
        return (0, h)

    def head3(h, *_):
        return (h, 0, 0)

    return kernel_call(
        kernel,
        "retain_backward",
        (heads,),
        [
            (q, (rows, KD), head),
            (k, (rows, KD), head),
            (v, (rows, VD), head),
            (d_r, (rows, VD), head),
            (state, (1, KD, VD), head3),
            (number[:, None], (rows, 1), fixed),
            (number[None, :], (1, rows), fixed),
            (entry, (rows, heads), fixed),
            (cosine, (rows, KD // 2), fixed),
            (sine, (rows, KD // 2), fixed),
        ],
        [((rows, KD), head), ((rows, KD), head), ((rows, VD), head)],
        [((rows, heads * KD), BF), ((rows, heads * KD), F32), ((rows, heads * VD), F32)],
        0,
        prefetch=(log_decay,),
        stay=True,
    )


def state_backward(k, v, exit_weight, leaving, dk, dv, cosine, sine, tile=256):
    rows = k.shape[0]
    heads = k.shape[1] // KD

    def kernel(
        k_ref, v_ref, exit_ref, leaving_ref, dk_in, dv_in, cos_ref, sin_ref, dk_ref, dv_ref
    ):
        for h in range(heads):
            at, wide = slice(h * KD, (h + 1) * KD), slice(h * VD, (h + 1) * VD)
            weight = exit_ref[:, h : h + 1]
            kd = (k_ref[:, at].astype(F32) * weight).astype(BF)
            d_k = dk_in[:, at] + weight * lax.dot_general(
                v_ref[:, wide], leaving_ref[h], (((1,), (1,)), ((), ())), preferred_element_type=F32
            )
            dk_ref[:, at] = turn(d_k, cos_ref[...], -sin_ref[...]).astype(BF)
            d_v = dv_in[:, wide] + jnp.dot(kd, leaving_ref[h], preferred_element_type=F32)
            dv_ref[:, wide] = d_v.astype(BF)

    return kernel_call(
        kernel,
        "state_backward",
        (rows // tile,),
        [
            (k, (tile, heads * KD), row_tile),
            (v, (tile, heads * VD), row_tile),
            (exit_weight, (tile, heads), row_tile),
            (leaving, leaving.shape, fixed3),
            (dk, (tile, heads * KD), row_tile),
            (dv, (tile, heads * VD), row_tile),
            (cosine, (tile, KD // 2), row_tile),
            (sine, (tile, KD // 2), row_tile),
        ],
        [((tile, heads * KD), row_tile), ((tile, heads * VD), row_tile)],
        [((rows, heads * KD), BF), ((rows, heads * VD), BF)],
        0,
        stay=True,
    )


def second_norm(inputs, side, kept, other, gain, shift, tile=128):
    half, width = kept.shape
    steps = half // tile

    def kernel(side_ref, x_ref, kept_ref, other_ref, gain_ref, shift_ref, mid_ref, n2_ref):
        mid = x_ref[...].astype(F32) + (kept_ref[...].astype(F32) + other_ref[...].astype(F32))
        mid_ref[...] = mid
        hat, _ = standardize(mid)
        n2_ref[...] = (hat * gain_ref[...] + shift_ref[...]).astype(BF)

    return kernel_call(
        kernel,
        "second_norm",
        (steps,),
        [
            (inputs, (tile, width), lambda i, side_ref: (side_ref[0] * steps + i, 0)),
            (kept, (tile, width), row_tile),
            (other, (tile, width), row_tile),
            (gain[None, :], (1, width), fixed),
            (shift[None, :], (1, width), fixed),
        ],
        [((tile, width), row_tile)] * 2,
        [((half, width), F32), ((half, width), BF)],
        6,
        prefetch=(side[None],),
    )


def norm_backward(x, x_rows, kept, other, base, base_rows, gain, side, tile=128):
    half, width = kept.shape
    steps = half // tile

    def kernel(
        side_ref, x_ref, kept_ref, other_ref, base_ref, gain_ref,
        out_ref, low_ref, gain_out, bias_out,
    ):
        @pl.when(pl.program_id(0) == 0)
        def _():
            gain_out[...] = jnp.zeros_like(gain_out)
            bias_out[...] = jnp.zeros_like(bias_out)

        d_n = kept_ref[...].astype(F32) + other_ref[...].astype(F32)
        hat, dev = standardize(x_ref[...].astype(F32))
        gain_out[...] += jnp.sum(d_n * hat, axis=0, keepdims=True)
        bias_out[...] += jnp.sum(d_n, axis=0, keepdims=True)
        out = base_ref[...].astype(F32) + standardize_back(d_n * gain_ref[...], hat, dev)
        out_ref[...] = out
        low_ref[...] = out.astype(BF)

    def picked(i, side_ref):
        return (side_ref[0] * steps + i, 0)

    return kernel_call(
        kernel,
        "norm_backward",
        (steps,),
        [
            (x, (tile, width), picked if x_rows else row_tile),
            (kept, (tile, width), row_tile),
            (other, (tile, width), row_tile),
            (base, (tile, width), picked if base_rows else row_tile),
            (gain[None, :], (1, width), fixed),
        ],
        [((tile, width), row_tile)] * 2 + [((1, width), fixed)] * 2,
        [((half, width), F32), ((half, width), BF), ((1, width), F32), ((1, width), F32)],
        0,
        prefetch=(side[None],),
        stay=True,
    )


def partial_rows(values, mats, which, added=(), pieces=1, tile=512):
    rows, width = values[0].shape[0], mats[0][0].shape[0]
    half, count = rows // 2, len(values)

    def kernel(which_ref, *refs):
        total = sum(
            lax.dot_general(v[...], m[...], (((1,), (1,)), ((), ())), preferred_element_type=F32)
            for v, m in zip(refs[:count], refs[count : 2 * count])
        )
        if added:
            total = total + jnp.concatenate(
                [ref[...].astype(F32) for ref in refs[2 * count : 2 * count + len(added)]], axis=0
            )
        for piece, ref in enumerate(refs[-pieces:]):
            ref[...] = total[piece * half // pieces : (piece + 1) * half // pieces].astype(BF)

    def column_tile(i, *_):
        return (0, i)

    ins = [(v, (half, v.shape[1]), lambda i, which_ref: (which_ref[0], 0)) for v in values]
    ins += [
        (m, (tile, v.shape[1]), lambda i, *_, at=at: (i, at)) for v, (m, at) in zip(values, mats)
    ]
    ins += [(part, (part.shape[0], tile), column_tile) for part in added]
    return kernel_call(
        kernel,
        "partial_rows",
        (width // tile,),
        ins,
        [((half // pieces, tile), column_tile)] * pieces,
        [((half // pieces, width), BF)] * pieces,
        0,
        prefetch=(which[None],),
        stay=True,
    )


def finish_output(mid, kept, other, shift, tile=256):
    half, width = mid.shape

    def kernel(mid_ref, kept_ref, other_ref, shift_ref, out_ref):
        ffn = kept_ref[...].astype(F32) + other_ref[...].astype(F32)
        out_ref[...] = (mid_ref[...] + ffn + shift_ref[...]).astype(BF)

    return kernel_call(
        kernel,
        "finish_output",
        (half // tile,),
        [
            (mid, (tile, width), row_tile),
            (kept, (tile, width), row_tile),
            (other, (tile, width), row_tile),
            (shift[None, :], (1, width), fixed),
        ],
        [((tile, width), row_tile)],
        [((half, width), BF)],
        0,
        stay=True,
    )[0]


def passed(small):
    def kernel(in_ref, out_ref):
        out_ref[...] = in_ref[...]

    return kernel_call(
        kernel,
        "passed",
        (1,),
        [(small, small.shape, fixed)],
        [(small.shape, fixed)],
        [(small.shape, small.dtype)],
        0,
    )[0]


def both_halves(mine, other, side, kind, tile=256):
    half, width = mine.shape
    mine_block, other_block, pick = half_tiles(side, half // tile, tile, width)
    return kernel_call(
        pick,
        "both_halves",
        (2 * half // tile,),
        [(mine, *mine_block), (other, *other_block)],
        [((tile, width), row_tile)],
        [((2 * half, width), kind)],
        0,
        prefetch=(side[None],),
        stay=True,
    )[0]


def gradient(x, *dys, tile=256):
    rows, width = x.shape
    cols = [dy.shape[1] for dy in dys]

    def kernel(x_ref, *refs):
        at = 0
        for dy_ref in refs[:-1]:
            refs[-1][:, at : at + dy_ref.shape[1]] = lax.dot_general(
                x_ref[...], dy_ref[...], (((0,), (0,)), ((), ())), preferred_element_type=F32
            ).astype(BF)
            at += dy_ref.shape[1]

    return kernel_call(
        kernel,
        "gradient",
        (width // tile,),
        [(x, (rows, tile), lambda i, *_: (0, i))] + [(dy, dy.shape, fixed) for dy in dys],
        [((tile, sum(cols)), row_tile)],
        [((width, sum(cols)), BF)],
        0,
    )[0]


def ring_add(grads, arrived, place, step, left, right, parts):
    size = lax.axis_size("seq")
    rows = grads[0].shape[0] // size
    kind = BF if step < size else F32

    def kernel(place_ref, *refs):
        for i in range(2):
            total = refs[i][...].astype(F32)
            if arrived:
                total = total + refs[2 + i][...].astype(F32)
            refs[i - 2][...] = total.astype(kind)

    def own(sign, part):
        def index(i, place_ref):
            return (ring_owner(place_ref[0] + sign * step, size), part)

        return index

    blocks = [(rows, grad.shape[1] // parts) for grad in grads]
    ins = [(grads[0], blocks[0], own(-1, left)), (grads[1], blocks[1], own(1, right))]
    ins += [(block, block.shape, fixed) for block in arrived]
    return kernel_call(
        kernel,
        "ring_add",
        (1,),
        ins,
        [(block, fixed) for block in blocks],
        [(block, kind) for block in blocks],
        0,
        prefetch=(place[None],),
    )


def body(
    inputs,
    cotangent,
    lengths,
    offsets,
    first_gain,
    first_bias,
    query_weight,
    key_weight,
    value_weight,
    gate_weight,
    group_gain,
    group_bias,
    out_weight,
    second_gain,
    second_bias,
    up_weight,
    up_bias,
    down_weight,
    down_bias,
):
    size = lax.axis_size("seq")
    rows, width = inputs.shape
    shard = first_gain.shape[0]
    unit = group_gain.shape[0]
    heads = query_weight.shape[1] // KD
    half = rows // 2
    tp_me = lax.axis_index("tp")
    side = lax.rem(tp_me, 2)
    mine = side * half

    qk_own = jnp.concatenate([query_weight, key_weight], axis=1).astype(BF)
    v_own = value_weight.astype(BF)
    own_vector = jnp.concatenate(
        [
            first_gain,
            first_bias,
            second_gain,
            second_bias,
            down_bias,
            group_gain,
            group_bias,
            up_bias,
        ]
    ).astype(BF)[None, :]
    clock = Clock(2)
    qk_ring = gather(qk_own)
    v_ring = gather(v_own)
    x = inputs
    (x,) = clock.add(0, qk_ring, x)
    (x,) = clock.add(1, v_ring, x)
    g_own = gate_weight.astype(BF)
    o_own = out_weight.astype(BF).T
    u_own = up_weight.astype(BF)
    w_own = down_weight.astype(BF).T
    g_ring, o_ring, u_ring, w_ring = [gather(own) for own in (g_own, o_own, u_own, w_own)]
    for lane, ring in enumerate((g_ring, o_ring, u_ring, w_ring)):
        clock.add(lane % 2, ring)

    first_row = lax.axis_index("seq") * rows
    log_decay = jnp.log(
        1.0
        - jnp.exp2(-5.0 - (tp_me * heads + jnp.arange(heads, dtype=jnp.int32)).astype(jnp.float32))
    )
    number, entry_weight, exit_weight, cosine, sine = block_decay(
        first_row, rows, lengths, offsets, log_decay
    )
    entry_cols, exit_cols = entry_weight.T, exit_weight.T
    table = own_vector
    distance = 1
    while distance < size:
        table = doubled(table, distance)
        x, table = clock.tick(x, table, count=2)
        distance *= 2
    table = table[jnp.arange(size) ^ lax.axis_index("seq")].astype(F32)

    def wide(i):
        return table[:, i * shard : (i + 1) * shard].reshape(-1)

    def narrow(i):
        start = 5 * shard + i * unit
        return table[:, start : start + unit].reshape(-1)

    gain_one, bias_one, gain_two, bias_two, down_shift = [wide(i) for i in range(5)]
    group_scale, group_shift, up_shift = [narrow(i) for i in range(3)]

    n1 = norm_rows(x, gain_one, bias_one)
    grad_down_bias = jnp.sum(cotangent.astype(F32), axis=0)
    n1, grad_down_bias = barrier(n1, grad_down_bias)
    n1, cosine, sine, number, entry_cols, exit_cols = clock.tick(
        n1, cosine, sine, number, entry_cols, exit_cols
    )
    n1 = clock.until(v_ring, n1)

    n1 = clock.tick(n1)
    q, k, qk_mat = project_turn(n1, qk_ring.result(), cosine, sine)
    q, k, n1 = clock.tick(q, k, n1, count=2)
    v, v_mat = project(n1, v_ring.result())
    v, q, k = clock.tick(v, q, k, count=2)
    local_out, local_state = retain(q, k, v, number, exit_cols, log_decay)
    local_out, local_state = clock.tick(local_out, local_state)
    state_parts = Others(local_state.astype(BF), 1).second()
    local_out = clock.until(o_ring, local_out)

    def gathered_state(first, rest, direction):
        total, weight = first.astype(F32), 1.0
        for turn, part in enumerate(rest, 1):
            block = first_row - direction * turn * rows
            passed = passing_weight(block, rows, lengths, offsets, log_decay)
            weight = weight * passed
            total = total + weight[:, None, None] * part.astype(F32)
        return total.astype(BF)

    state = gathered_state(state_parts[0], state_parts[1:], 1)
    state, local_out = barrier(state, local_out)
    state = clock.tick(state)
    y, gate, r_hat, r_dev, g_mat = gate_forward(
        n1, g_ring.result(), q, entry_cols, state, local_out, group_scale, group_shift
    )
    y = clock.tick(y, count=2)
    o_mat = assemble(o_ring.result())
    y, o_mat = clock.tick(y, o_mat)

    def pick(values, which):
        return lax.dynamic_slice_in_dim(values, which * half, half)

    def tp_first(make, value):
        sent = make(pick(value, 1 - side)).astype(BF)
        sent, value = clock.tick(sent, value)
        sent = swap(sent, 1)
        return (make(pick(value, side)) + sent.astype(F32)).astype(BF)

    kept = tp_first(lambda part: dot(part, o_mat, ((1,), (1,))), y)
    kept = clock.tick(kept)
    other = swap(kept, 2)
    kept = clock.tick(kept, count=7)
    kept, other = barrier(kept, other)
    mid, n2_mine = second_norm(inputs, side, kept, other, gain_two, bias_two)
    n2_other = swap(n2_mine, 1)
    n2_mine, n2_other = barrier(n2_mine, n2_other)
    n2_mine, n2_other = clock.until(w_ring, n2_mine, n2_other)
    n2, act, d_up, grad_up_bias, u_mat, w_mat = feed_forward(
        n2_mine, n2_other, side, u_ring.result(), up_shift, cotangent, w_ring.result()
    )

    line = Line(grad_up_bias)
    pairs_two = [(i, i ^ 2) for i in range(lax.axis_size("tp"))]
    pairs_one = [(i, i ^ 1) for i in range(lax.axis_size("tp"))]

    def to_partner(block, pieces=2):
        count = block.shape[0] // pieces
        return [
            line.send(block[i * count : (i + 1) * count], "tp", pairs_one) for i in range(pieces)
        ]

    def partial_sent(values, mats, pieces=2, cost=0):
        parts = line.run(
            lambda *v: partial_rows(v, mats, 1 - side, pieces=pieces), *values, cost=cost
        )
        parts = parts if isinstance(parts, tuple) else (parts,)
        return [line.send(part, "tp", pairs_one) for part in parts]

    def partial_kept(values, mats, sent, cost=0):
        return line.run(lambda *v: partial_rows(v, mats, side, sent), *values, cost=cost)

    sent_two = partial_sent((d_up,), ((u_mat, 0),), 1)
    grad_w = line.run(gradient, cotangent, act, cost=23)
    kept_two = partial_kept((d_up,), ((u_mat, 0),), sent_two)
    other_two = line.send(kept_two, "tp", pairs_two)
    grad_u = line.run(gradient, n2, d_up, cost=23)
    wu_back = reduce(grad_w, grad_u)
    line.tick(wu_back, wu_back, wu_back)
    d_mid, d_branch_mine, grad_second_gain, grad_second_bias = line.run(
        lambda kept, other: norm_backward(
            mid, False, kept, other, cotangent, True, gain_two, side
        ),
        kept_two,
        other_two,
        cost=6,
    )
    d_branch_other = to_partner(d_branch_mine, 1)[0]
    line.tick(wu_back, cost=23)

    d_branch, d_gate, d_r, grad_group_gain, grad_group_bias, own_grad = line.run(
        lambda mine, other: gate_backward(
            mine,
            other,
            side,
            o_mat,
            gate,
            r_hat,
            r_dev,
            group_scale,
            group_shift,
            q,
            entry_cols,
        ),
        d_branch_mine,
        d_branch_other,
        cost=6,
    )
    others = Others(own_grad, -1, line.send)
    d_q, d_k, d_v = line.run(
        lambda d_r: retain_backward(
            q, k, v, d_r, state, number, entry_cols, log_decay, cosine, sine
        ),
        d_r,
        cost=6,
    )
    leaving_parts = others.second()
    line.tick(wu_back)
    grad_o = line.run(gradient, d_branch, y, cost=6)
    grad_g = line.run(gradient, n1, d_gate)
    line.tick(wu_back)
    og_back = reduce(grad_o, grad_g)
    line.tick(og_back)
    leaving = line.run(lambda first, *rest: gathered_state(first, rest, -1), *leaving_parts)
    d_k, d_v = line.run(
        lambda d_k, d_v: state_backward(k, v, exit_cols, leaving, d_k, d_v, cosine, sine),
        d_k,
        d_v,
        cost=6,
    )
    grad_v = line.run(gradient, n1, d_v)
    line.tick(wu_back, og_back)
    grad_qk = line.run(gradient, n1, d_q, d_k, cost=6)
    line.tick(wu_back)
    vqk_back = reduce(grad_v, grad_qk)
    line.tick(vqk_back)
    d_all = (d_gate, d_v, d_q, d_k)
    mats_all = ((g_mat, 0), (v_mat, 0), (qk_mat, 0), (qk_mat, 1))
    sent_one = partial_sent(d_all, mats_all, 1, cost=6)
    grad_second_gain = line.fill(grad_second_gain, 23)
    line.tick(og_back, vqk_back)
    kept_one = partial_kept(d_all, mats_all, sent_one, cost=6)
    other_one = line.send(kept_one, "tp", pairs_two)
    grad_second_gain = line.fill(grad_second_gain, 23)
    line.tick(og_back, vqk_back)
    line.tick(og_back, vqk_back)
    _, grad_mine, grad_first_gain, grad_first_bias = line.run(
        lambda kept, other: norm_backward(
            inputs, True, kept, other, d_mid, False, gain_one, side
        ),
        kept_one,
        other_one,
        cost=6,
    )
    grad_other = to_partner(grad_mine, 1)[0]
    sent_out = partial_sent((act,), ((w_mat, 0),), 1, cost=23)
    line.tick(og_back, vqk_back, cost=12)
    grad_inputs = line.run(
        lambda mine, other: both_halves(mine, other, side, F32), grad_mine, grad_other
    )
    kept_out = partial_kept((act,), ((w_mat, 0),), sent_out)
    other_out = line.send(kept_out, "tp", pairs_two)
    grad_second_gain = line.fill(grad_second_gain, 23)
    line.tick(og_back, vqk_back)

    grad_up_bias = line.token
    table = jnp.concatenate(
        [
            vector.reshape(size, -1)
            for vector in (
                grad_first_gain,
                grad_first_bias,
                grad_second_gain,
                grad_second_bias,
                grad_down_bias,
                grad_group_gain,
                grad_group_bias,
                grad_up_bias,
            )
        ],
        axis=1,
    )
    line.token = grad_inputs
    table, sent = halved(line, table)
    line.tick(vqk_back, og_back)
    while table.shape[0] > 1:
        table = line.run(lambda kept, sent: kept + sent, table, sent)
        table, sent = halved(line, table)
        line.tick(vqk_back, og_back)
    small = line.run(lambda kept, sent: kept + sent, table, sent)[0]
    halves = small[: 4 * shard]
    sent = line.send(halves, "tp", pairs_one)
    output_mine = line.run(
        lambda kept, other: finish_output(mid, kept, other, down_shift), kept_out, other_out
    )
    output_other = to_partner(output_mine, 1)[0]
    while not (og_back.ended and vqk_back.ended):
        line.tick(vqk_back, og_back)
    output = line.run(
        lambda mine, other: both_halves(mine, other, side, BF), output_mine, output_other
    )
    halves = halves + sent
    grad_inputs = line.token
    own = [halves[i * shard : (i + 1) * shard] for i in range(4)]
    own_down_bias = small[4 * shard : 5 * shard]
    own_units = [small[5 * shard + i * unit : 5 * shard + (i + 1) * unit] for i in range(3)]
    own_w, own_u = wu_back.result()
    own_o, own_g = og_back.result()
    own_v, own_qk = vqk_back.result()
    own_q, own_k = own_qk[:, : heads * KD], own_qk[:, heads * KD :]
    return (
        output,
        grad_inputs,
        own[0],
        own[1],
        own_q,
        own_k,
        own_v,
        own_g,
        own_units[0],
        own_units[1],
        own_o.T,
        own[2],
        own[3],
        own_u,
        own_units[2],
        own_w.T,
        own_down_bias,
    )


def solution(mesh):
    placed = (
        P("seq", None),
        P("seq", None),
        P(),
        P(),
        P("seq"),
        P("seq"),
        P("seq", "tp"),
        P("seq", "tp"),
        P("seq", "tp"),
        P("seq", "tp"),
        P(("tp", "seq")),
        P(("tp", "seq")),
        P("tp", "seq"),
        P("seq"),
        P("seq"),
        P("seq", "tp"),
        P(("tp", "seq")),
        P("tp", "seq"),
        P("seq"),
    )
    return jax.shard_map(
        body,
        mesh=mesh,
        in_specs=placed,
        out_specs=(
            P("seq", None),
            P("seq", None),
            P("seq"),
            P("seq"),
            P("seq", "tp"),
            P("seq", "tp"),
            P("seq", "tp"),
            P("seq", "tp"),
            P(("tp", "seq")),
            P(("tp", "seq")),
            P("tp", "seq"),
            P("seq"),
            P("seq"),
            P("seq", "tp"),
            P(("tp", "seq")),
            P("tp", "seq"),
            P("seq"),
        ),
        check_vma=False,
    )
```

```python
import math

import jax
import jax.numpy as jnp
from jax import lax
from jax.experimental import pallas as pl
from jax.experimental.pallas import tpu as pltpu
from jax.sharding import PartitionSpec as P

KD = 256
VD = 512
EPS = 1e-05
BF = jnp.bfloat16
F32 = jnp.float32
RING_MOST = 16


def dot(a, b, dims):
    return lax.dot_general(a, b, (dims, ((), ())), preferred_element_type=F32)


class Others:
    def __init__(self, block, direction, send=lax.ppermute):
        self.size = lax.axis_size("seq")
        self.block, self.direction, self.send = block, direction, send
        turns = max(1, self.size // 4)
        self.paired = turns == 2
        steps = [2] if self.paired else range(1, turns + 1)
        self.parts = [self.shift(direction * step) for step in steps]

    def shift(self, distance):
        route = [(i, i + distance) for i in range(self.size) if 0 <= i + distance < self.size]
        return self.send(self.block, "seq", route)

    def second(self):
        if self.paired:
            (far,) = self.parts
            first = lax.rem(lax.axis_index("seq"), 2) == (0 if self.direction > 0 else 1)
            near = jnp.where(first, self.block, far)
            near = self.send(near, "seq", [(i, i ^ 1) for i in range(self.size)])
            self.parts = [near, far]
        return self.parts


def ring_owner(place, size):
    place = lax.rem(place + 2 * size, size)
    return jnp.where(place < size // 2, 2 * place, 2 * (size - 1 - place) + 1)


def ring_place(index, size):
    return jnp.where(index % 2 == 0, index // 2, size - 1 - index // 2)


def ring_routes(size):
    order = list(range(0, size, 2)) + list(range(size - 1, 0, -2))
    ahead = [(order[i], order[(i + 1) % size]) for i in range(size)]
    return ahead, [(b, a) for a, b in ahead]


class Weight:
    def __init__(self, own, parts=(), sign=0):
        self.size = len(parts) + 1
        self.rows, self.cols = own.shape
        self.arrays = [own, *parts]
        self.count, self.sign = self.size, sign
        self.shape = (self.size * self.rows, self.cols)
        self.ins = [(array, None, None) for array in self.arrays]
        self.outs = [(None, None)]
        self.shapes = [(self.shape, own.dtype)]
        self.scratch = [
            pltpu.VMEM(self.shape, own.dtype),
            pltpu.SemaphoreType.DMA((self.count,)),
            pltpu.SemaphoreType.DMA,
        ]

    def copies(self, parts, whole, sems):
        if self.size == 1:
            return [pltpu.make_async_copy(parts[0], whole, sems.at[0])]
        place = ring_place(lax.axis_index("seq"), self.size)
        owners = [ring_owner(place + self.sign * k, self.size) for k in range(self.size)]
        return [
            pltpu.make_async_copy(part, whole.at[pl.ds(owner * self.rows, self.rows)], sems.at[i])
            for i, (part, owner) in enumerate(zip(parts, owners))
        ]

    def load(self, parts, out, whole, sems, out_sem):
        @pl.when(pl.program_id(0) == 0)
        def _():
            copies = self.copies(parts, whole, sems)
            for copy in copies:
                copy.start()
            for copy in copies:
                copy.wait()
            pltpu.make_async_copy(whole, out, out_sem).start()

    def end(self, out, whole, out_sem):
        @pl.when(pl.program_id(0) == pl.num_programs(0) - 1)
        def _():
            pltpu.make_async_copy(whole, out, out_sem).wait()


def assemble(weight):
    def kernel(*refs):
        parts, (out, whole, sems, out_sem) = refs[: weight.count], refs[weight.count :]
        weight.load(parts, out, whole, sems, out_sem)
        weight.end(out, whole, out_sem)

    return kernel_call(
        kernel, "assemble", (1,), weight.ins, weight.outs, weight.shapes, 4, scratch=weight.scratch
    )[0]


def barrier(*values):
    return lax.optimization_barrier(values)


class Gather:
    def __init__(self, ahead, back):
        self.size = lax.axis_size("seq")
        self.own = self.now = [ahead, back]
        self.parts = [[], []]
        self.left = self.size - 1

    def tick(self, *values):
        *self.now, first = barrier(*self.now, values[0])
        if self.left > 0:
            self.now = [
                lax.ppermute(block, "seq", route)
                for block, route in zip(self.now, ring_routes(self.size))
            ]
            for part, block in zip(self.parts, self.now):
                part.append(block)
        self.left -= 1
        return (first, *values[1:])

    @property
    def ended(self):
        return self.left < 0

    def result(self):
        return [
            Weight(own, parts, sign) for own, parts, sign in zip(self.own, self.parts, (-1, 1))
        ]


class Line:
    cost = 0

    def __init__(self, token):
        self.token = token

    def run(self, function, *values, cost=0):
        *values, self.token = barrier(*values, self.token)
        Line.cost = cost
        out = function(*values)
        Line.cost = 0
        first, *rest = out if isinstance(out, (tuple, list)) else (out,)
        first, self.token = barrier(first, self.token)
        return (first, *rest) if len(rest) else first

    def send(self, block, axis, route):
        block, self.token = barrier(block, self.token)
        return lax.ppermute(block, axis, route)

    def tick(self, *rings, cost=0):
        for ring in rings:
            if not ring.ended:
                self.token = ring.go(ring.add(self.token, cost))

    def fill(self, small, cost):
        return self.run(passed, small, cost=cost)

    def meet(self, *values):
        *values, self.token = barrier(*values, self.token)
        return values


class Reduce:
    def __init__(self, ahead, back, turned, cut):
        self.size = lax.axis_size("seq")
        self.grads = (ahead, back)
        self.form = (turned, cut)
        self.place = ring_place(lax.axis_index("seq"), self.size)
        self.arrived = ()
        self.step = 0

    def add(self, token, cost=0):
        self.step += 1
        if self.arrived:
            *self.arrived, token = barrier(*self.arrived, token)
        Line.cost = cost
        self.now = ring_add(self.grads, self.arrived, self.place, self.step, *self.form)
        Line.cost = 0
        *self.now, token = barrier(*self.now, token)
        return token

    def go(self, token):
        if self.step < self.size:
            *self.now, token = barrier(*self.now, token)
            self.arrived = [
                lax.ppermute(block, "seq", route)
                for block, route in zip(self.now, ring_routes(self.size))
            ]
        return token

    @property
    def ended(self):
        return self.step >= self.size

    def result(self):
        return self.now


class Builtin:
    def __init__(self, value):
        self.value = value
        self.ended = True

    def result(self):
        return self.value


class Clock:
    def __init__(self, *rings):
        self.queue = [(ring, left) for ring, left in rings if not ring.ended]
        self.active = []
        self.turn = 0

    def tick(self, *values, count=1):
        for _ in range(count):
            if self.queue and (not self.active or self.active[-1].left <= self.queue[0][1]):
                self.active.append(self.queue.pop(0)[0])
                values = self.active[-1].tick(*values)
            elif self.active:
                self.turn = (self.turn + 1) % len(self.active)
                ring = self.active[self.turn]
                values = ring.tick(*values)
                if ring.ended:
                    self.active.remove(ring)
        return values[0] if len(values) == 1 else tuple(values)

    def until(self, ring, *values):
        while not ring.ended:
            values = self.tick(*values)
            values = values if isinstance(values, tuple) else (values,)
        return values[0] if len(values) == 1 else values


def gather(ahead, back):
    if lax.axis_size("seq") > RING_MOST:
        return Builtin(
            [Weight(lax.all_gather(own, "seq", axis=0, tiled=True)) for own in (ahead, back)]
        )
    return Gather(ahead, back)


def doubled(rows, distance):
    route = [(i, i ^ distance) for i in range(lax.axis_size("seq"))]
    return jnp.concatenate([rows, lax.ppermute(rows, "seq", route)], axis=0)


def reduce(ahead, back, turned=False, cut=False):
    if lax.axis_size("seq") > RING_MOST:
        first, second = [
            lax.psum_scatter(grad.astype(F32), "seq", scatter_dimension=0, tiled=True)
            for grad in (ahead, back)
        ]
        first = first.T if turned else first
        return Builtin([first, *jnp.split(second, 2, axis=1)] if cut else [first, second])
    return Reduce(ahead, back, turned, cut)


def halved(line, table):
    distance = table.shape[0] // 2
    route = [(i, i ^ distance) for i in range(lax.axis_size("seq"))]
    high = (lax.axis_index("seq") // distance) % 2
    kept = lax.dynamic_slice_in_dim(table, high * distance, distance)
    sent = lax.dynamic_slice_in_dim(table, (1 - high) * distance, distance)
    return kept, line.send(sent, "seq", route)


def swap(block, bit):
    return lax.ppermute(block, "tp", [(i, i ^ bit) for i in range(lax.axis_size("tp"))])


def token_layout(first_row, row_total, lengths, offsets):
    position = first_row + jnp.arange(row_total, dtype=jnp.int32)
    inside = (position[:, None] >= offsets[None, :]) & (
        position[:, None] < offsets[None, :] + lengths[None, :]
    )
    member = inside.astype(jnp.int32)
    labels = jnp.arange(1, lengths.shape[0] + 1, dtype=jnp.int32)
    number = jnp.sum(member * labels[None, :], axis=1) - 1
    seq_start = jnp.sum(member * offsets[None, :], axis=1)
    return (number, position - seq_start)


def passing_weight(first_row, row_total, lengths, offsets, log_decay):
    before = token_layout(first_row - 1, 1, lengths, offsets)[0][0]
    last = token_layout(first_row + row_total - 1, 1, lengths, offsets)[0][0]
    return jnp.where((last == before) & (before >= 0), jnp.exp(log_decay * row_total), 0.0)


def block_decay(first_row, row_total, lengths, offsets, log_decay):
    number, within = token_layout(first_row, row_total, lengths, offsets)
    before = token_layout(first_row - 1, 1, lengths, offsets)[0][0]
    final_seq = number[row_total - 1]
    slot_index = jnp.arange(row_total).astype(jnp.float32)
    entry_weight = jnp.where(
        ((number == before) & (number >= 0))[None, :],
        jnp.exp(log_decay[:, None] * (slot_index[None, :] + 1.0)),
        0.0,
    )
    exit_weight = jnp.where(
        ((number == final_seq) & (number >= 0))[None, :],
        jnp.exp(log_decay[:, None] * (row_total - 1.0 - slot_index[None, :])),
        0.0,
    )
    half_size = KD // 2
    frequency = jnp.exp(-math.log(10000.0) * 2.0 * jnp.arange(half_size).astype(jnp.float32) / KD)
    angles = within.astype(jnp.float32)[:, None] * frequency[None, :]
    return (number, entry_weight, exit_weight, jnp.cos(angles), jnp.sin(angles))


def standardize(values):
    average = jnp.mean(values, axis=-1, keepdims=True)
    centred = values - average
    variance = jnp.mean(centred * centred, axis=-1, keepdims=True)
    scale = lax.rsqrt(variance + EPS)
    return centred * scale, scale


def standardize_back(d_normed, normed, scale):
    first = jnp.mean(d_normed, axis=-1, keepdims=True)
    second = jnp.mean(d_normed * normed, axis=-1, keepdims=True)
    return scale * (d_normed - first - normed * second)


def kernel_call(body, name, grid, ins, outs, shapes, weight, prefetch=(), vmem=24, scratch=(), stay=False):
    arrays = [a for a, _, _ in ins]
    arrays = [
        pltpu.with_memory_space_constraint(a, pltpu.HBM) if stay or block is None else a
        for a, block, _ in ins
    ]
    return pl.pallas_call(
        body,
        out_shape=[jax.ShapeDtypeStruct(s, t) for s, t in shapes],
        grid_spec=pltpu.PrefetchScalarGridSpec(
            num_scalar_prefetch=len(prefetch),
            grid=grid,
            in_specs=[spec(block, index) for _, block, index in ins],
            out_specs=[
                pl.BlockSpec(memory_space=pl.ANY) if block is None else pl.BlockSpec(block, index)
                for block, index in outs
            ],
            scratch_shapes=list(scratch),
        ),
        compiler_params=pltpu.CompilerParams(vmem_limit_bytes=vmem * 2**20),
        cost_estimate=pl.CostEstimate(
            flops=weight * 10**9 // 2 + Line.cost * 10**9, bytes_accessed=0, transcendentals=0
        ),
        name=name,
    )(*prefetch, *arrays)


def spec(block, index):
    if block is None:
        return pl.BlockSpec(memory_space=pl.ANY)
    if index in (fixed, fixed3):
        return pl.BlockSpec(block, index, pipeline_mode=pl.Buffered(1))
    return pl.BlockSpec(block, index)


def row_tile(i, *_):
    return (i, 0)


def fixed(*_):
    return (0, 0)


def fixed3(*_):
    return (0, 0, 0)


def turn(values, cosine, sine):
    low, high = values[:, : KD // 2], values[:, KD // 2 :]
    return jnp.concatenate([low * cosine - high * sine, high * cosine + low * sine], axis=1)


def norm_rows(x, gain, shift, tile=256):
    rows, width = x.shape

    def kernel(x_ref, gain_ref, shift_ref, out_ref):
        hat, _ = standardize(x_ref[...].astype(F32))
        out_ref[...] = (hat * gain_ref[...] + shift_ref[...]).astype(BF)

    return kernel_call(
        kernel,
        "first_norm",
        (rows // tile,),
        [
            (x, (tile, width), row_tile),
            (gain[None, :], (1, width), fixed),
            (shift[None, :], (1, width), fixed),
        ],
        [((tile, width), row_tile)],
        [((rows, width), BF)],
        6,
    )[0]


def project_turn(n1, weight, cosine, sine, tile=256):
    rows, width = n1.shape
    cols = weight.cols // 2

    def kernel(n1_ref, cos_ref, sin_ref, *refs):
        parts, (q_ref, k_ref, out, mat_ref, sems, out_sem) = (
            refs[: weight.count],
            refs[weight.count :],
        )
        weight.load(parts, out, mat_ref, sems, out_sem)
        raw = jnp.dot(n1_ref[...], mat_ref[...], preferred_element_type=F32)
        cos, sin = cos_ref[...], sin_ref[...]
        for at in range(0, cols, KD):
            q_ref[:, at : at + KD] = turn(raw[:, at : at + KD], cos, sin).astype(BF)
            k_ref[:, at : at + KD] = turn(raw[:, cols + at : cols + at + KD], cos, sin).astype(BF)
        weight.end(out, mat_ref, out_sem)

    return kernel_call(
        kernel,
        "query_key",
        (rows // tile,),
        [
            (n1, (tile, width), row_tile),
            (cosine, (tile, KD // 2), row_tile),
            (sine, (tile, KD // 2), row_tile),
            *weight.ins,
        ],
        [((tile, cols), row_tile)] * 2 + weight.outs,
        [((rows, cols), BF)] * 2 + weight.shapes,
        9,
        scratch=weight.scratch,
    )


def project(n1, weight, tile=256):
    rows, width = n1.shape

    def kernel(n1_ref, *refs):
        parts, (v_ref, out, mat_ref, sems, out_sem) = refs[: weight.count], refs[weight.count :]
        weight.load(parts, out, mat_ref, sems, out_sem)
        v_ref[...] = jnp.dot(n1_ref[...], mat_ref[...], preferred_element_type=F32).astype(BF)
        weight.end(out, mat_ref, out_sem)

    return kernel_call(
        kernel,
        "value",
        (rows // tile,),
        [(n1, (tile, width), row_tile), *weight.ins],
        [((tile, weight.cols), row_tile)] + weight.outs,
        [((rows, weight.cols), BF)] + weight.shapes,
        9,
        scratch=weight.scratch,
    )


def decay_block(first, count, wide, number_col, number_row, log_decay):
    distance = (
        first
        + lax.broadcasted_iota(jnp.int32, (count, wide), 0)
        - lax.broadcasted_iota(jnp.int32, (count, wide), 1)
    )
    linked = (number_col == number_row) & (number_col >= 0) & (distance >= 0)
    exponent = jnp.maximum(distance, 0).astype(F32)
    return jnp.where(linked, jnp.exp(log_decay * exponent), 0.0)


def own_column(table):
    here = lax.broadcasted_iota(jnp.int32, table.shape, 1) == pl.program_id(0)
    return jnp.sum(jnp.where(here, table, 0.0), axis=1, keepdims=True)


def retain(q, k, v, number, exit_weight, log_decay, tile=256):
    rows = q.shape[0]
    heads = q.shape[1] // KD

    def kernel(decay_ref, q_ref, k_ref, v_ref, col_ref, row_ref, exit_ref, out_ref, state_ref):
        decay = decay_ref[pl.program_id(0)]
        for first in range(0, rows, tile):
            wide = first + tile
            scores = lax.dot_general(
                q_ref[first:wide], k_ref[:wide], (((1,), (1,)), ((), ())), preferred_element_type=F32
            )
            mask = decay_block(first, tile, wide, col_ref[first:wide], row_ref[:, :wide], decay)
            out_ref[first:wide] = jnp.dot(
                (scores * mask).astype(BF), v_ref[:wide], preferred_element_type=F32
            )
        kd = (k_ref[...].astype(F32) * own_column(exit_ref[...])).astype(BF)
        state_ref[0] = lax.dot_general(
            kd, v_ref[...], (((0,), (0,)), ((), ())), preferred_element_type=F32
        )

    def head(h, *_):
        return (0, h)

    def head3(h, *_):
        return (h, 0, 0)

    return kernel_call(
        kernel,
        "retain",
        (heads,),
        [
            (q, (rows, KD), head),
            (k, (rows, KD), head),
            (v, (rows, VD), head),
            (number[:, None], (rows, 1), fixed),
            (number[None, :], (1, rows), fixed),
            (exit_weight, (rows, heads), fixed),
        ],
        [((rows, VD), head), ((1, KD, VD), head3)],
        [((rows, heads * VD), F32), ((heads, KD, VD), F32)],
        8,
        prefetch=(log_decay,),
    )


def gate_forward(n1, weight, q, entry, state, local_out, scale, shift, tile=256):
    rows, width = n1.shape
    cols = weight.cols
    heads = cols // VD

    def kernel(
        n1_ref, q_ref, entry_ref, state_ref, local_ref, scale_ref, shift_ref, *refs
    ):
        parts, (y_ref, gate_ref, hat_ref, dev_ref, out, mat_ref, sems, out_sem) = (
            refs[: weight.count],
            refs[weight.count :],
        )
        weight.load(parts, out, mat_ref, sems, out_sem)
        gate = jnp.dot(n1_ref[...], mat_ref[...], preferred_element_type=F32)
        gate_ref[...] = gate
        swish = gate * jax.nn.sigmoid(gate)
        devs = []
        for h in range(heads):
            at = slice(h * VD, (h + 1) * VD)
            qd = (q_ref[:, h * KD : (h + 1) * KD].astype(F32) * entry_ref[:, h : h + 1]).astype(BF)
            r = local_ref[:, at] + jnp.dot(qd, state_ref[h], preferred_element_type=F32)
            hat, dev = standardize(r)
            hat_ref[:, at] = hat
            devs.append(dev)
            affine = hat * scale_ref[:, at] + shift_ref[:, at]
            y_ref[:, at] = (affine * swish[:, at]).astype(BF)
        dev_ref[...] = jnp.concatenate(devs, axis=1)
        weight.end(out, mat_ref, out_sem)

    return kernel_call(
        kernel,
        "gate_forward",
        (rows // tile,),
        [
            (n1, (tile, width), row_tile),
            (q, (tile, heads * KD), row_tile),
            (entry, (tile, heads), row_tile),
            (state, state.shape, fixed3),
            (local_out, (tile, cols), row_tile),
            (scale[None, :], (1, cols), fixed),
            (shift[None, :], (1, cols), fixed),
            *weight.ins,
        ],
        [((tile, cols), row_tile)] * 3 + [((tile, heads), row_tile)] + weight.outs,
        [((rows, cols), BF), ((rows, cols), F32), ((rows, cols), F32), ((rows, heads), F32)]
        + weight.shapes,
        12,
        scratch=weight.scratch,
        vmem=32,
    )


def gate_backward(
    db_mine, db_other, side, out_mat, gate, hat, dev, scale, shift, q, entry, tile=256
):
    half, width = db_mine.shape
    rows = 2 * half
    cols = out_mat.shape[1]
    heads = cols // VD
    mine_block, other_block, pick = half_tiles(side, half // tile, tile, width)

    def kernel(
        side_ref, mine_ref, other_ref, mat_ref, gate_ref, hat_ref, dev_ref, scale_ref, shift_ref,
        q_ref, entry_ref, db_ref, dg_ref, dr_ref, gain_ref, bias_ref, state_ref, total_ref,
    ):
        pick(side_ref, mine_ref, other_ref, db_ref)

        @pl.when(pl.program_id(0) == 0)
        def _():
            gain_ref[...] = jnp.zeros_like(gain_ref)
            bias_ref[...] = jnp.zeros_like(bias_ref)
            total_ref[...] = jnp.zeros_like(total_ref)

        d_y = jnp.dot(db_ref[...], mat_ref[...], preferred_element_type=F32)
        for h in range(heads):
            at = slice(h * VD, (h + 1) * VD)
            z, dy, r_hat = gate_ref[:, at], d_y[:, at], hat_ref[:, at]
            sigma = jax.nn.sigmoid(z)
            affine = r_hat * scale_ref[:, at] + shift_ref[:, at]
            dg_ref[:, at] = (dy * affine * (sigma * (1.0 + z * (1.0 - sigma)))).astype(BF)
            d_affine = dy * (z * sigma)
            gain_ref[:, at] += jnp.sum(d_affine * r_hat, axis=0, keepdims=True)
            bias_ref[:, at] += jnp.sum(d_affine, axis=0, keepdims=True)
            d_hat = d_affine * scale_ref[:, at]
            d_r = standardize_back(d_hat, r_hat, dev_ref[:, h : h + 1]).astype(BF)
            dr_ref[:, at] = d_r
            qd = (q_ref[:, h * KD : (h + 1) * KD].astype(F32) * entry_ref[:, h : h + 1]).astype(BF)
            total_ref[h] += lax.dot_general(
                qd, d_r, (((0,), (0,)), ((), ())), preferred_element_type=F32
            )

        @pl.when(pl.program_id(0) == pl.num_programs(0) - 1)
        def _():
            state_ref[...] = total_ref[...].astype(BF)

    return kernel_call(
        kernel,
        "gate_backward",
        (rows // tile,),
        [
            (db_mine, *mine_block),
            (db_other, *other_block),
            (out_mat, (width, cols), fixed),
            (gate, (tile, cols), row_tile),
            (hat, (tile, cols), row_tile),
            (dev, (tile, heads), row_tile),
            (scale[None, :], (1, cols), fixed),
            (shift[None, :], (1, cols), fixed),
            (q, (tile, heads * KD), row_tile),
            (entry, (tile, heads), row_tile),
        ],
        [((tile, width), row_tile)] + [((tile, cols), row_tile)] * 2 + [((1, cols), fixed)] * 2
        + [((heads, KD, VD), fixed3)],
        [
            ((rows, width), BF),
            ((rows, cols), BF),
            ((rows, cols), BF),
            ((1, cols), F32),
            ((1, cols), F32),
            ((heads, KD, VD), BF),
        ],
        0,
        prefetch=(side[None],),
        scratch=[pltpu.VMEM((heads, KD, VD), F32)],
        stay=True,
    )


def half_tiles(side, steps, tile, width):
    def within(which):
        def index(i, side_ref):
            return (jnp.clip(i - (side_ref[0] ^ which) * steps, 0, steps - 1), 0)

        return index

    def pick(side_ref, mine_ref, other_ref, out_ref):
        own = pl.program_id(0) // steps == side_ref[0]

        @pl.when(own)
        def _():
            out_ref[...] = mine_ref[...].astype(out_ref.dtype)

        @pl.when(jnp.logical_not(own))
        def _():
            out_ref[...] = other_ref[...].astype(out_ref.dtype)

    return ((tile, width), within(0)), ((tile, width), within(1)), pick


def feed_forward(n2_mine, n2_other, side, up, up_shift, cotangent, down, tile=256):
    half, width = n2_mine.shape
    rows = 2 * half
    cols = up.cols
    mine_block, other_block, pick = half_tiles(side, half // tile, tile, width)

    def kernel(
        side_ref, mine_ref, other_ref, shift_ref, cot_ref, *refs
    ):
        up_parts, refs = refs[: up.count], refs[up.count :]
        down_parts, refs = refs[: down.count], refs[down.count :]
        n2_ref, act_ref, dup_ref, sum_ref, sent_ref, kept_ref, up_out, down_out, *refs = refs
        up_ref, up_sems, up_sem, down_ref, down_sems, down_sem = refs
        up.load(up_parts, up_out, up_ref, up_sems, up_sem)
        down.load(down_parts, down_out, down_ref, down_sems, down_sem)

        @pl.when(pl.program_id(0) == 0)
        def _():
            sum_ref[...] = jnp.zeros_like(sum_ref)

        pick(side_ref, mine_ref, other_ref, n2_ref)

        for at in range(0, cols, 256):
            part = slice(at, at + 256)
            z = jnp.dot(n2_ref[...], up_ref[:, part], preferred_element_type=F32)
            z = z + shift_ref[:, part]
            d_act = jnp.dot(cot_ref[...], down_ref[:, part], preferred_element_type=F32)
            below = 0.5 * (1.0 + lax.erf(z * (0.5**0.5)))
            act_ref[:, part] = (z * below).astype(BF)
            slope = below + z * (jnp.exp(-0.5 * z * z) * (1.0 / math.sqrt(2.0 * math.pi)))
            d_up = (slope * d_act).astype(BF)
            dup_ref[:, part] = d_up
            sum_ref[:, part] += jnp.sum(d_up.astype(F32), axis=0, keepdims=True)
        own = pl.program_id(0) // (half // tile) == side_ref[0]
        for at in range(0, width, 512):
            part = slice(at, at + 512)
            d_n2 = lax.dot_general(
                dup_ref[...], up_ref[part], (((1,), (1,)), ((), ())), preferred_element_type=F32
            )

            @pl.when(own)
            def _(part=part, d_n2=d_n2):
                kept_ref[:, part] = d_n2

            @pl.when(jnp.logical_not(own))
            def _(part=part, d_n2=d_n2):
                sent_ref[:, part] = d_n2.astype(BF)

        up.end(up_out, up_ref, up_sem)
        down.end(down_out, down_ref, down_sem)

    return kernel_call(
        kernel,
        "feed_forward",
        (rows // tile,),
        [
            (n2_mine, *mine_block),
            (n2_other, *other_block),
            (up_shift[None, :], (1, cols), fixed),
            (cotangent, (tile, width), row_tile),
            *up.ins,
            *down.ins,
        ],
        [((tile, width), row_tile)]
        + [((tile, cols), row_tile)] * 2
        + [((1, cols), fixed), other_block, mine_block]
        + up.outs
        + down.outs,
        [((rows, width), BF), ((rows, cols), BF), ((rows, cols), BF), ((1, cols), F32)]
        + [((half, width), BF), ((half, width), F32)]
        + up.shapes
        + down.shapes,
        16,
        scratch=up.scratch + down.scratch,
        vmem=44,
        prefetch=(side[None],),
    )


def retain_backward(q, k, v, d_r, state, number, entry, log_decay, cosine, sine, tile=256):
    rows = q.shape[0]
    heads = q.shape[1] // KD

    def kernel(
        decay_ref, q_ref, k_ref, v_ref, dr_ref, state_ref, col_ref, row_ref, entry_ref,
        cos_ref, sin_ref, dq_ref, dk_ref, dv_ref,
    ):
        decay = decay_ref[pl.program_id(0)]
        across = (((1,), (1,)), ((), ()))
        down = (((0,), (0,)), ((), ()))
        for first in reversed(range(0, rows, tile)):
            wide = first + tile
            here = slice(first, wide)
            q_i, dr_i = q_ref[here], dr_ref[here]
            mask = decay_block(first, tile, wide, col_ref[here], row_ref[:, :wide], decay)
            scores = lax.dot_general(q_i, k_ref[:wide], across, preferred_element_type=F32)
            weights = (scores * mask).astype(BF)
            d_scores = lax.dot_general(dr_i, v_ref[:wide], across, preferred_element_type=F32)
            d_scores = (d_scores * mask).astype(BF)
            dq = jnp.dot(d_scores, k_ref[:wide], preferred_element_type=F32)
            dq = dq + own_column(entry_ref[here]) * lax.dot_general(
                dr_i, state_ref[0], across, preferred_element_type=F32
            )
            dq_ref[here] = turn(dq, cos_ref[here], -sin_ref[here]).astype(BF)
            dk = lax.dot_general(d_scores, q_i, down, preferred_element_type=F32)
            dv = lax.dot_general(weights, dr_i, down, preferred_element_type=F32)
            if wide == rows:
                dk_ref[...] = dk
                dv_ref[...] = dv
            else:
                dk_ref[:wide] += dk
                dv_ref[:wide] += dv

    def head(h, *_):
        return (0, h)

    def head3(h, *_):
        return (h, 0, 0)

    return kernel_call(
        kernel,
        "retain_backward",
        (heads,),
        [
            (q, (rows, KD), head),
            (k, (rows, KD), head),
            (v, (rows, VD), head),
            (d_r, (rows, VD), head),
            (state, (1, KD, VD), head3),
            (number[:, None], (rows, 1), fixed),
            (number[None, :], (1, rows), fixed),
            (entry, (rows, heads), fixed),
            (cosine, (rows, KD // 2), fixed),
            (sine, (rows, KD // 2), fixed),
        ],
        [((rows, KD), head), ((rows, KD), head), ((rows, VD), head)],
        [((rows, heads * KD), BF), ((rows, heads * KD), F32), ((rows, heads * VD), F32)],
        0,
        prefetch=(log_decay,),
        stay=True,
    )


def state_backward(k, v, exit_weight, leaving, dk, dv, cosine, sine, tile=256):
    rows = k.shape[0]
    heads = k.shape[1] // KD

    def kernel(
        k_ref, v_ref, exit_ref, leaving_ref, dk_in, dv_in, cos_ref, sin_ref, dk_ref, dv_ref
    ):
        for h in range(heads):
            at, wide = slice(h * KD, (h + 1) * KD), slice(h * VD, (h + 1) * VD)
            weight = exit_ref[:, h : h + 1]
            kd = (k_ref[:, at].astype(F32) * weight).astype(BF)
            d_k = dk_in[:, at] + weight * lax.dot_general(
                v_ref[:, wide], leaving_ref[h], (((1,), (1,)), ((), ())), preferred_element_type=F32
            )
            dk_ref[:, at] = turn(d_k, cos_ref[...], -sin_ref[...]).astype(BF)
            d_v = dv_in[:, wide] + jnp.dot(kd, leaving_ref[h], preferred_element_type=F32)
            dv_ref[:, wide] = d_v.astype(BF)

    return kernel_call(
        kernel,
        "state_backward",
        (rows // tile,),
        [
            (k, (tile, heads * KD), row_tile),
            (v, (tile, heads * VD), row_tile),
            (exit_weight, (tile, heads), row_tile),
            (leaving, leaving.shape, fixed3),
            (dk, (tile, heads * KD), row_tile),
            (dv, (tile, heads * VD), row_tile),
            (cosine, (tile, KD // 2), row_tile),
            (sine, (tile, KD // 2), row_tile),
        ],
        [((tile, heads * KD), row_tile), ((tile, heads * VD), row_tile)],
        [((rows, heads * KD), BF), ((rows, heads * VD), BF)],
        0,
        stay=True,
    )


def second_norm(inputs, side, kept, other, gain, shift, tile=128):
    half, width = kept.shape
    steps = half // tile

    def kernel(side_ref, x_ref, kept_ref, other_ref, gain_ref, shift_ref, mid_ref, n2_ref):
        mid = x_ref[...].astype(F32) + (kept_ref[...].astype(F32) + other_ref[...].astype(F32))
        mid_ref[...] = mid
        hat, _ = standardize(mid)
        n2_ref[...] = (hat * gain_ref[...] + shift_ref[...]).astype(BF)

    return kernel_call(
        kernel,
        "second_norm",
        (steps,),
        [
            (inputs, (tile, width), lambda i, side_ref: (side_ref[0] * steps + i, 0)),
            (kept, (tile, width), row_tile),
            (other, (tile, width), row_tile),
            (gain[None, :], (1, width), fixed),
            (shift[None, :], (1, width), fixed),
        ],
        [((tile, width), row_tile)] * 2,
        [((half, width), F32), ((half, width), BF)],
        6,
        prefetch=(side[None],),
    )


def norm_backward(x, x_rows, kept, other, base, base_rows, gain, side, tile=128):
    half, width = kept.shape
    steps = half // tile

    def kernel(
        side_ref, x_ref, kept_ref, other_ref, base_ref, gain_ref,
        out_ref, low_ref, gain_out, bias_out,
    ):
        @pl.when(pl.program_id(0) == 0)
        def _():
            gain_out[...] = jnp.zeros_like(gain_out)
            bias_out[...] = jnp.zeros_like(bias_out)

        d_n = kept_ref[...].astype(F32) + other_ref[...].astype(F32)
        hat, dev = standardize(x_ref[...].astype(F32))
        gain_out[...] += jnp.sum(d_n * hat, axis=0, keepdims=True)
        bias_out[...] += jnp.sum(d_n, axis=0, keepdims=True)
        out = base_ref[...].astype(F32) + standardize_back(d_n * gain_ref[...], hat, dev)
        out_ref[...] = out
        low_ref[...] = out.astype(BF)

    def picked(i, side_ref):
        return (side_ref[0] * steps + i, 0)

    return kernel_call(
        kernel,
        "norm_backward",
        (steps,),
        [
            (x, (tile, width), picked if x_rows else row_tile),
            (kept, (tile, width), row_tile),
            (other, (tile, width), row_tile),
            (base, (tile, width), picked if base_rows else row_tile),
            (gain[None, :], (1, width), fixed),
        ],
        [((tile, width), row_tile)] * 2 + [((1, width), fixed)] * 2,
        [((half, width), F32), ((half, width), BF), ((1, width), F32), ((1, width), F32)],
        0,
        prefetch=(side[None],),
        stay=True,
    )


def partial_rows(values, mats, which, added=(), pieces=1, tile=512):
    rows, width = values[0].shape[0], mats[0][0].shape[0]
    half, count = rows // 2, len(values)

    def kernel(which_ref, *refs):
        total = sum(
            lax.dot_general(v[...], m[...], (((1,), (1,)), ((), ())), preferred_element_type=F32)
            for v, m in zip(refs[:count], refs[count : 2 * count])
        )
        if added:
            total = total + jnp.concatenate(
                [ref[...].astype(F32) for ref in refs[2 * count : 2 * count + len(added)]], axis=0
            )
        for piece, ref in enumerate(refs[-pieces:]):
            ref[...] = total[piece * half // pieces : (piece + 1) * half // pieces].astype(BF)

    def column_tile(i, *_):
        return (0, i)

    ins = [(v, (half, v.shape[1]), lambda i, which_ref: (which_ref[0], 0)) for v in values]
    ins += [
        (m, (tile, v.shape[1]), lambda i, *_, at=at: (i, at)) for v, (m, at) in zip(values, mats)
    ]
    ins += [(part, (part.shape[0], tile), column_tile) for part in added]
    return kernel_call(
        kernel,
        "partial_rows",
        (width // tile,),
        ins,
        [((half // pieces, tile), column_tile)] * pieces,
        [((half // pieces, width), BF)] * pieces,
        0,
        prefetch=(which[None],),
        stay=True,
    )


def add_sent(kept, sent, tile=256):
    half, width = kept.shape

    def kernel(kept_ref, sent_ref, out_ref):
        out_ref[...] = (kept_ref[...] + sent_ref[...].astype(F32)).astype(BF)

    return kernel_call(
        kernel,
        "add_sent",
        (half // tile,),
        [(kept, (tile, width), row_tile), (sent, (tile, width), row_tile)],
        [((tile, width), row_tile)],
        [((half, width), BF)],
        0,
        stay=True,
    )[0]


def finish_output(mid, kept, other, shift, tile=256):
    half, width = mid.shape

    def kernel(mid_ref, kept_ref, other_ref, shift_ref, out_ref):
        ffn = kept_ref[...].astype(F32) + other_ref[...].astype(F32)
        out_ref[...] = (mid_ref[...] + ffn + shift_ref[...]).astype(BF)

    return kernel_call(
        kernel,
        "finish_output",
        (half // tile,),
        [
            (mid, (tile, width), row_tile),
            (kept, (tile, width), row_tile),
            (other, (tile, width), row_tile),
            (shift[None, :], (1, width), fixed),
        ],
        [((tile, width), row_tile)],
        [((half, width), BF)],
        0,
        stay=True,
    )[0]


def owners_table(size, vectors):
    if size > RING_MOST:
        return jnp.concatenate([vector.reshape(size, -1) for vector in vectors], axis=1)
    wide = [vector.shape[1] // size for vector in vectors]

    def kernel(*refs):
        at = 0
        for ref, width in zip(refs, wide):
            for i in range(size):
                refs[-1][i : i + 1, at : at + width] = ref[:, i * width : (i + 1) * width]
            at += width

    return kernel_call(
        kernel,
        "owners_table",
        (1,),
        [(vector, vector.shape, fixed) for vector in vectors],
        [((size, sum(wide)), fixed)],
        [((size, sum(wide)), F32)],
        0,
    )[0]


def passed(small):
    def kernel(in_ref, out_ref):
        out_ref[...] = in_ref[...]

    return kernel_call(
        kernel,
        "passed",
        (1,),
        [(small, small.shape, fixed)],
        [(small.shape, fixed)],
        [(small.shape, small.dtype)],
        0,
    )[0]


def both_halves(mine, other, side, kind, tile=256):
    half, width = mine.shape
    mine_block, other_block, pick = half_tiles(side, half // tile, tile, width)
    return kernel_call(
        pick,
        "both_halves",
        (2 * half // tile,),
        [(mine, *mine_block), (other, *other_block)],
        [((tile, width), row_tile)],
        [((2 * half, width), kind)],
        0,
        prefetch=(side[None],),
        stay=True,
    )[0]


def gradient(x, *dys, tile=256):
    rows, width = x.shape
    cols = [dy.shape[1] for dy in dys]

    def kernel(x_ref, *refs):
        at = 0
        for dy_ref in refs[:-1]:
            refs[-1][:, at : at + dy_ref.shape[1]] = lax.dot_general(
                x_ref[...], dy_ref[...], (((0,), (0,)), ((), ())), preferred_element_type=F32
            ).astype(BF)
            at += dy_ref.shape[1]

    return kernel_call(
        kernel,
        "gradient",
        (width // tile,),
        [(x, (rows, tile), lambda i, *_: (0, i))] + [(dy, dy.shape, fixed) for dy in dys],
        [((tile, sum(cols)), row_tile)],
        [((width, sum(cols)), BF)],
        0,
    )[0]


def ring_add(grads, arrived, place, step, turned, cut):
    size = lax.axis_size("seq")
    rows = grads[0].shape[0] // size
    last = step == size
    kind = F32 if last else BF

    def kernel(place_ref, *refs):
        outs = refs[2 + len(arrived) :]
        for i in range(2):
            total = refs[i][...].astype(F32)
            if arrived:
                total = total + refs[2 + i][...].astype(F32)
            if last and turned and i == 0:
                total = total.T
            if last and cut and i == 1:
                width = total.shape[1] // 2
                outs[1][...] = total[:, :width]
                outs[2][...] = total[:, width:]
            else:
                outs[i][...] = total.astype(kind)

    def own(sign):
        def index(i, place_ref):
            return (ring_owner(place_ref[0] + sign * step, size), 0)

        return index

    blocks = [(rows, grad.shape[1]) for grad in grads]
    outs = list(blocks)
    if last and turned:
        outs[0] = blocks[0][::-1]
    if last and cut:
        outs[1:] = [(rows, blocks[1][1] // 2)] * 2
    grads = [pltpu.with_memory_space_constraint(grad, pltpu.HBM) for grad in grads]
    ins = [(grads[0], blocks[0], own(-1)), (grads[1], blocks[1], own(1))]
    ins += [(block, block.shape, fixed) for block in arrived]
    return kernel_call(
        kernel,
        "ring_add",
        (1,),
        ins,
        [(block, fixed) for block in outs],
        [(block, kind) for block in outs],
        0,
        prefetch=(place[None],),
    )


def body(
    inputs,
    cotangent,
    lengths,
    offsets,
    first_gain,
    first_bias,
    query_weight,
    key_weight,
    value_weight,
    gate_weight,
    group_gain,
    group_bias,
    out_weight,
    second_gain,
    second_bias,
    up_weight,
    up_bias,
    down_weight,
    down_bias,
):
    size = lax.axis_size("seq")
    rows, width = inputs.shape
    shard = first_gain.shape[0]
    unit = group_gain.shape[0]
    heads = query_weight.shape[1] // KD
    half = rows // 2
    tp_me = lax.axis_index("tp")
    side = lax.rem(tp_me, 2)
    mine = side * half

    qk_own = jnp.concatenate([query_weight, key_weight], axis=1).astype(BF)
    v_own = value_weight.astype(BF)
    own_vector = jnp.concatenate(
        [
            first_gain,
            first_bias,
            second_gain,
            second_bias,
            down_bias,
            group_gain,
            group_bias,
            up_bias,
        ]
    ).astype(BF)[None, :]
    qkv_ring = gather(qk_own, v_own)
    go_ring = gather(gate_weight.astype(BF), out_weight.astype(BF).T)
    uw_ring = gather(up_weight.astype(BF), down_weight.astype(BF).T)
    clock = Clock((qkv_ring, 0), (go_ring, 1), (uw_ring, 0))
    x = clock.tick(inputs)

    first_row = lax.axis_index("seq") * rows
    log_decay = jnp.log(
        1.0
        - jnp.exp2(-5.0 - (tp_me * heads + jnp.arange(heads, dtype=jnp.int32)).astype(jnp.float32))
    )
    number, entry_weight, exit_weight, cosine, sine = block_decay(
        first_row, rows, lengths, offsets, log_decay
    )
    entry_cols, exit_cols = entry_weight.T, exit_weight.T
    table = own_vector
    distance = 1
    while distance < size:
        table = doubled(table, distance)
        table = clock.tick(table)
        distance *= 2
    table = table[jnp.arange(size) ^ lax.axis_index("seq")].astype(F32)

    def wide(i):
        return table[:, i * shard : (i + 1) * shard].reshape(-1)

    def narrow(i):
        start = 5 * shard + i * unit
        return table[:, start : start + unit].reshape(-1)

    gain_one, bias_one, gain_two, bias_two, down_shift = [wide(i) for i in range(5)]
    group_scale, group_shift, up_shift = [narrow(i) for i in range(3)]

    n1 = norm_rows(x, gain_one, bias_one)
    grad_down_bias = jnp.sum(cotangent.astype(F32), axis=0)
    n1, grad_down_bias = barrier(n1, grad_down_bias)
    n1, cosine, sine, number, entry_cols, exit_cols = clock.tick(
        n1, cosine, sine, number, entry_cols, exit_cols
    )
    n1 = clock.until(qkv_ring, n1)

    qk_weight, v_weight = qkv_ring.result()
    q, k, qk_mat = project_turn(n1, qk_weight, cosine, sine)
    n1, q, k = barrier(n1, q, k)
    n1 = clock.tick(n1)
    v, v_mat = project(n1, v_weight)
    v, q, k = clock.tick(v, q, k)
    local_out, local_state = retain(q, k, v, number, exit_cols, log_decay)
    local_out, local_state = clock.tick(local_out, local_state)
    state_parts = Others(local_state.astype(BF), 1).second()
    local_out = clock.until(go_ring, local_out)

    def gathered_state(first, rest, direction):
        total, weight = first.astype(F32), 1.0
        for turn, part in enumerate(rest, 1):
            block = first_row - direction * turn * rows
            passed = passing_weight(block, rows, lengths, offsets, log_decay)
            weight = weight * passed
            total = total + weight[:, None, None] * part.astype(F32)
        return total.astype(BF)

    state = gathered_state(state_parts[0], state_parts[1:], 1)
    state, local_out = barrier(state, local_out)
    g_weight, o_weight = go_ring.result()
    y, gate, r_hat, r_dev, g_mat = gate_forward(
        n1, g_weight, q, entry_cols, state, local_out, group_scale, group_shift
    )
    y = clock.tick(y)
    o_mat = assemble(o_weight)
    y, o_mat = barrier(y, o_mat)

    def pick(values, which):
        return lax.dynamic_slice_in_dim(values, which * half, half)

    def tp_first(make, value):
        sent = make(pick(value, 1 - side)).astype(BF)
        sent, value = clock.tick(sent, value)
        sent = swap(sent, 1)
        return (make(pick(value, side)) + sent.astype(F32)).astype(BF)

    kept = tp_first(lambda part: dot(part, o_mat, ((1,), (1,))), y)
    other = swap(kept, 2)
    kept = clock.tick(kept, count=4)
    kept, other = barrier(kept, other)
    mid, n2_mine = second_norm(inputs, side, kept, other, gain_two, bias_two)
    n2_other = swap(n2_mine, 1)
    n2_mine, n2_other = barrier(n2_mine, n2_other)
    n2_mine, n2_other = clock.until(uw_ring, n2_mine, n2_other)
    u_weight, w_weight = uw_ring.result()
    n2, act, d_up, grad_up_bias, sent_two, kept_two, u_mat, w_mat = feed_forward(
        n2_mine, n2_other, side, u_weight, up_shift, cotangent, w_weight
    )

    line = Line(grad_up_bias)
    pairs_two = [(i, i ^ 2) for i in range(lax.axis_size("tp"))]
    pairs_one = [(i, i ^ 1) for i in range(lax.axis_size("tp"))]

    def to_partner(block, pieces=2):
        count = block.shape[0] // pieces
        return [
            line.send(block[i * count : (i + 1) * count], "tp", pairs_one) for i in range(pieces)
        ]

    def partial_sent(values, mats, pieces=2, cost=0):
        parts = line.run(
            lambda *v: partial_rows(v, mats, 1 - side, pieces=pieces), *values, cost=cost
        )
        parts = parts if isinstance(parts, tuple) else (parts,)
        return [line.send(part, "tp", pairs_one) for part in parts]

    def partial_kept(values, mats, sent, cost=0):
        return line.run(lambda *v: partial_rows(v, mats, side, sent), *values, cost=cost)

    sent_two = line.send(sent_two, "tp", pairs_one)
    grad_w = line.run(gradient, cotangent, act, cost=23)
    kept_two = line.run(add_sent, kept_two, sent_two)
    other_two = line.send(kept_two, "tp", pairs_two)
    grad_u = line.run(gradient, n2, d_up, cost=23)
    wu_back = reduce(grad_w, grad_u, turned=True)
    line.tick(wu_back, wu_back, wu_back)
    d_mid, d_branch_mine, grad_second_gain, grad_second_bias = line.run(
        lambda kept, other: norm_backward(
            mid, False, kept, other, cotangent, True, gain_two, side
        ),
        kept_two,
        other_two,
        cost=6,
    )
    d_branch_other = to_partner(d_branch_mine, 1)[0]
    line.tick(wu_back, cost=23)

    d_branch, d_gate, d_r, grad_group_gain, grad_group_bias, own_grad = line.run(
        lambda mine, other: gate_backward(
            mine,
            other,
            side,
            o_mat,
            gate,
            r_hat,
            r_dev,
            group_scale,
            group_shift,
            q,
            entry_cols,
        ),
        d_branch_mine,
        d_branch_other,
        cost=6,
    )
    others = Others(own_grad, -1, line.send)
    line.tick(wu_back)
    d_q, d_k, d_v = line.run(
        lambda d_r: retain_backward(
            q, k, v, d_r, state, number, entry_cols, log_decay, cosine, sine
        ),
        d_r,
        cost=6,
    )
    leaving_parts = others.second()
    line.tick(wu_back)
    grad_o = line.run(gradient, d_branch, y, cost=6)
    line.tick(wu_back)
    grad_g = line.run(gradient, n1, d_gate, cost=6)
    og_back = reduce(grad_o, grad_g, turned=True)
    line.tick(og_back)
    leaving = line.run(lambda first, *rest: gathered_state(first, rest, -1), *leaving_parts)
    d_k, d_v = line.run(
        lambda d_k, d_v: state_backward(k, v, exit_cols, leaving, d_k, d_v, cosine, sine),
        d_k,
        d_v,
        cost=6,
    )
    line.tick(wu_back)
    grad_v = line.run(gradient, n1, d_v)
    grad_qk = line.run(gradient, n1, d_q, d_k, cost=6)
    vqk_back = reduce(grad_v, grad_qk, cut=True)
    line.tick(vqk_back, og_back)
    d_all = (d_gate, d_v, d_q, d_k)
    mats_all = ((g_mat, 0), (v_mat, 0), (qk_mat, 0), (qk_mat, 1))
    sent_one = partial_sent(d_all, mats_all, 1, cost=6)
    grad_second_gain = line.fill(grad_second_gain, 23)
    line.tick(og_back, vqk_back)
    kept_one = partial_kept(d_all, mats_all, sent_one, cost=6)
    other_one = line.send(kept_one, "tp", pairs_two)
    grad_second_gain = line.fill(grad_second_gain, 23)
    line.tick(og_back, vqk_back)
    part_out = line.run(lambda act: partial_rows((act,), ((w_mat, 0),), 1 - side), act)
    line.tick(og_back, vqk_back)
    _, grad_mine, grad_first_gain, grad_first_bias = line.run(
        lambda kept, other: norm_backward(
            inputs, True, kept, other, d_mid, False, gain_one, side
        ),
        kept_one,
        other_one,
        cost=6,
    )
    grad_other = to_partner(grad_mine, 1)[0]
    sent_out = line.send(part_out, "tp", pairs_one)
    line.tick(og_back, vqk_back, cost=12)
    grad_inputs = line.run(
        lambda mine, other: both_halves(mine, other, side, F32), grad_mine, grad_other
    )
    kept_out = partial_kept((act,), ((w_mat, 0),), (sent_out,))
    other_out = line.send(kept_out, "tp", pairs_two)
    grad_second_gain = line.fill(grad_second_gain, 23)
    line.tick(og_back, vqk_back)

    grad_up_bias = line.token
    table = line.run(
        lambda *vectors: owners_table(size, vectors),
        grad_first_gain,
        grad_first_bias,
        grad_second_gain,
        grad_second_bias,
        grad_down_bias[None, :],
        grad_group_gain,
        grad_group_bias,
        grad_up_bias,
    )
    line.token = grad_inputs
    table, sent = halved(line, table)
    line.tick(vqk_back, og_back)
    output_mine = line.run(
        lambda kept, other: finish_output(mid, kept, other, down_shift),
        kept_out,
        other_out,
        cost=6,
    )
    while table.shape[0] > 1:
        table = line.run(lambda kept, sent: kept + sent, table, sent)
        table, sent = halved(line, table)
        line.tick(vqk_back, og_back)
    output_other = to_partner(output_mine, 1)[0]
    small = line.run(lambda kept, sent: kept + sent, table, sent)[0]
    halves = small[: 4 * shard]
    sent = line.send(halves, "tp", pairs_one)
    while not (og_back.ended and vqk_back.ended):
        line.tick(vqk_back, og_back)
    output = line.run(
        lambda mine, other: both_halves(mine, other, side, BF), output_mine, output_other
    )
    halves = halves + sent
    grad_inputs = line.token
    own = [halves[i * shard : (i + 1) * shard] for i in range(4)]
    own_down_bias = small[4 * shard : 5 * shard]
    own_units = [small[5 * shard + i * unit : 5 * shard + (i + 1) * unit] for i in range(3)]
    own_w, own_u = wu_back.result()
    own_o, own_g = og_back.result()
    own_v, own_q, own_k = vqk_back.result()
    return (
        output,
        grad_inputs,
        own[0],
        own[1],
        own_q,
        own_k,
        own_v,
        own_g,
        own_units[0],
        own_units[1],
        own_o,
        own[2],
        own[3],
        own_u,
        own_units[2],
        own_w,
        own_down_bias,
    )


def solution(mesh):
    placed = (
        P("seq", None),
        P("seq", None),
        P(),
        P(),
        P("seq"),
        P("seq"),
        P("seq", "tp"),
        P("seq", "tp"),
        P("seq", "tp"),
        P("seq", "tp"),
        P(("tp", "seq")),
        P(("tp", "seq")),
        P("tp", "seq"),
        P("seq"),
        P("seq"),
        P("seq", "tp"),
        P(("tp", "seq")),
        P("tp", "seq"),
        P("seq"),
    )
    return jax.shard_map(
        body,
        mesh=mesh,
        in_specs=placed,
        out_specs=(
            P("seq", None),
            P("seq", None),
            P("seq"),
            P("seq"),
            P("seq", "tp"),
            P("seq", "tp"),
            P("seq", "tp"),
            P("seq", "tp"),
            P(("tp", "seq")),
            P(("tp", "seq")),
            P("tp", "seq"),
            P("seq"),
            P("seq"),
            P("seq", "tp"),
            P(("tp", "seq")),
            P("tp", "seq"),
            P("seq"),
        ),
        check_vma=False,
    )
```

```python
import math

import jax
import jax.numpy as jnp
from jax import lax
from jax.experimental import pallas as pl
from jax.experimental.pallas import tpu as pltpu
from jax.sharding import PartitionSpec as P

KD = 256
VD = 512
EPS = 1e-05
BF = jnp.bfloat16
F32 = jnp.float32
RING_MOST = 16


def dot(a, b, dims):
    return lax.dot_general(a, b, (dims, ((), ())), preferred_element_type=F32)


class Others:
    def __init__(self, block, direction, send=lax.ppermute):
        self.size = lax.axis_size("seq")
        self.block, self.direction, self.send = block, direction, send
        turns = max(1, self.size // 4)
        self.paired = turns == 2
        steps = [2] if self.paired else range(1, turns + 1)
        self.parts = [self.shift(direction * step) for step in steps]

    def shift(self, distance):
        route = [(i, i + distance) for i in range(self.size) if 0 <= i + distance < self.size]
        return self.send(self.block, "seq", route)

    def second(self):
        if self.paired:
            (far,) = self.parts
            first = lax.rem(lax.axis_index("seq"), 2) == (0 if self.direction > 0 else 1)
            near = jnp.where(first, self.block, far)
            near = self.send(near, "seq", [(i, i ^ 1) for i in range(self.size)])
            self.parts = [near, far]
        return self.parts


def ring_owner(place, size):
    place = lax.rem(place + 2 * size, size)
    return jnp.where(place < size // 2, 2 * place, 2 * (size - 1 - place) + 1)


def ring_place(index, size):
    return jnp.where(index % 2 == 0, index // 2, size - 1 - index // 2)


def ring_routes(size):
    order = list(range(0, size, 2)) + list(range(size - 1, 0, -2))
    ahead = [(order[i], order[(i + 1) % size]) for i in range(size)]
    return ahead, [(b, a) for a, b in ahead]


class Weight:
    def __init__(self, own, parts=(), sign=0):
        self.size = len(parts) + 1
        self.rows, self.cols = own.shape
        self.arrays = [own, *parts]
        self.count, self.sign = self.size, sign
        self.shape = (self.size * self.rows, self.cols)
        self.ins = [(array, None, None) for array in self.arrays]
        self.outs = [(None, None)]
        self.shapes = [(self.shape, own.dtype)]
        self.scratch = [
            pltpu.VMEM(self.shape, own.dtype),
            pltpu.SemaphoreType.DMA((self.count,)),
            pltpu.SemaphoreType.DMA,
        ]

    def copies(self, parts, whole, sems):
        if self.size == 1:
            return [pltpu.make_async_copy(parts[0], whole, sems.at[0])]
        place = ring_place(lax.axis_index("seq"), self.size)
        owners = [ring_owner(place + self.sign * k, self.size) for k in range(self.size)]
        return [
            pltpu.make_async_copy(part, whole.at[pl.ds(owner * self.rows, self.rows)], sems.at[i])
            for i, (part, owner) in enumerate(zip(parts, owners))
        ]

    def load(self, parts, out, whole, sems, out_sem):
        @pl.when(pl.program_id(0) == 0)
        def _():
            copies = self.copies(parts, whole, sems)
            for copy in copies:
                copy.start()
            for copy in copies:
                copy.wait()
            pltpu.make_async_copy(whole, out, out_sem).start()

    def end(self, out, whole, out_sem):
        @pl.when(pl.program_id(0) == pl.num_programs(0) - 1)
        def _():
            pltpu.make_async_copy(whole, out, out_sem).wait()


def assemble(weight):
    def kernel(*refs):
        parts, (out, whole, sems, out_sem) = refs[: weight.count], refs[weight.count :]
        weight.load(parts, out, whole, sems, out_sem)
        weight.end(out, whole, out_sem)

    return kernel_call(
        kernel, "assemble", (1,), weight.ins, weight.outs, weight.shapes, 4, scratch=weight.scratch
    )[0]


def barrier(*values):
    return lax.optimization_barrier(values)


class Gather:
    def __init__(self, ahead, back):
        self.size = lax.axis_size("seq")
        self.own = self.now = [ahead, back]
        self.parts = [[], []]
        self.left = self.size - 1

    def tick(self, *values):
        *self.now, first = barrier(*self.now, values[0])
        if self.left > 0:
            self.now = [
                lax.ppermute(block, "seq", route)
                for block, route in zip(self.now, ring_routes(self.size))
            ]
            for part, block in zip(self.parts, self.now):
                part.append(block)
        self.left -= 1
        return (first, *values[1:])

    @property
    def ended(self):
        return self.left < 0

    def result(self):
        return [
            Weight(own, parts, sign) for own, parts, sign in zip(self.own, self.parts, (-1, 1))
        ]


class Line:
    cost = 0

    def __init__(self, token):
        self.token = token

    def run(self, function, *values, cost=0):
        *values, self.token = barrier(*values, self.token)
        Line.cost = cost
        out = function(*values)
        Line.cost = 0
        first, *rest = out if isinstance(out, (tuple, list)) else (out,)
        first, self.token = barrier(first, self.token)
        return (first, *rest) if len(rest) else first

    def send(self, block, axis, route):
        block, self.token = barrier(block, self.token)
        return lax.ppermute(block, axis, route)

    def tick(self, *rings, cost=0):
        for ring in rings:
            if not ring.ended:
                self.token = ring.go(ring.add(self.token, cost))

    def fill(self, small, cost):
        return self.run(passed, small, cost=cost)

    def meet(self, *values):
        *values, self.token = barrier(*values, self.token)
        return values


class Reduce:
    def __init__(self, ahead, back, turned, cut):
        self.size = lax.axis_size("seq")
        self.grads = (ahead, back)
        self.form = (turned, cut)
        self.place = ring_place(lax.axis_index("seq"), self.size)
        self.arrived = ()
        self.step = 0

    def add(self, token, cost=0):
        self.step += 1
        if self.arrived:
            *self.arrived, token = barrier(*self.arrived, token)
        Line.cost = cost
        self.now = ring_add(self.grads, self.arrived, self.place, self.step, *self.form)
        Line.cost = 0
        *self.now, token = barrier(*self.now, token)
        return token

    def go(self, token):
        if self.step < self.size:
            *self.now, token = barrier(*self.now, token)
            self.arrived = [
                lax.ppermute(block, "seq", route)
                for block, route in zip(self.now, ring_routes(self.size))
            ]
        return token

    @property
    def ended(self):
        return self.step >= self.size

    def result(self):
        return self.now


class Builtin:
    def __init__(self, value):
        self.value = value
        self.ended = True

    def result(self):
        return self.value


class Clock:
    def __init__(self, *rings):
        self.queue = [(ring, left) for ring, left in rings if not ring.ended]
        self.active = []
        self.turn = 0

    def tick(self, *values, count=1):
        for _ in range(count):
            if self.queue and (not self.active or self.active[-1].left <= self.queue[0][1]):
                self.active.append(self.queue.pop(0)[0])
                values = self.active[-1].tick(*values)
            elif self.active:
                self.turn = (self.turn + 1) % len(self.active)
                ring = self.active[self.turn]
                values = ring.tick(*values)
                if ring.ended:
                    self.active.remove(ring)
        return values[0] if len(values) == 1 else tuple(values)

    def until(self, ring, *values):
        while not ring.ended:
            values = self.tick(*values)
            values = values if isinstance(values, tuple) else (values,)
        return values[0] if len(values) == 1 else values


def gather(ahead, back):
    if lax.axis_size("seq") > RING_MOST:
        return Builtin(
            [Weight(lax.all_gather(own, "seq", axis=0, tiled=True)) for own in (ahead, back)]
        )
    return Gather(ahead, back)


def doubled(rows, distance):
    route = [(i, i ^ distance) for i in range(lax.axis_size("seq"))]
    return jnp.concatenate([rows, lax.ppermute(rows, "seq", route)], axis=0)


def reduce(ahead, back, turned=False, cut=False):
    if lax.axis_size("seq") > RING_MOST:
        first, second = [
            lax.psum_scatter(grad.astype(F32), "seq", scatter_dimension=0, tiled=True)
            for grad in (ahead, back)
        ]
        first = first.T if turned else first
        return Builtin([first, *jnp.split(second, 2, axis=1)] if cut else [first, second])
    return Reduce(ahead, back, turned, cut)


def halved(line, table):
    distance = table.shape[0] // 2
    route = [(i, i ^ distance) for i in range(lax.axis_size("seq"))]
    high = (lax.axis_index("seq") // distance) % 2
    kept = lax.dynamic_slice_in_dim(table, high * distance, distance)
    sent = lax.dynamic_slice_in_dim(table, (1 - high) * distance, distance)
    return kept, line.send(sent, "seq", route)


def swap(block, bit):
    return lax.ppermute(block, "tp", [(i, i ^ bit) for i in range(lax.axis_size("tp"))])


def token_layout(first_row, row_total, lengths, offsets):
    position = first_row + jnp.arange(row_total, dtype=jnp.int32)
    inside = (position[:, None] >= offsets[None, :]) & (
        position[:, None] < offsets[None, :] + lengths[None, :]
    )
    member = inside.astype(jnp.int32)
    labels = jnp.arange(1, lengths.shape[0] + 1, dtype=jnp.int32)
    number = jnp.sum(member * labels[None, :], axis=1) - 1
    seq_start = jnp.sum(member * offsets[None, :], axis=1)
    return (number, position - seq_start)


def passing_weight(first_row, row_total, lengths, offsets, log_decay):
    before = token_layout(first_row - 1, 1, lengths, offsets)[0][0]
    last = token_layout(first_row + row_total - 1, 1, lengths, offsets)[0][0]
    return jnp.where((last == before) & (before >= 0), jnp.exp(log_decay * row_total), 0.0)


def block_decay(first_row, row_total, lengths, offsets, log_decay):
    number, within = token_layout(first_row, row_total, lengths, offsets)
    before = token_layout(first_row - 1, 1, lengths, offsets)[0][0]
    final_seq = number[row_total - 1]
    slot_index = jnp.arange(row_total).astype(jnp.float32)
    entry_weight = jnp.where(
        ((number == before) & (number >= 0))[None, :],
        jnp.exp(log_decay[:, None] * (slot_index[None, :] + 1.0)),
        0.0,
    )
    exit_weight = jnp.where(
        ((number == final_seq) & (number >= 0))[None, :],
        jnp.exp(log_decay[:, None] * (row_total - 1.0 - slot_index[None, :])),
        0.0,
    )
    half_size = KD // 2
    frequency = jnp.exp(-math.log(10000.0) * 2.0 * jnp.arange(half_size).astype(jnp.float32) / KD)
    angles = within.astype(jnp.float32)[:, None] * frequency[None, :]
    return (number, entry_weight, exit_weight, jnp.cos(angles), jnp.sin(angles))


def standardize(values):
    average = jnp.mean(values, axis=-1, keepdims=True)
    centred = values - average
    variance = jnp.mean(centred * centred, axis=-1, keepdims=True)
    scale = lax.rsqrt(variance + EPS)
    return centred * scale, scale


def standardize_back(d_normed, normed, scale):
    first = jnp.mean(d_normed, axis=-1, keepdims=True)
    second = jnp.mean(d_normed * normed, axis=-1, keepdims=True)
    return scale * (d_normed - first - normed * second)


def kernel_call(body, name, grid, ins, outs, shapes, weight, prefetch=(), vmem=24, scratch=(), stay=False):
    arrays = [a for a, _, _ in ins]
    arrays = [
        pltpu.with_memory_space_constraint(a, pltpu.HBM) if stay or block is None else a
        for a, block, _ in ins
    ]
    return pl.pallas_call(
        body,
        out_shape=[jax.ShapeDtypeStruct(s, t) for s, t in shapes],
        grid_spec=pltpu.PrefetchScalarGridSpec(
            num_scalar_prefetch=len(prefetch),
            grid=grid,
            in_specs=[spec(block, index) for _, block, index in ins],
            out_specs=[
                pl.BlockSpec(memory_space=pl.ANY) if block is None else pl.BlockSpec(block, index)
                for block, index in outs
            ],
            scratch_shapes=list(scratch),
        ),
        compiler_params=pltpu.CompilerParams(vmem_limit_bytes=vmem * 2**20),
        cost_estimate=pl.CostEstimate(
            flops=weight * 10**9 // 2 + Line.cost * 10**9, bytes_accessed=0, transcendentals=0
        ),
        name=name,
    )(*prefetch, *arrays)


def spec(block, index):
    if block is None:
        return pl.BlockSpec(memory_space=pl.ANY)
    if index in (fixed, fixed3):
        return pl.BlockSpec(block, index, pipeline_mode=pl.Buffered(1))
    return pl.BlockSpec(block, index)


def row_tile(i, *_):
    return (i, 0)


def fixed(*_):
    return (0, 0)


def fixed3(*_):
    return (0, 0, 0)


def turn(values, cosine, sine):
    low, high = values[:, : KD // 2], values[:, KD // 2 :]
    return jnp.concatenate([low * cosine - high * sine, high * cosine + low * sine], axis=1)


def norm_rows(x, gain, shift, tile=256):
    rows, width = x.shape

    def kernel(x_ref, gain_ref, shift_ref, out_ref):
        hat, _ = standardize(x_ref[...].astype(F32))
        out_ref[...] = (hat * gain_ref[...] + shift_ref[...]).astype(BF)

    return kernel_call(
        kernel,
        "first_norm",
        (rows // tile,),
        [
            (x, (tile, width), row_tile),
            (gain[None, :], (1, width), fixed),
            (shift[None, :], (1, width), fixed),
        ],
        [((tile, width), row_tile)],
        [((rows, width), BF)],
        6,
    )[0]


def project_turn(n1, weight, cosine, sine, tile=256):
    rows, width = n1.shape
    cols = weight.cols // 2

    def kernel(n1_ref, cos_ref, sin_ref, *refs):
        parts, (q_ref, k_ref, out, mat_ref, sems, out_sem) = (
            refs[: weight.count],
            refs[weight.count :],
        )
        weight.load(parts, out, mat_ref, sems, out_sem)
        raw = jnp.dot(n1_ref[...], mat_ref[...], preferred_element_type=F32)
        cos, sin = cos_ref[...], sin_ref[...]
        for at in range(0, cols, KD):
            q_ref[:, at : at + KD] = turn(raw[:, at : at + KD], cos, sin).astype(BF)
            k_ref[:, at : at + KD] = turn(raw[:, cols + at : cols + at + KD], cos, sin).astype(BF)
        weight.end(out, mat_ref, out_sem)

    return kernel_call(
        kernel,
        "query_key",
        (rows // tile,),
        [
            (n1, (tile, width), row_tile),
            (cosine, (tile, KD // 2), row_tile),
            (sine, (tile, KD // 2), row_tile),
            *weight.ins,
        ],
        [((tile, cols), row_tile)] * 2 + weight.outs,
        [((rows, cols), BF)] * 2 + weight.shapes,
        9,
        scratch=weight.scratch,
        stay=True,
    )


def project(n1, weight, tile=256):
    rows, width = n1.shape

    def kernel(n1_ref, *refs):
        parts, (v_ref, out, mat_ref, sems, out_sem) = refs[: weight.count], refs[weight.count :]
        weight.load(parts, out, mat_ref, sems, out_sem)
        v_ref[...] = jnp.dot(n1_ref[...], mat_ref[...], preferred_element_type=F32).astype(BF)
        weight.end(out, mat_ref, out_sem)

    return kernel_call(
        kernel,
        "value",
        (rows // tile,),
        [(n1, (tile, width), row_tile), *weight.ins],
        [((tile, weight.cols), row_tile)] + weight.outs,
        [((rows, weight.cols), BF)] + weight.shapes,
        9,
        scratch=weight.scratch,
        stay=True,
    )


def decay_block(first, count, wide, number_col, number_row, log_decay):
    distance = (
        first
        + lax.broadcasted_iota(jnp.int32, (count, wide), 0)
        - lax.broadcasted_iota(jnp.int32, (count, wide), 1)
    )
    linked = (number_col == number_row) & (number_col >= 0) & (distance >= 0)
    exponent = jnp.maximum(distance, 0).astype(F32)
    return jnp.where(linked, jnp.exp(log_decay * exponent), 0.0)


def own_column(table):
    here = lax.broadcasted_iota(jnp.int32, table.shape, 1) == pl.program_id(0)
    return jnp.sum(jnp.where(here, table, 0.0), axis=1, keepdims=True)


def retain(q, k, v, number, exit_weight, log_decay, tile=256):
    rows = q.shape[0]
    heads = q.shape[1] // KD

    def kernel(decay_ref, q_ref, k_ref, v_ref, col_ref, row_ref, exit_ref, out_ref, state_ref):
        decay = decay_ref[pl.program_id(0)]
        for first in range(0, rows, tile):
            wide = first + tile
            scores = lax.dot_general(
                q_ref[first:wide], k_ref[:wide], (((1,), (1,)), ((), ())), preferred_element_type=F32
            )
            mask = decay_block(first, tile, wide, col_ref[first:wide], row_ref[:, :wide], decay)
            out_ref[first:wide] = jnp.dot(
                (scores * mask).astype(BF), v_ref[:wide], preferred_element_type=F32
            )
        kd = (k_ref[...].astype(F32) * own_column(exit_ref[...])).astype(BF)
        state_ref[0] = lax.dot_general(
            kd, v_ref[...], (((0,), (0,)), ((), ())), preferred_element_type=F32
        )

    def head(h, *_):
        return (0, h)

    def head3(h, *_):
        return (h, 0, 0)

    return kernel_call(
        kernel,
        "retain",
        (heads,),
        [
            (q, (rows, KD), head),
            (k, (rows, KD), head),
            (v, (rows, VD), head),
            (number[:, None], (rows, 1), fixed),
            (number[None, :], (1, rows), fixed),
            (exit_weight, (rows, heads), fixed),
        ],
        [((rows, VD), head), ((1, KD, VD), head3)],
        [((rows, heads * VD), F32), ((heads, KD, VD), F32)],
        8,
        prefetch=(log_decay,),
    )


def gate_forward(n1, weight, q, entry, state, local_out, scale, shift, tile=256):
    rows, width = n1.shape
    cols = weight.cols
    heads = cols // VD

    def kernel(
        n1_ref, q_ref, entry_ref, state_ref, local_ref, scale_ref, shift_ref, *refs
    ):
        parts, (y_ref, gate_ref, hat_ref, dev_ref, out, mat_ref, sems, out_sem) = (
            refs[: weight.count],
            refs[weight.count :],
        )
        weight.load(parts, out, mat_ref, sems, out_sem)
        gate = jnp.dot(n1_ref[...], mat_ref[...], preferred_element_type=F32)
        gate_ref[...] = gate
        swish = gate * jax.nn.sigmoid(gate)
        devs = []
        for h in range(heads):
            at = slice(h * VD, (h + 1) * VD)
            qd = (q_ref[:, h * KD : (h + 1) * KD].astype(F32) * entry_ref[:, h : h + 1]).astype(BF)
            r = local_ref[:, at] + jnp.dot(qd, state_ref[h], preferred_element_type=F32)
            hat, dev = standardize(r)
            hat_ref[:, at] = hat
            devs.append(dev)
            affine = hat * scale_ref[:, at] + shift_ref[:, at]
            y_ref[:, at] = (affine * swish[:, at]).astype(BF)
        dev_ref[...] = jnp.concatenate(devs, axis=1)
        weight.end(out, mat_ref, out_sem)

    return kernel_call(
        kernel,
        "gate_forward",
        (rows // tile,),
        [
            (n1, (tile, width), row_tile),
            (q, (tile, heads * KD), row_tile),
            (entry, (tile, heads), row_tile),
            (state, state.shape, fixed3),
            (local_out, (tile, cols), row_tile),
            (scale[None, :], (1, cols), fixed),
            (shift[None, :], (1, cols), fixed),
            *weight.ins,
        ],
        [((tile, cols), row_tile)] * 3 + [((tile, heads), row_tile)] + weight.outs,
        [((rows, cols), BF), ((rows, cols), F32), ((rows, cols), F32), ((rows, heads), F32)]
        + weight.shapes,
        12,
        scratch=weight.scratch,
        vmem=32,
        stay=True,
    )


def gate_backward(
    db_mine, db_other, side, out_mat, gate, hat, dev, scale, shift, q, entry, tile=256
):
    half, width = db_mine.shape
    rows = 2 * half
    cols = out_mat.shape[1]
    heads = cols // VD
    mine_block, other_block, pick = half_tiles(side, half // tile, tile, width)

    def kernel(
        side_ref, mine_ref, other_ref, mat_ref, gate_ref, hat_ref, dev_ref, scale_ref, shift_ref,
        q_ref, entry_ref, db_ref, dg_ref, dr_ref, gain_ref, bias_ref, state_ref, total_ref,
    ):
        pick(side_ref, mine_ref, other_ref, db_ref)

        @pl.when(pl.program_id(0) == 0)
        def _():
            gain_ref[...] = jnp.zeros_like(gain_ref)
            bias_ref[...] = jnp.zeros_like(bias_ref)
            total_ref[...] = jnp.zeros_like(total_ref)

        d_y = jnp.dot(db_ref[...], mat_ref[...], preferred_element_type=F32)
        for h in range(heads):
            at = slice(h * VD, (h + 1) * VD)
            z, dy, r_hat = gate_ref[:, at], d_y[:, at], hat_ref[:, at]
            sigma = jax.nn.sigmoid(z)
            affine = r_hat * scale_ref[:, at] + shift_ref[:, at]
            dg_ref[:, at] = (dy * affine * (sigma * (1.0 + z * (1.0 - sigma)))).astype(BF)
            d_affine = dy * (z * sigma)
            gain_ref[:, at] += jnp.sum(d_affine * r_hat, axis=0, keepdims=True)
            bias_ref[:, at] += jnp.sum(d_affine, axis=0, keepdims=True)
            d_hat = d_affine * scale_ref[:, at]
            d_r = standardize_back(d_hat, r_hat, dev_ref[:, h : h + 1]).astype(BF)
            dr_ref[:, at] = d_r
            qd = (q_ref[:, h * KD : (h + 1) * KD].astype(F32) * entry_ref[:, h : h + 1]).astype(BF)
            total_ref[h] += lax.dot_general(
                qd, d_r, (((0,), (0,)), ((), ())), preferred_element_type=F32
            )

        @pl.when(pl.program_id(0) == pl.num_programs(0) - 1)
        def _():
            state_ref[...] = total_ref[...].astype(BF)

    return kernel_call(
        kernel,
        "gate_backward",
        (rows // tile,),
        [
            (db_mine, *mine_block),
            (db_other, *other_block),
            (out_mat, (width, cols), fixed),
            (gate, (tile, cols), row_tile),
            (hat, (tile, cols), row_tile),
            (dev, (tile, heads), row_tile),
            (scale[None, :], (1, cols), fixed),
            (shift[None, :], (1, cols), fixed),
            (q, (tile, heads * KD), row_tile),
            (entry, (tile, heads), row_tile),
        ],
        [((tile, width), row_tile)] + [((tile, cols), row_tile)] * 2 + [((1, cols), fixed)] * 2
        + [((heads, KD, VD), fixed3)],
        [
            ((rows, width), BF),
            ((rows, cols), BF),
            ((rows, cols), BF),
            ((1, cols), F32),
            ((1, cols), F32),
            ((heads, KD, VD), BF),
        ],
        0,
        prefetch=(side[None],),
        scratch=[pltpu.VMEM((heads, KD, VD), F32)],
        stay=True,
    )


def half_tiles(side, steps, tile, width):
    def within(which):
        def index(i, side_ref):
            return (jnp.clip(i - (side_ref[0] ^ which) * steps, 0, steps - 1), 0)

        return index

    def pick(side_ref, mine_ref, other_ref, out_ref):
        own = pl.program_id(0) // steps == side_ref[0]

        @pl.when(own)
        def _():
            out_ref[...] = mine_ref[...].astype(out_ref.dtype)

        @pl.when(jnp.logical_not(own))
        def _():
            out_ref[...] = other_ref[...].astype(out_ref.dtype)

    return ((tile, width), within(0)), ((tile, width), within(1)), pick


def feed_forward(n2_mine, n2_other, side, up, up_shift, cotangent, down, tile=256):
    half, width = n2_mine.shape
    rows = 2 * half
    cols = up.cols
    mine_block, other_block, pick = half_tiles(side, half // tile, tile, width)

    def kernel(
        side_ref, mine_ref, other_ref, shift_ref, cot_ref, *refs
    ):
        up_parts, refs = refs[: up.count], refs[up.count :]
        down_parts, refs = refs[: down.count], refs[down.count :]
        n2_ref, act_ref, dup_ref, sum_ref, sent_ref, kept_ref, up_out, down_out, *refs = refs
        up_ref, up_sems, up_sem, down_ref, down_sems, down_sem = refs
        up.load(up_parts, up_out, up_ref, up_sems, up_sem)
        down.load(down_parts, down_out, down_ref, down_sems, down_sem)

        @pl.when(pl.program_id(0) == 0)
        def _():
            sum_ref[...] = jnp.zeros_like(sum_ref)

        pick(side_ref, mine_ref, other_ref, n2_ref)

        for at in range(0, cols, 1024):
            part = slice(at, at + 1024)
            z = jnp.dot(n2_ref[...], up_ref[:, part], preferred_element_type=F32)
            z = z + shift_ref[:, part]
            d_act = jnp.dot(cot_ref[...], down_ref[:, part], preferred_element_type=F32)
            below = 0.5 * (1.0 + lax.erf(z * (0.5**0.5)))
            act_ref[:, part] = (z * below).astype(BF)
            slope = below + z * (jnp.exp(-0.5 * z * z) * (1.0 / math.sqrt(2.0 * math.pi)))
            d_up = (slope * d_act).astype(BF)
            dup_ref[:, part] = d_up
            sum_ref[:, part] += jnp.sum(d_up.astype(F32), axis=0, keepdims=True)
        own = pl.program_id(0) // (half // tile) == side_ref[0]
        for at in range(0, width, 512):
            part = slice(at, at + 512)
            d_n2 = lax.dot_general(
                dup_ref[...], up_ref[part], (((1,), (1,)), ((), ())), preferred_element_type=F32
            )

            @pl.when(own)
            def _(part=part, d_n2=d_n2):
                kept_ref[:, part] = d_n2

            @pl.when(jnp.logical_not(own))
            def _(part=part, d_n2=d_n2):
                sent_ref[:, part] = d_n2.astype(BF)

        up.end(up_out, up_ref, up_sem)
        down.end(down_out, down_ref, down_sem)

    return kernel_call(
        kernel,
        "feed_forward",
        (rows // tile,),
        [
            (n2_mine, *mine_block),
            (n2_other, *other_block),
            (up_shift[None, :], (1, cols), fixed),
            (cotangent, (tile, width), row_tile),
            *up.ins,
            *down.ins,
        ],
        [((tile, width), row_tile)]
        + [((tile, cols), row_tile)] * 2
        + [((1, cols), fixed), other_block, mine_block]
        + up.outs
        + down.outs,
        [((rows, width), BF), ((rows, cols), BF), ((rows, cols), BF), ((1, cols), F32)]
        + [((half, width), BF), ((half, width), F32)]
        + up.shapes
        + down.shapes,
        16,
        scratch=up.scratch + down.scratch,
        vmem=44,
        prefetch=(side[None],),
        stay=True,
    )


def retain_backward(q, k, v, d_r, state, number, entry, log_decay, cosine, sine, tile=256):
    rows = q.shape[0]
    heads = q.shape[1] // KD

    def kernel(
        decay_ref, q_ref, k_ref, v_ref, dr_ref, state_ref, col_ref, row_ref, entry_ref,
        cos_ref, sin_ref, dq_ref, dk_ref, dv_ref,
    ):
        decay = decay_ref[pl.program_id(0)]
        across = (((1,), (1,)), ((), ()))
        down = (((0,), (0,)), ((), ()))
        for first in reversed(range(0, rows, tile)):
            wide = first + tile
            here = slice(first, wide)
            q_i, dr_i = q_ref[here], dr_ref[here]
            mask = decay_block(first, tile, wide, col_ref[here], row_ref[:, :wide], decay)
            scores = lax.dot_general(q_i, k_ref[:wide], across, preferred_element_type=F32)
            weights = (scores * mask).astype(BF)
            d_scores = lax.dot_general(dr_i, v_ref[:wide], across, preferred_element_type=F32)
            d_scores = (d_scores * mask).astype(BF)
            dq = jnp.dot(d_scores, k_ref[:wide], preferred_element_type=F32)
            dq = dq + own_column(entry_ref[here]) * lax.dot_general(
                dr_i, state_ref[0], across, preferred_element_type=F32
            )
            dq_ref[here] = turn(dq, cos_ref[here], -sin_ref[here]).astype(BF)
            dk = lax.dot_general(d_scores, q_i, down, preferred_element_type=F32)
            dv = lax.dot_general(weights, dr_i, down, preferred_element_type=F32)
            if wide == rows:
                dk_ref[...] = dk
                dv_ref[...] = dv
            else:
                dk_ref[:wide] += dk
                dv_ref[:wide] += dv

    def head(h, *_):
        return (0, h)

    def head3(h, *_):
        return (h, 0, 0)

    return kernel_call(
        kernel,
        "retain_backward",
        (heads,),
        [
            (q, (rows, KD), head),
            (k, (rows, KD), head),
            (v, (rows, VD), head),
            (d_r, (rows, VD), head),
            (state, (1, KD, VD), head3),
            (number[:, None], (rows, 1), fixed),
            (number[None, :], (1, rows), fixed),
            (entry, (rows, heads), fixed),
            (cosine, (rows, KD // 2), fixed),
            (sine, (rows, KD // 2), fixed),
        ],
        [((rows, KD), head), ((rows, KD), head), ((rows, VD), head)],
        [((rows, heads * KD), BF), ((rows, heads * KD), F32), ((rows, heads * VD), F32)],
        0,
        prefetch=(log_decay,),
        stay=True,
    )


def state_backward(k, v, exit_weight, leaving, dk, dv, cosine, sine, tile=256):
    rows = k.shape[0]
    heads = k.shape[1] // KD

    def kernel(
        k_ref, v_ref, exit_ref, leaving_ref, dk_in, dv_in, cos_ref, sin_ref, dk_ref, dv_ref
    ):
        for h in range(heads):
            at, wide = slice(h * KD, (h + 1) * KD), slice(h * VD, (h + 1) * VD)
            weight = exit_ref[:, h : h + 1]
            kd = (k_ref[:, at].astype(F32) * weight).astype(BF)
            d_k = dk_in[:, at] + weight * lax.dot_general(
                v_ref[:, wide], leaving_ref[h], (((1,), (1,)), ((), ())), preferred_element_type=F32
            )
            dk_ref[:, at] = turn(d_k, cos_ref[...], -sin_ref[...]).astype(BF)
            d_v = dv_in[:, wide] + jnp.dot(kd, leaving_ref[h], preferred_element_type=F32)
            dv_ref[:, wide] = d_v.astype(BF)

    return kernel_call(
        kernel,
        "state_backward",
        (rows // tile,),
        [
            (k, (tile, heads * KD), row_tile),
            (v, (tile, heads * VD), row_tile),
            (exit_weight, (tile, heads), row_tile),
            (leaving, leaving.shape, fixed3),
            (dk, (tile, heads * KD), row_tile),
            (dv, (tile, heads * VD), row_tile),
            (cosine, (tile, KD // 2), row_tile),
            (sine, (tile, KD // 2), row_tile),
        ],
        [((tile, heads * KD), row_tile), ((tile, heads * VD), row_tile)],
        [((rows, heads * KD), BF), ((rows, heads * VD), BF)],
        0,
        stay=True,
    )


def second_norm(inputs, side, kept, other, gain, shift, tile=128):
    half, width = kept.shape
    steps = half // tile

    def kernel(side_ref, x_ref, kept_ref, other_ref, gain_ref, shift_ref, mid_ref, n2_ref):
        mid = x_ref[...].astype(F32) + (kept_ref[...].astype(F32) + other_ref[...].astype(F32))
        mid_ref[...] = mid
        hat, _ = standardize(mid)
        n2_ref[...] = (hat * gain_ref[...] + shift_ref[...]).astype(BF)

    return kernel_call(
        kernel,
        "second_norm",
        (steps,),
        [
            (inputs, (tile, width), lambda i, side_ref: (side_ref[0] * steps + i, 0)),
            (kept, (tile, width), row_tile),
            (other, (tile, width), row_tile),
            (gain[None, :], (1, width), fixed),
            (shift[None, :], (1, width), fixed),
        ],
        [((tile, width), row_tile)] * 2,
        [((half, width), F32), ((half, width), BF)],
        6,
        prefetch=(side[None],),
    )


def norm_backward(x, x_rows, kept, other, base, base_rows, gain, side, tile=128):
    half, width = kept.shape
    steps = half // tile

    def kernel(
        side_ref, x_ref, kept_ref, other_ref, base_ref, gain_ref,
        out_ref, low_ref, gain_out, bias_out,
    ):
        @pl.when(pl.program_id(0) == 0)
        def _():
            gain_out[...] = jnp.zeros_like(gain_out)
            bias_out[...] = jnp.zeros_like(bias_out)

        d_n = kept_ref[...].astype(F32) + other_ref[...].astype(F32)
        hat, dev = standardize(x_ref[...].astype(F32))
        gain_out[...] += jnp.sum(d_n * hat, axis=0, keepdims=True)
        bias_out[...] += jnp.sum(d_n, axis=0, keepdims=True)
        out = base_ref[...].astype(F32) + standardize_back(d_n * gain_ref[...], hat, dev)
        out_ref[...] = out
        low_ref[...] = out.astype(BF)

    def picked(i, side_ref):
        return (side_ref[0] * steps + i, 0)

    return kernel_call(
        kernel,
        "norm_backward",
        (steps,),
        [
            (x, (tile, width), picked if x_rows else row_tile),
            (kept, (tile, width), row_tile),
            (other, (tile, width), row_tile),
            (base, (tile, width), picked if base_rows else row_tile),
            (gain[None, :], (1, width), fixed),
        ],
        [((tile, width), row_tile)] * 2 + [((1, width), fixed)] * 2,
        [((half, width), F32), ((half, width), BF), ((1, width), F32), ((1, width), F32)],
        0,
        prefetch=(side[None],),
        stay=True,
    )


def partial_rows(values, mats, which, added=(), pieces=1, tile=512):
    rows, width = values[0].shape[0], mats[0][0].shape[0]
    half, count = rows // 2, len(values)

    def kernel(which_ref, *refs):
        total = sum(
            lax.dot_general(v[...], m[...], (((1,), (1,)), ((), ())), preferred_element_type=F32)
            for v, m in zip(refs[:count], refs[count : 2 * count])
        )
        if added:
            total = total + jnp.concatenate(
                [ref[...].astype(F32) for ref in refs[2 * count : 2 * count + len(added)]], axis=0
            )
        for piece, ref in enumerate(refs[-pieces:]):
            ref[...] = total[piece * half // pieces : (piece + 1) * half // pieces].astype(BF)

    def column_tile(i, *_):
        return (0, i)

    ins = [(v, (half, v.shape[1]), lambda i, which_ref: (which_ref[0], 0)) for v in values]
    ins += [
        (m, (tile, v.shape[1]), lambda i, *_, at=at: (i, at)) for v, (m, at) in zip(values, mats)
    ]
    ins += [(part, (part.shape[0], tile), column_tile) for part in added]
    return kernel_call(
        kernel,
        "partial_rows",
        (width // tile,),
        ins,
        [((half // pieces, tile), column_tile)] * pieces,
        [((half // pieces, width), BF)] * pieces,
        0,
        prefetch=(which[None],),
        stay=True,
    )


def add_sent(kept, sent, tile=256):
    half, width = kept.shape

    def kernel(kept_ref, sent_ref, out_ref):
        out_ref[...] = (kept_ref[...] + sent_ref[...].astype(F32)).astype(BF)

    return kernel_call(
        kernel,
        "add_sent",
        (half // tile,),
        [(kept, (tile, width), row_tile), (sent, (tile, width), row_tile)],
        [((tile, width), row_tile)],
        [((half, width), BF)],
        0,
        stay=True,
    )[0]


def finish_output(mid, kept, other, shift, tile=256):
    half, width = mid.shape

    def kernel(mid_ref, kept_ref, other_ref, shift_ref, out_ref):
        ffn = kept_ref[...].astype(F32) + other_ref[...].astype(F32)
        out_ref[...] = (mid_ref[...] + ffn + shift_ref[...]).astype(BF)

    return kernel_call(
        kernel,
        "finish_output",
        (half // tile,),
        [
            (mid, (tile, width), row_tile),
            (kept, (tile, width), row_tile),
            (other, (tile, width), row_tile),
            (shift[None, :], (1, width), fixed),
        ],
        [((tile, width), row_tile)],
        [((half, width), BF)],
        0,
        stay=True,
    )[0]


def owners_table(size, vectors):
    if size > RING_MOST:
        return jnp.concatenate([vector.reshape(size, -1) for vector in vectors], axis=1)
    wide = [vector.shape[1] // size for vector in vectors]

    def kernel(*refs):
        at = 0
        for ref, width in zip(refs, wide):
            for i in range(size):
                refs[-1][i : i + 1, at : at + width] = ref[:, i * width : (i + 1) * width]
            at += width

    return kernel_call(
        kernel,
        "owners_table",
        (1,),
        [(vector, vector.shape, fixed) for vector in vectors],
        [((size, sum(wide)), fixed)],
        [((size, sum(wide)), F32)],
        0,
    )[0]


def passed(small):
    def kernel(in_ref, out_ref):
        out_ref[...] = in_ref[...]

    return kernel_call(
        kernel,
        "passed",
        (1,),
        [(small, small.shape, fixed)],
        [(small.shape, fixed)],
        [(small.shape, small.dtype)],
        0,
    )[0]


def both_halves(mine, other, side, kind, tile=256):
    half, width = mine.shape
    mine_block, other_block, pick = half_tiles(side, half // tile, tile, width)
    return kernel_call(
        pick,
        "both_halves",
        (2 * half // tile,),
        [(mine, *mine_block), (other, *other_block)],
        [((tile, width), row_tile)],
        [((2 * half, width), kind)],
        0,
        prefetch=(side[None],),
        stay=True,
    )[0]


def gradient(x, *dys, tile=256):
    rows, width = x.shape
    cols = [dy.shape[1] for dy in dys]

    def kernel(x_ref, *refs):
        at = 0
        for dy_ref in refs[:-1]:
            refs[-1][:, at : at + dy_ref.shape[1]] = lax.dot_general(
                x_ref[...], dy_ref[...], (((0,), (0,)), ((), ())), preferred_element_type=F32
            ).astype(BF)
            at += dy_ref.shape[1]

    return kernel_call(
        kernel,
        "gradient",
        (width // tile,),
        [(x, (rows, tile), lambda i, *_: (0, i))] + [(dy, dy.shape, fixed) for dy in dys],
        [((tile, sum(cols)), row_tile)],
        [((width, sum(cols)), BF)],
        0,
    )[0]


def ring_add(grads, arrived, place, step, turned, cut):
    size = lax.axis_size("seq")
    rows = grads[0].shape[0] // size
    last = step == size
    kind = F32 if last else BF

    def kernel(place_ref, *refs):
        outs = refs[2 + len(arrived) :]
        for i in range(2):
            total = refs[i][...].astype(F32)
            if arrived:
                total = total + refs[2 + i][...].astype(F32)
            if last and turned and i == 0:
                total = total.T
            if last and cut and i == 1:
                width = total.shape[1] // 2
                outs[1][...] = total[:, :width]
                outs[2][...] = total[:, width:]
            else:
                outs[i][...] = total.astype(kind)

    def own(sign):
        def index(i, place_ref):
            return (ring_owner(place_ref[0] + sign * step, size), 0)

        return index

    blocks = [(rows, grad.shape[1]) for grad in grads]
    outs = list(blocks)
    if last and turned:
        outs[0] = blocks[0][::-1]
    if last and cut:
        outs[1:] = [(rows, blocks[1][1] // 2)] * 2
    grads = [pltpu.with_memory_space_constraint(grad, pltpu.HBM) for grad in grads]
    ins = [(grads[0], blocks[0], own(-1)), (grads[1], blocks[1], own(1))]
    ins += [(block, block.shape, fixed) for block in arrived]
    return kernel_call(
        kernel,
        "ring_add",
        (1,),
        ins,
        [(block, fixed) for block in outs],
        [(block, kind) for block in outs],
        0,
        prefetch=(place[None],),
    )


def body(
    inputs,
    cotangent,
    lengths,
    offsets,
    first_gain,
    first_bias,
    query_weight,
    key_weight,
    value_weight,
    gate_weight,
    group_gain,
    group_bias,
    out_weight,
    second_gain,
    second_bias,
    up_weight,
    up_bias,
    down_weight,
    down_bias,
):
    size = lax.axis_size("seq")
    rows, width = inputs.shape
    shard = first_gain.shape[0]
    unit = group_gain.shape[0]
    heads = query_weight.shape[1] // KD
    half = rows // 2
    tp_me = lax.axis_index("tp")
    side = lax.rem(tp_me, 2)
    mine = side * half

    qk_own = jnp.concatenate([query_weight, key_weight], axis=1).astype(BF)
    v_own = value_weight.astype(BF)
    own_vector = jnp.concatenate(
        [
            first_gain,
            first_bias,
            second_gain,
            second_bias,
            down_bias,
            group_gain,
            group_bias,
            up_bias,
        ]
    ).astype(BF)[None, :]
    qkv_ring = gather(qk_own, v_own)
    go_ring = gather(gate_weight.astype(BF), out_weight.astype(BF).T)
    uw_ring = gather(up_weight.astype(BF), down_weight.astype(BF).T)
    clock = Clock((qkv_ring, 0), (go_ring, 1), (uw_ring, 0))
    x = clock.tick(inputs)

    first_row = lax.axis_index("seq") * rows
    log_decay = jnp.log(
        1.0
        - jnp.exp2(-5.0 - (tp_me * heads + jnp.arange(heads, dtype=jnp.int32)).astype(jnp.float32))
    )
    number, entry_weight, exit_weight, cosine, sine = block_decay(
        first_row, rows, lengths, offsets, log_decay
    )
    entry_cols, exit_cols = entry_weight.T, exit_weight.T
    table = own_vector
    distance = 1
    while distance < size:
        table = doubled(table, distance)
        table = clock.tick(table)
        distance *= 2
    table = table[jnp.arange(size) ^ lax.axis_index("seq")].astype(F32)

    def wide(i):
        return table[:, i * shard : (i + 1) * shard].reshape(-1)

    def narrow(i):
        start = 5 * shard + i * unit
        return table[:, start : start + unit].reshape(-1)

    gain_one, bias_one, gain_two, bias_two, down_shift = [wide(i) for i in range(5)]
    group_scale, group_shift, up_shift = [narrow(i) for i in range(3)]

    n1 = norm_rows(x, gain_one, bias_one)
    grad_down_bias = jnp.sum(cotangent.astype(F32), axis=0)
    n1, grad_down_bias = barrier(n1, grad_down_bias)
    n1, cosine, sine, number, entry_cols, exit_cols = clock.tick(
        n1, cosine, sine, number, entry_cols, exit_cols
    )
    n1 = clock.until(qkv_ring, n1)

    n1 = clock.tick(n1)
    qk_weight, v_weight = qkv_ring.result()
    q, k, qk_mat = project_turn(n1, qk_weight, cosine, sine)
    n1, q, k = barrier(n1, q, k)
    n1 = clock.tick(n1)
    v, v_mat = project(n1, v_weight)
    v, q, k = clock.tick(v, q, k)
    local_out, local_state = retain(q, k, v, number, exit_cols, log_decay)
    local_out, local_state = clock.tick(local_out, local_state)
    state_parts = Others(local_state.astype(BF), 1).second()
    local_out = clock.until(go_ring, local_out)

    def gathered_state(first, rest, direction):
        total, weight = first.astype(F32), 1.0
        for turn, part in enumerate(rest, 1):
            block = first_row - direction * turn * rows
            passed = passing_weight(block, rows, lengths, offsets, log_decay)
            weight = weight * passed
            total = total + weight[:, None, None] * part.astype(F32)
        return total.astype(BF)

    state = gathered_state(state_parts[0], state_parts[1:], 1)
    state, local_out = barrier(state, local_out)
    g_weight, o_weight = go_ring.result()
    y, gate, r_hat, r_dev, g_mat = gate_forward(
        n1, g_weight, q, entry_cols, state, local_out, group_scale, group_shift
    )
    y = clock.tick(y)
    o_mat = assemble(o_weight)
    y, o_mat = barrier(y, o_mat)

    def pick(values, which):
        return lax.dynamic_slice_in_dim(values, which * half, half)

    def tp_first(make, value):
        sent = make(pick(value, 1 - side)).astype(BF)
        sent, value = clock.tick(sent, value)
        sent = swap(sent, 1)
        return (make(pick(value, side)) + sent.astype(F32)).astype(BF)

    kept = tp_first(lambda part: dot(part, o_mat, ((1,), (1,))), y)
    other = swap(kept, 2)
    kept = clock.tick(kept, count=4)
    kept, other = barrier(kept, other)
    mid, n2_mine = second_norm(inputs, side, kept, other, gain_two, bias_two)
    n2_other = swap(n2_mine, 1)
    n2_mine, n2_other = barrier(n2_mine, n2_other)
    n2_mine, n2_other = clock.until(uw_ring, n2_mine, n2_other)
    u_weight, w_weight = uw_ring.result()
    n2, act, d_up, grad_up_bias, sent_two, kept_two, u_mat, w_mat = feed_forward(
        n2_mine, n2_other, side, u_weight, up_shift, cotangent, w_weight
    )

    line = Line(grad_up_bias)
    pairs_two = [(i, i ^ 2) for i in range(lax.axis_size("tp"))]
    pairs_one = [(i, i ^ 1) for i in range(lax.axis_size("tp"))]

    def to_partner(block, pieces=2):
        count = block.shape[0] // pieces
        return [
            line.send(block[i * count : (i + 1) * count], "tp", pairs_one) for i in range(pieces)
        ]

    def partial_sent(values, mats, pieces=2, cost=0):
        parts = line.run(
            lambda *v: partial_rows(v, mats, 1 - side, pieces=pieces), *values, cost=cost
        )
        parts = parts if isinstance(parts, tuple) else (parts,)
        return [line.send(part, "tp", pairs_one) for part in parts]

    def partial_kept(values, mats, sent, cost=0):
        return line.run(lambda *v: partial_rows(v, mats, side, sent), *values, cost=cost)

    sent_two = line.send(sent_two, "tp", pairs_one)
    grad_w = line.run(gradient, cotangent, act, cost=23)
    kept_two = line.run(add_sent, kept_two, sent_two)
    other_two = line.send(kept_two, "tp", pairs_two)
    grad_u = line.run(gradient, n2, d_up, cost=23)
    wu_back = reduce(grad_w, grad_u, turned=True)
    line.tick(wu_back, wu_back, wu_back)
    d_mid, d_branch_mine, grad_second_gain, grad_second_bias = line.run(
        lambda kept, other: norm_backward(
            mid, False, kept, other, cotangent, True, gain_two, side
        ),
        kept_two,
        other_two,
        cost=6,
    )
    d_branch_other = to_partner(d_branch_mine, 1)[0]
    line.tick(wu_back, cost=23)

    d_branch, d_gate, d_r, grad_group_gain, grad_group_bias, own_grad = line.run(
        lambda mine, other: gate_backward(
            mine,
            other,
            side,
            o_mat,
            gate,
            r_hat,
            r_dev,
            group_scale,
            group_shift,
            q,
            entry_cols,
        ),
        d_branch_mine,
        d_branch_other,
        cost=6,
    )
    others = Others(own_grad, -1, line.send)
    line.tick(wu_back)
    d_q, d_k, d_v = line.run(
        lambda d_r: retain_backward(
            q, k, v, d_r, state, number, entry_cols, log_decay, cosine, sine
        ),
        d_r,
        cost=6,
    )
    leaving_parts = others.second()
    grad_o = line.run(gradient, d_branch, y, cost=6)
    line.tick(wu_back)
    grad_g = line.run(gradient, n1, d_gate, cost=6)
    og_back = reduce(grad_o, grad_g, turned=True)
    leaving = line.run(lambda first, *rest: gathered_state(first, rest, -1), *leaving_parts)
    line.tick(og_back)
    d_k, d_v = line.run(
        lambda d_k, d_v: state_backward(k, v, exit_cols, leaving, d_k, d_v, cosine, sine),
        d_k,
        d_v,
    )
    line.tick(wu_back)
    grad_v = line.run(gradient, n1, d_v, cost=6)
    grad_qk = line.run(gradient, n1, d_q, d_k)
    vqk_back = reduce(grad_v, grad_qk, cut=True)
    line.tick(wu_back)
    line.tick(vqk_back)
    line.tick(og_back)
    d_all = (d_gate, d_v, d_q, d_k)
    mats_all = ((g_mat, 0), (v_mat, 0), (qk_mat, 0), (qk_mat, 1))
    sent_one = partial_sent(d_all, mats_all, 1, cost=6)
    grad_second_gain = line.fill(grad_second_gain, 23)
    line.tick(og_back, vqk_back)
    kept_one = partial_kept(d_all, mats_all, sent_one, cost=6)
    other_one = line.send(kept_one, "tp", pairs_two)
    grad_second_gain = line.fill(grad_second_gain, 23)
    line.tick(og_back, vqk_back)
    part_out = line.run(lambda act: partial_rows((act,), ((w_mat, 0),), 1 - side), act)
    line.tick(og_back, vqk_back)
    _, grad_mine, grad_first_gain, grad_first_bias = line.run(
        lambda kept, other: norm_backward(
            inputs, True, kept, other, d_mid, False, gain_one, side
        ),
        kept_one,
        other_one,
        cost=6,
    )
    grad_other = to_partner(grad_mine, 1)[0]
    sent_out = line.send(part_out, "tp", pairs_one)
    line.tick(og_back, vqk_back, cost=12)
    kept_out = partial_kept((act,), ((w_mat, 0),), (sent_out,))
    other_out = line.send(kept_out, "tp", pairs_two)
    grad_inputs = line.run(
        lambda mine, other: both_halves(mine, other, side, F32), grad_mine, grad_other, cost=23
    )
    line.tick(og_back, vqk_back)

    grad_up_bias = line.token
    table = line.run(
        lambda *vectors: owners_table(size, vectors),
        grad_first_gain,
        grad_first_bias,
        grad_second_gain,
        grad_second_bias,
        grad_down_bias[None, :],
        grad_group_gain,
        grad_group_bias,
        grad_up_bias,
    )
    line.token = grad_inputs
    table, sent = halved(line, table)
    line.tick(vqk_back, og_back)
    output_mine = line.run(
        lambda kept, other: finish_output(mid, kept, other, down_shift),
        kept_out,
        other_out,
        cost=6,
    )
    while table.shape[0] > 1:
        table = line.run(lambda kept, sent: kept + sent, table, sent)
        table, sent = halved(line, table)
        line.tick(vqk_back, og_back)
    output_other = to_partner(output_mine, 1)[0]
    small = line.run(lambda kept, sent: kept + sent, table, sent)[0]
    halves = small[: 4 * shard]
    sent = line.send(halves, "tp", pairs_one)
    while not (og_back.ended and vqk_back.ended):
        line.tick(vqk_back, og_back)
    output = line.run(
        lambda mine, other: both_halves(mine, other, side, BF), output_mine, output_other
    )
    halves = halves + sent
    grad_inputs = line.token
    own = [halves[i * shard : (i + 1) * shard] for i in range(4)]
    own_down_bias = small[4 * shard : 5 * shard]
    own_units = [small[5 * shard + i * unit : 5 * shard + (i + 1) * unit] for i in range(3)]
    own_w, own_u = wu_back.result()
    own_o, own_g = og_back.result()
    own_v, own_q, own_k = vqk_back.result()
    return (
        output,
        grad_inputs,
        own[0],
        own[1],
        own_q,
        own_k,
        own_v,
        own_g,
        own_units[0],
        own_units[1],
        own_o,
        own[2],
        own[3],
        own_u,
        own_units[2],
        own_w,
        own_down_bias,
    )


def solution(mesh):
    placed = (
        P("seq", None),
        P("seq", None),
        P(),
        P(),
        P("seq"),
        P("seq"),
        P("seq", "tp"),
        P("seq", "tp"),
        P("seq", "tp"),
        P("seq", "tp"),
        P(("tp", "seq")),
        P(("tp", "seq")),
        P("tp", "seq"),
        P("seq"),
        P("seq"),
        P("seq", "tp"),
        P(("tp", "seq")),
        P("tp", "seq"),
        P("seq"),
    )
    return jax.shard_map(
        body,
        mesh=mesh,
        in_specs=placed,
        out_specs=(
            P("seq", None),
            P("seq", None),
            P("seq"),
            P("seq"),
            P("seq", "tp"),
            P("seq", "tp"),
            P("seq", "tp"),
            P("seq", "tp"),
            P(("tp", "seq")),
            P(("tp", "seq")),
            P("tp", "seq"),
            P("seq"),
            P("seq"),
            P("seq", "tp"),
            P(("tp", "seq")),
            P("tp", "seq"),
            P("seq"),
        ),
        check_vma=False,
    )
```
